32 devices in a mesh: dp: 8 (over z, y), tensor: 4 (over x, core).
Axes of the slice: x: 2, y: 2, z: 4, core: 2. Of those that a mesh axis runs over, the one named last changes fastest.
Arguments:
- image: bfloat16 [8, 1024, 1536], P('dp', 'tensor'), may hold values from -8 to 8
- text: bfloat16 [8, 154, 1536], P('dp'), may hold values from -8 to 8
- cond: float32 [8, 1536], P('dp'), may hold values from -6 to 6
- w_ada: float32 [2, 1536, 6, 1536], P(None, 'dp', None, 'tensor'), may hold values from -0.15625 to 0.15625
- w_qkv: float32 [2, 1536, 3, 1536], P(None, 'dp', None, 'tensor'), may hold values from -0.15625 to 0.15625
- w_out: float32 [2, 1536, 1536], P(None, ('tensor', 'dp')), may hold values from -1.25 to 1.25
- w_up: float32 [2, 1536, 6144], P(None, 'dp', 'tensor'), may hold values from -0.15625 to 0.15625
- w_down: float32 [2, 6144, 1536], P(None, ('tensor', 'dp')), may hold values from -0.078125 to 0.078125
- grad_image: bfloat16 [8, 1024, 1536], P('dp', 'tensor'), may hold values from -6 to 6
- grad_text: bfloat16 [8, 154, 1536], P('dp'), may hold values from -6 to 6
Outputs:
- image_out: bfloat16 [8, 1024, 1536], P('dp', 'tensor')
- text_out: bfloat16 [8, 154, 1536], P('dp')
- image_grad: float32 [8, 1024, 1536], P('dp', 'tensor')
- text_grad: float32 [8, 154, 1536], P('dp')
- cond_grad: float32 [8, 1536], P('dp')
- shift_grad: float32 [8, 2, 1536], P('dp', None, 'tensor')
- w_ada_grad: float32 [2, 1536, 6, 1536], P(None, 'dp', None, 'tensor')
- w_qkv_grad: float32 [2, 1536, 3, 1536], P(None, 'dp', None, 'tensor')
- w_out_grad: float32 [2, 1536, 1536], P(None, ('tensor', 'dp'))
- w_up_grad: float32 [2, 1536, 6144], P(None, 'dp', 'tensor')
- w_down_grad: float32 [2, 6144, 1536], P(None, ('tensor', 'dp'))
The draws below stay inside these ranges and needn't reach their ends.
All inputs are finite; a program needn't handle non-finite values.
Results may differ from the reference program's by a relative error of at most 0.022.
The reference program's roundings to bfloat16 on the way count: a program that leaves them out, or rounds other values in their place, can miss the bound.
Values may be sent and summed in bfloat16 or wider, within the bound.
A program may use at most 256 MiB of HBM per device.

```python
import jax
import jax.numpy as jnp
from jax import lax

HEADS = 24
HEAD_DIM = 64
D = 1536
FF = 6144
IMG = 1024
TXT = 154
SEQS = 8


def raised(drawn, stream_key, source, target, shards_of, factor):
    owner, partner = [(jnp.arange(drawn.shape[position]) // (drawn.shape[position] // shards_of)).reshape([-1 if axis == position else 1 for axis in range(drawn.ndim)]) for position in (source, target)]
    chosen = jax.random.permutation(stream_key, shards_of)[partner]
    strong = (owner == chosen) | (owner == (partner + shards_of // 2) % shards_of)
    return jnp.where(strong, factor * drawn, drawn)


def block_levels(stream_key, shape, pieces, smallest, largest):
    level, own = 1.0, jax.random.fold_in(stream_key, 6)
    for axis_at, blocks in pieces:
        steps = jnp.exp(jax.random.uniform(jax.random.fold_in(own, axis_at), (blocks,), jnp.float32, smallest / len(pieces), largest / len(pieces)))
        level = level * jnp.repeat(steps, shape[axis_at] // blocks).reshape([-1 if axis == axis_at else 1 for axis in range(len(shape))])
    return level


def normal_values(key, extent, scale, limit, shards=(), kind=jnp.bfloat16):
    entries = jax.random.normal(key, extent, jnp.float32) * scale
    if len(shards) > 0:
        entries = block_levels(key, extent, shards, -0.22, 0.18) * entries
    return jnp.clip(entries, min=-limit, max=limit).astype(kind)


def heavy_noise(key, dims, scale, limit, split, heavy, kind=jnp.bfloat16):
    entries = scale * jax.random.normal(key, dims, jnp.float32)
    if split:
        entries = entries * block_levels(key, dims, split, -0.22, 0.18)
    return jnp.clip(raised(entries, jax.random.fold_in(key, 3), *heavy), -limit, limit).astype(kind)


def setup_inputs(seed: int = 0) -> dict:
    streams_of = jax.random.split(jax.random.key(seed), 11)
    return {
        "image": heavy_noise(streams_of[0], (SEQS, IMG, D), 1.0, 8.0, ((0, 8), (1, 4)), (0, 2, 8, 2.0)),
        "text": heavy_noise(streams_of[1], (SEQS, TXT, D), 1.0, 8.0, ((0, 8),), (0, 2, 8, 2.0)),
        "cond": normal_values(streams_of[2], (SEQS, D), 1.0, 6.0, ((0, 8),), jnp.float32),
        "w_ada": normal_values(streams_of[3], (2, D, 6, D), D ** -0.5, 0.15625, ((1, 8), (3, 4)), jnp.float32),
        "w_qkv": normal_values(streams_of[4], (2, D, 3, D), D ** -0.5, 0.15625, ((1, 8), (3, 4)), jnp.float32),
        "w_out": normal_values(streams_of[5], (2, D, D), (max(D // 64, 16)) ** -0.5, 1.25, ((1, 32),), jnp.float32),
        "w_up": normal_values(streams_of[6], (2, D, FF), D ** -0.5, 0.15625, ((1, 8), (2, 4)), jnp.float32),
        "w_down": normal_values(streams_of[7], (2, FF, D), FF ** -0.5, 0.078125, ((1, 32),), jnp.float32),
        "grad_image": normal_values(streams_of[8], (SEQS, IMG, D), 1.0, 6.0, ((0, 8), (1, 4))),
        "grad_text": normal_values(streams_of[9], (SEQS, TXT, D), 1.0, 6.0, ((0, 8),)),
    }


@jax.custom_vjp
def low(v):
    return lax.optimization_barrier(v.astype(jnp.bfloat16)).astype(jnp.float32)

@jax.custom_vjp
def low_back(v):
    return v

def low_keep(v):
    return (low(v), None)

def low_pass(kept, grad):
    return (grad,)

def back_keep(v):
    return (v, None)

def back_low(kept, grad):
    return (low(grad),)
low.defvjp(low_keep, low_pass)
low_back.defvjp(back_keep, back_low)
EPS = 1e-06
PRECISE = lax.Precision.HIGHEST

def layer_norm(values):
    average = lax.optimization_barrier(jnp.mean(values, axis=-1, keepdims=True))
    centred = values - average
    spread = lax.optimization_barrier(jnp.mean(centred * centred, axis=-1, keepdims=True))
    return centred * lax.rsqrt(spread + EPS)

def matmul(left, right):
    return jnp.dot(left, right, precision=PRECISE, preferred_element_type=jnp.float32)

def head_attention(block):
    queries, key_rows, value_rows = block
    scores = low_back(matmul(queries, key_rows.T) * HEAD_DIM ** (-0.5))
    attn_probs = low(jax.nn.softmax(scores, axis=-1))
    return matmul(attn_probs, value_rows)

def modulate(cond, w_ada):
    ada_low = low(w_ada)
    cond_low = low(jax.nn.silu(cond))
    return low_back(jnp.einsum('d,sdkf->skf', cond_low, ada_low, precision=PRECISE))

def one_sequence(image, text, modulation, w_qkv, w_out, w_up, w_down):
    qkv_low = low(w_qkv)
    out_low = low(w_out)
    up_low = low(w_up)
    down_low = low(w_down)
    streams = [image, text]
    first_in = [low(layer_norm(streams[stream]) * (1.0 + modulation[stream, 1]) + modulation[stream, 0]) for stream in range(2)]
    joint = jnp.concatenate([jnp.einsum('td,dkf->ktf', first_in[stream], qkv_low[stream], precision=PRECISE) for stream in range(2)], axis=1)
    joint = low_back(low(joint))
    num_rows = joint.shape[1]
    blocks = joint.reshape(3, num_rows, HEADS, HEAD_DIM).transpose(2, 0, 1, 3)
    attn_out = lax.map(jax.checkpoint(head_attention), (blocks[:, 0], blocks[:, 1], blocks[:, 2]))
    mixed = low_back(low(attn_out.transpose(1, 0, 2).reshape(num_rows, HEADS * HEAD_DIM)))
    mixed_rows = [mixed[:IMG], mixed[IMG:]]
    results = []
    for stream in range(2):
        branch = low_back(matmul(mixed_rows[stream], out_low[stream]))
        middle = streams[stream] + modulation[stream, 2] * branch
        second_in = low(layer_norm(middle) * (1.0 + modulation[stream, 4]) + modulation[stream, 3])
        pre_act = low_back(matmul(second_in, up_low[stream]))
        hidden = low(jax.nn.gelu(pre_act, approximate=True))
        ffn = low_back(matmul(hidden, down_low[stream]))
        results.append(middle + modulation[stream, 5] * ffn)
    return (results[0], results[1])

def reference(image, text, cond, w_ada, w_qkv, w_out, w_up, w_down, grad_image, grad_text):
    masters = (w_ada, w_qkv, w_out, w_up, w_down)

    def per_sequence(summed, inputs):
        image_seq, text_seq, cond_seq, image_cot, text_cot = inputs
        modulation, mod_pullback = jax.vjp(modulate, cond_seq, w_ada)
        outputs, pullback = jax.vjp(one_sequence, image_seq.astype(jnp.float32), text_seq.astype(jnp.float32), modulation, w_qkv, w_out, w_up, w_down)
        gradients = pullback((image_cot.astype(jnp.float32), text_cot.astype(jnp.float32)))
        cond_part, ada_part = mod_pullback(gradients[2])
        added = (ada_part,) + tuple(gradients[3:])
        summed = tuple((running + extra for running, extra in zip(summed, added)))
        return (summed, (outputs[0].astype(jnp.bfloat16), outputs[1].astype(jnp.bfloat16), gradients[0], gradients[1], cond_part, gradients[2][:, 3]))
    starts = tuple((jnp.zeros_like(master) for master in masters))
    summed, per_seq = lax.scan(per_sequence, starts, (image, text, cond, grad_image, grad_text))
    return (per_seq[0], per_seq[1], per_seq[2], per_seq[3], per_seq[4], per_seq[5], summed[0], summed[1], summed[2], summed[3], summed[4])
```

```python
import jax
import jax.numpy as jnp
from jax import lax
from jax.sharding import PartitionSpec as P

HEAD_DIM = 64
EPS = 1e-06
LOW = jnp.bfloat16
WIDE = jnp.float32
TEXT_TILE = 16


def dot(left, right, dims):
    return lax.dot_general(left, right, (dims, ((), ())), preferred_element_type=WIDE)


def layer_norm(values):
    average = jnp.mean(values, axis=-1, keepdims=True)
    centred = values - average
    spread = jnp.mean(centred * centred, axis=-1, keepdims=True)
    return centred * lax.rsqrt(spread + EPS)


def gelu_tanh(values):
    return jax.nn.gelu(values, approximate=True)


def ring_to_dp(place, size):
    return jnp.where(place < size // 2, 2 * place, 2 * (size - 1 - place) + 1)


def dp_to_ring(index, size):
    return jnp.where(index % 2 == 0, index // 2, size - 1 - index // 2)


def ring_pairs(size, step):
    order = list(range(0, size, 2)) + list(range(size - 1, 0, -2))
    return [(order[p], order[(p + step) % size]) for p in range(size)]


def gather_dp(block, size):
    rows = block.shape[0]
    if size != 8:
        return lax.all_gather(block, "dp", axis=0, tiled=True)
    place = dp_to_ring(lax.axis_index("dp"), size)
    full = jnp.zeros((size * rows,) + block.shape[1:], block.dtype)

    def put(full, piece, at, offset):
        start = ring_to_dp(at % size, size) * rows + offset
        return lax.dynamic_update_slice_in_dim(full, piece, start, 0)

    full = put(full, block, place, 0)
    up, down = block, block
    for step in range(1, size // 2):
        up = lax.ppermute(up, "dp", ring_pairs(size, 1))
        down = lax.ppermute(down, "dp", ring_pairs(size, -1))
        full = put(full, up, place - step + size, 0)
        full = put(full, down, place + step, 0)
    half = rows // 2
    up = lax.ppermute(up[:half], "dp", ring_pairs(size, 1))
    down = lax.ppermute(down[half:], "dp", ring_pairs(size, -1))
    full = put(full, up, place + size // 2, 0)
    full = put(full, down, place + size // 2, half)
    return full


def scatter_dp(grad, size):
    rows = grad.shape[0] // size
    if size != 8:
        return lax.psum_scatter(grad, "dp", scatter_dimension=0, tiled=True).astype(WIDE)
    place = dp_to_ring(lax.axis_index("dp"), size)
    half = rows // 2

    def own(at, offset):
        start = ring_to_dp(at % size, size) * rows + offset
        return lax.dynamic_slice_in_dim(grad, start, half, 0)

    parts = []
    for direction, offset in ((1, 0), (-1, half)):
        moving = own(place - direction + size, offset)
        for step in range(1, size):
            moving = lax.ppermute(moving, "dp", ring_pairs(size, direction))
            mine = own(place - direction * (step + 1) + 2 * size, offset)
            moving = moving.astype(WIDE) + mine.astype(WIDE)
            if step < size - 1:
                moving = moving.astype(LOW)
        parts.append(moving)
    return jnp.concatenate(parts, axis=0)


CORE = [(i, i ^ 1) for i in range(4)]
CHIP = [(i, i ^ 2) for i in range(4)]


def gather_rows(own):
    near = lax.ppermute(own, "tensor", CORE)
    far = lax.ppermute(own, "tensor", CHIP)
    last = lax.ppermute(far, "tensor", CORE)
    return [own, near, far, last]


def scatter_rows(parts):
    low = [part.astype(LOW) for part in parts]
    sent = lax.ppermute(jnp.concatenate([low[1], low[3]]), "tensor", CORE)
    rows = parts[0].shape[0]
    far = (low[2].astype(WIDE) + sent[rows:].astype(WIDE)).astype(LOW)
    far = lax.ppermute(far, "tensor", CHIP)
    return low[0].astype(WIDE) + sent[:rows].astype(WIDE) + far.astype(WIDE)


def gather_streams(own):
    split = own[0].shape[0]
    blocks = gather_rows(jnp.concatenate(own, axis=0))
    return [
        jnp.concatenate([block[:split] for block in blocks], axis=0),
        jnp.concatenate([block[split:] for block in blocks], axis=0),
    ]


def scatter_streams(partials):
    split = partials[0].shape[0] // 4
    text = partials[1].shape[0] // 4
    parts = [
        jnp.concatenate(
            [partials[0][b * split : (b + 1) * split], partials[1][b * text : (b + 1) * text]]
        )
        for b in range(4)
    ]
    own = scatter_rows(parts)
    return [own[:split], own[split:]]


def to_heads(rows, heads):
    return rows.reshape(rows.shape[0], heads, HEAD_DIM).transpose(1, 0, 2)


def from_heads(blocks):
    return blocks.transpose(1, 0, 2).reshape(blocks.shape[1], -1)


def attend(block, bias):
    queries, keys, values = block
    scores = dot(queries, keys, ((1,), (1,))) * HEAD_DIM ** (-0.5) + bias
    row_max = jnp.max(scores, axis=-1, keepdims=True)
    shifted = jnp.exp(scores - row_max)
    row_sum = jnp.sum(shifted, axis=-1, keepdims=True)
    output = dot((shifted / row_sum).astype(LOW), values, ((1,), (0,)))
    return output.astype(LOW), row_max[:, 0] + jnp.log(row_sum[:, 0])


def attend_back(block, bias):
    queries, keys, values, log_total, grad_output = block
    scaling = HEAD_DIM ** (-0.5)
    scores = dot(queries, keys, ((1,), (1,))) * scaling + bias
    probs = jnp.exp(scores - log_total[:, None])
    grad_probs = dot(grad_output, values, ((1,), (1,)))
    row_dot = jnp.sum(grad_probs * probs, axis=-1, keepdims=True)
    grad_scores = (probs * (grad_probs - row_dot)).astype(LOW)
    grad_queries = (dot(grad_scores, keys, ((1,), (0,))) * scaling).astype(LOW)
    grad_keys = (dot(grad_scores, queries, ((0,), (0,))) * scaling).astype(LOW)
    grad_values = dot(probs.astype(LOW), grad_output, ((0,), (0,))).astype(LOW)
    return grad_queries, grad_keys, grad_values


def local(size, image, text, cond, w_ada, w_qkv, w_out, w_up, w_down, grad_image, grad_text):
    index = lax.axis_index("tensor")
    dp_index = lax.axis_index("dp")
    seqs = size
    image_rows, width = image.shape[1], image.shape[2]
    text_tokens = text.shape[1]
    text_rows = -(-text_tokens // (4 * TEXT_TILE)) * TEXT_TILE
    text_pad = 4 * text_rows - text_tokens
    width_here = w_ada.shape[-1]
    ada_rows = w_ada.shape[1]
    heads_here = w_qkv.shape[-1] // HEAD_DIM
    rows_of = [image_rows, text_rows]

    def gathered(weight, stream):
        block = weight[stream].astype(LOW)
        return gather_dp(block.reshape(block.shape[0], -1), size)

    qkv_full = [gathered(w_qkv, stream) for stream in range(2)]
    out_full = [gathered(w_out, stream) for stream in range(2)]
    up_full, down_full = [None, None], [None, None]
    for stream in range(2):
        up_full[stream] = gathered(w_up, stream)
        down_full[stream] = gathered(w_down, stream)

    cond_low = jax.nn.silu(cond).astype(LOW)
    cond_rows = lax.all_to_all(
        cond_low.reshape(seqs, ada_rows), "dp", split_axis=0, concat_axis=0, tiled=True
    )
    ada_low = w_ada.astype(LOW)
    mod_parts = jnp.einsum("nd,sdkf->nskf", cond_rows, ada_low, preferred_element_type=WIDE)
    mod_parts = lax.all_to_all(mod_parts, "dp", split_axis=0, concat_axis=0, tiled=True)
    modulation = lax.all_gather(jnp.sum(mod_parts, axis=0), "tensor", axis=2, tiled=True)

    def mod_row(stream, which):
        return modulation[stream, which][None, :]

    def own_text(rows):
        padded = jnp.pad(rows, ((0, text_pad), (0, 0)))
        return lax.dynamic_slice_in_dim(padded, index * text_rows, text_rows, 0)

    streams = [image[0].astype(WIDE), own_text(text[0]).astype(WIDE)]
    cotangent = [grad_image[0].astype(WIDE), own_text(grad_text[0]).astype(WIDE)]
    normed_in = [layer_norm(residual) for residual in streams]
    first_in = [
        (normed_in[s] * (1.0 + mod_row(s, 1)) + mod_row(s, 0)).astype(LOW) for s in range(2)
    ]
    attn_rows = gather_streams(first_in)
    joint = jnp.concatenate(
        [dot(attn_rows[s], qkv_full[s], ((1,), (0,))).astype(LOW) for s in range(2)], axis=0
    )
    places = jnp.arange(4 * text_rows)
    token = ((places // text_rows) ^ index) * text_rows + places % text_rows
    bias = jnp.concatenate(
        [jnp.zeros((4 * image_rows,), WIDE), jnp.where(token < text_tokens, 0.0, -1e30)]
    )[None, :]
    queries, keys, values = [to_heads(part, heads_here) for part in jnp.split(joint, 3, axis=1)]
    attn_out, log_total = lax.map(lambda block: attend(block, bias), (queries, keys, values))
    mixed = from_heads(attn_out)
    split_at = 4 * image_rows
    mixed_rows = [mixed[:split_at], mixed[split_at:]]
    branches = scatter_streams([dot(mixed_rows[s], out_full[s], ((1,), (0,))) for s in range(2)])
    middle = [streams[s] + mod_row(s, 2) * branches[s] for s in range(2)]
    normed_mid = [layer_norm(residual) for residual in middle]
    second_in = [
        (normed_mid[s] * (1.0 + mod_row(s, 4)) + mod_row(s, 3)).astype(LOW) for s in range(2)
    ]
    ffn_grad = [(mod_row(s, 5) * cotangent[s]).astype(LOW) for s in range(2)]
    ffn_rows = gather_streams(ffn_grad)
    mlp_rows = gather_streams(second_in)
    ffn_parts, up_grad, down_grad, second_parts = [], [], [], []
    for s in range(2):
        pre_act = dot(mlp_rows[s], up_full[s], ((1,), (0,)))
        hidden = gelu_tanh(pre_act).astype(LOW)
        ffn_parts.append(dot(hidden, down_full[s], ((1,), (0,))))
        hidden_grad = dot(ffn_rows[s], down_full[s], ((1,), (1,)))
        pre_grad = jax.vjp(gelu_tanh, pre_act)[1](hidden_grad)[0].astype(LOW)
        second_parts.append(dot(pre_grad, up_full[s], ((1,), (1,))))
        down_grad.append(dot(hidden, ffn_rows[s], ((0,), (0,))).astype(LOW))
        up_grad.append(dot(mlp_rows[s], pre_grad, ((0,), (0,))).astype(LOW))
    down_sum, up_sum = [None, None], [None, None]
    for s in range(2):
        down_sum[s] = scatter_dp(down_grad[s], size)
        up_sum[s] = scatter_dp(up_grad[s], size)
    second_grad = scatter_streams(second_parts)
    ffn = scatter_streams(ffn_parts)
    results = [(middle[s] + mod_row(s, 5) * ffn[s]).astype(LOW) for s in range(2)]
    middle_grad = [
        cotangent[s]
        + jax.vjp(layer_norm, middle[s])[1](second_grad[s] * (1.0 + mod_row(s, 4)))[0]
        for s in range(2)
    ]
    branch_grad = [(mod_row(s, 2) * middle_grad[s]).astype(LOW) for s in range(2)]
    branch_rows = gather_streams(branch_grad)
    out_grad = [dot(mixed_rows[s], branch_rows[s], ((0,), (0,))).astype(LOW) for s in range(2)]
    out_sum = [scatter_dp(grad, size) for grad in out_grad]
    mixed_grad = jnp.concatenate(
        [dot(branch_rows[s], out_full[s], ((1,), (1,))).astype(LOW) for s in range(2)], axis=0
    )
    grads = lax.map(
        lambda block: attend_back(block, bias),
        (queries, keys, values, log_total, to_heads(mixed_grad, heads_here)),
    )
    joint_grad = jnp.concatenate([from_heads(grad) for grad in grads], axis=1)
    joint_rows = [joint_grad[:split_at], joint_grad[split_at:]]
    qkv_grad = [dot(attn_rows[s], joint_rows[s], ((0,), (0,))).astype(LOW) for s in range(2)]
    qkv_sum = [scatter_dp(grad, size) for grad in qkv_grad]
    first_grad = scatter_streams([dot(joint_rows[s], qkv_full[s], ((1,), (1,))) for s in range(2)])
    input_grad = [
        middle_grad[s]
        + jax.vjp(layer_norm, streams[s])[1](first_grad[s] * (1.0 + mod_row(s, 1)))[0]
        for s in range(2)
    ]
    mod_terms = jnp.stack(
        [
            jnp.stack(
                [
                    jnp.sum(first_grad[s], axis=0),
                    jnp.sum(first_grad[s] * normed_in[s], axis=0),
                    jnp.sum(middle_grad[s] * branches[s], axis=0),
                    jnp.sum(second_grad[s], axis=0),
                    jnp.sum(second_grad[s] * normed_mid[s], axis=0),
                    jnp.sum(cotangent[s] * ffn[s], axis=0),
                ]
            )
            for s in range(2)
        ]
    )
    mod_split = mod_terms.reshape(2, 6, 4, width_here).transpose(2, 0, 1, 3)
    mod_sum = jnp.sum(
        lax.all_to_all(mod_split, "tensor", split_axis=0, concat_axis=0, tiled=True), axis=0
    )
    shift_grad = mod_sum[:, 3]
    mod_grad = lax.all_gather(mod_sum.astype(LOW), "dp", axis=0, tiled=False)
    ada_grad = jnp.einsum("nd,nskf->sdkf", cond_rows, mod_grad, preferred_element_type=WIDE)
    act_parts = jnp.einsum("nskf,sdkf->nd", mod_grad, ada_low, preferred_element_type=WIDE)
    act_parts = lax.all_to_all(act_parts, "dp", split_axis=0, concat_axis=0, tiled=True)
    act_grad = lax.psum(act_parts.reshape(1, width), "tensor")
    cond_grad = jax.vjp(jax.nn.silu, cond)[1](act_grad)[0]

    def whole_text(rows):
        blocks = lax.all_gather(rows, "tensor", axis=0, tiled=True)
        return blocks[:text_tokens][None]

    def shard(sums, like):
        return jnp.stack(sums).reshape(like.shape)

    return (
        results[0][None],
        whole_text(results[1]),
        input_grad[0][None],
        whole_text(input_grad[1]),
        cond_grad,
        shift_grad[None],
        ada_grad,
        shard(qkv_sum, w_qkv),
        shard(out_sum, w_out),
        shard(up_sum, w_up),
        shard(down_sum, w_down),
    )


def solution(mesh):
    size = mesh.shape["dp"]

    def step(*args):
        return local(size, *args)

    return jax.shard_map(
        step,
        mesh=mesh,
        in_specs=(
            P("dp", "tensor", None),
            P("dp", None, None),
            P("dp", None),
            P(None, "dp", None, "tensor"),
            P(None, "dp", None, "tensor"),
            P(None, ("tensor", "dp"), None),
            P(None, "dp", "tensor"),
            P(None, ("tensor", "dp"), None),
            P("dp", "tensor", None),
            P("dp", None, None),
        ),
        out_specs=(
            P("dp", "tensor", None),
            P("dp", None, None),
            P("dp", "tensor", None),
            P("dp", None, None),
            P("dp", None),
            P("dp", None, "tensor"),
            P(None, "dp", None, "tensor"),
            P(None, "dp", None, "tensor"),
            P(None, ("tensor", "dp"), None),
            P(None, "dp", "tensor"),
            P(None, ("tensor", "dp"), None),
        ),
        check_vma=False,
    )
```

```python
import functools

import jax
import jax.numpy as jnp
from jax import lax
from jax.experimental import pallas as pl
from jax.experimental.pallas import tpu as pltpu
from jax.sharding import PartitionSpec as P

HEAD_DIM = 64
EPS = 1e-06
LOW = jnp.bfloat16
WIDE = jnp.float32
TEXT_TILE = 64
POOL_TILE = 8
LANES = 128
NT, NN, TN = ((1,), (1,)), ((1,), (0,)), ((0,), (0,))


def dot(left, right, dims):
    return lax.dot_general(left, right, (dims, ((), ())), preferred_element_type=WIDE)


def layer_norm(values):
    average = jnp.mean(values, axis=-1, keepdims=True)
    centred = values - average
    spread = jnp.mean(centred * centred, axis=-1, keepdims=True)
    return centred * lax.rsqrt(spread + EPS)


def gelu_tanh(values):
    return jax.nn.gelu(values, approximate=True)


MESH = pl.DeviceIdType.MESH
RING = 8


def ring_dp(place):
    place = place % RING
    return 2 * place + (place // (RING // 2)) * (2 * RING - 1 - 4 * place)


def ring_place():
    index = lax.axis_index("dp")
    return index // 2 + (index % 2) * (RING - 1 - 2 * (index // 2))


def ring_sides(place):
    tensor = lax.axis_index("tensor")
    return (ring_dp(place + 1), tensor), (ring_dp(place + RING - 1), tensor)


def meet(sides):
    barrier = pltpu.get_barrier_semaphore()
    for side in sides:
        pl.semaphore_signal(barrier, inc=1, device_id=side, device_id_type=MESH)
    pl.semaphore_wait(barrier, len(sides))


def half_of(rows, columns, way):
    if rows // 2 % 16 == 0:
        return way * (rows // 2), rows // 2, 0, columns
    return 0, rows, way * (columns // 2), columns // 2


class GatherRing:
    STEPS = RING // 2

    def __init__(self, blocks, fulls, sems):
        self.blocks, self.fulls = blocks, fulls
        self.own_sem, self.send_sem, self.recv_sem = sems
        self.place = ring_place()
        self.sides = ring_sides(self.place)

    @staticmethod
    def scratch(count):
        steps = RING // 2
        return [
            pltpu.SemaphoreType.DMA((count,)),
            pltpu.SemaphoreType.DMA((count, 2, steps)),
            pltpu.SemaphoreType.DMA((count, 2, steps)),
        ]

    def copy(self, i, way, step):
        rows, columns = self.blocks[i].shape
        at = self.place + (RING - step if way == 0 else step)
        top, high, left, wide = 0, rows, 0, columns
        if step == self.STEPS - 1:
            top, high, left, wide = half_of(rows, columns, way)
        there = self.fulls[i].at[pl.ds(ring_dp(at) * rows + top, high), pl.ds(left, wide)]
        here = there if step else self.blocks[i]
        return pltpu.make_async_remote_copy(
            src_ref=here,
            dst_ref=there,
            send_sem=self.send_sem.at[i, way, step],
            recv_sem=self.recv_sem.at[i, way, step],
            device_id=self.sides[way],
            device_id_type=MESH,
        )

    def own(self, i):
        rows = self.blocks[i].shape[0]
        start = ring_dp(self.place) * rows
        return pltpu.make_async_copy(
            self.blocks[i], self.fulls[i].at[pl.ds(start, rows)], self.own_sem.at[i]
        )

    def start(self):
        for i in range(len(self.blocks)):
            for way in range(2):
                self.copy(i, way, 0).start()
            self.own(i).start()

    def step(self, step):
        for i in range(len(self.blocks)):
            for way in range(2):
                self.copy(i, way, step - 1).wait_recv()
                if step < self.STEPS:
                    self.copy(i, way, step).start()

    def end(self):
        for i in range(len(self.blocks)):
            self.own(i).wait()
            for way in range(2):
                for step in range(self.STEPS):
                    self.copy(i, way, step).wait_send()


class ScatterRing:
    STEPS = RING - 1

    def __init__(self, grads, sums, scratch):
        self.grads, self.sums = grads, sums
        count = len(grads)
        self.mine, self.got = scratch[:count], scratch[count : 2 * count]
        self.mine_sem, self.send_sem, self.recv_sem = scratch[2 * count :]
        self.place = ring_place()
        self.sides = ring_sides(self.place)

    @staticmethod
    def scratch(shapes):
        sizes = [half_of(rows // RING, columns, 0) for rows, columns in shapes]
        halves = [(2, RING, high, wide) for _, high, _, wide in sizes]
        gots = [(2, RING - 1, high, wide) for _, high, _, wide in sizes]
        count = len(shapes)
        return [
            *[pltpu.VMEM(shape, LOW) for shape in halves],
            *[pltpu.VMEM(shape, LOW) for shape in gots],
            pltpu.SemaphoreType.DMA((count, 2, RING)),
            pltpu.SemaphoreType.DMA((count, 2, RING - 1)),
            pltpu.SemaphoreType.DMA((count, 2, RING - 1)),
        ]

    def load(self, i, way, step):
        rows, columns = self.grads[i].shape[0] // RING, self.grads[i].shape[1]
        at = self.place + (2 * RING - step - 1 if way == 0 else step + 1)
        top, high, left, wide = half_of(rows, columns, way)
        return pltpu.make_async_copy(
            self.grads[i].at[pl.ds(ring_dp(at) * rows + top, high), pl.ds(left, wide)],
            self.mine[i].at[way, step],
            self.mine_sem.at[i, way, step],
        )

    def copy(self, i, way, step):
        return pltpu.make_async_remote_copy(
            src_ref=self.mine[i].at[way, step],
            dst_ref=self.got[i].at[way, step],
            send_sem=self.send_sem.at[i, way, step],
            recv_sem=self.recv_sem.at[i, way, step],
            device_id=self.sides[way],
            device_id_type=MESH,
        )

    def load_all(self):
        for step in range(RING):
            for i in range(len(self.grads)):
                for way in range(2):
                    self.load(i, way, step).start()

    def start(self):
        for i in range(len(self.grads)):
            for way in range(2):
                self.load(i, way, 0).wait()
                self.copy(i, way, 0).start()

    def step(self, step):
        for i in range(len(self.grads)):
            rows, columns = self.grads[i].shape[0] // RING, self.grads[i].shape[1]
            for way in range(2):
                top, high, left, wide = half_of(rows, columns, way)
                self.load(i, way, step).wait()
                self.copy(i, way, step - 1).wait_recv()
                total = self.mine[i][way, step].astype(WIDE) + self.got[i][way, step - 1].astype(WIDE)
                if step < self.STEPS:
                    self.mine[i][way, step] = total.astype(LOW)
                    self.copy(i, way, step).start()
                else:
                    self.sums[i][pl.ds(top, high), pl.ds(left, wide)] = total

    def end(self):
        for i in range(len(self.grads)):
            for way in range(2):
                for step in range(self.STEPS):
                    self.copy(i, way, step).wait_send()


ANY = pl.BlockSpec(memory_space=pl.ANY)
WHOLE = pl.BlockSpec(memory_space=pltpu.VMEM)
VMEM_LIMIT = 56 << 20


def gather_kernel(count, *refs):
    ring = GatherRing(refs[:count], refs[count : 2 * count], refs[2 * count :])
    meet(ring.sides)
    ring.start()
    for step in range(1, ring.STEPS + 1):
        ring.step(step)
    ring.end()


def gather_ring(blocks, ident):
    count = len(blocks)
    return pl.pallas_call(
        functools.partial(gather_kernel, count),
        out_shape=[
            jax.ShapeDtypeStruct((RING * block.shape[0], block.shape[1]), block.dtype)
            for block in blocks
        ],
        in_specs=[ANY] * count,
        out_specs=[ANY] * count,
        scratch_shapes=GatherRing.scratch(count),
        compiler_params=pltpu.CompilerParams(
            collective_id=ident, has_side_effects=True, vmem_limit_bytes=VMEM_LIMIT
        ),
        name="gather_ring",
    )(*blocks)


def scatter_kernel(count, *refs):
    ring = ScatterRing(refs[:count], refs[count : 2 * count], refs[2 * count :])
    ring.load_all()
    meet(ring.sides)
    ring.start()
    for step in range(1, ring.STEPS + 1):
        ring.step(step)
    ring.end()


def scatter_ring(grads, ident):
    count = len(grads)
    return pl.pallas_call(
        functools.partial(scatter_kernel, count),
        out_shape=[
            jax.ShapeDtypeStruct((grad.shape[0] // RING, grad.shape[1]), WIDE) for grad in grads
        ],
        in_specs=[ANY] * count,
        out_specs=[WHOLE] * count,
        scratch_shapes=ScatterRing.scratch([grad.shape for grad in grads]),
        compiler_params=pltpu.CompilerParams(
            collective_id=ident, has_side_effects=True, vmem_limit_bytes=VMEM_LIMIT
        ),
        name="scatter_ring",
    )(*grads)


def gather_dp(blocks, size, ident):
    if size == RING:
        return gather_ring(blocks, ident)
    return [lax.all_gather(block, "dp", axis=0, tiled=True) for block in blocks]


def scatter_dp(grads, size, ident):
    if size == RING:
        return scatter_ring(grads, ident)
    return [
        lax.psum_scatter(grad, "dp", scatter_dimension=0, tiled=True).astype(WIDE)
        for grad in grads
    ]


def beside(ring, blocks, size, ident, before, after):
    blocks = lax.optimization_barrier(tuple(blocks) + tuple(before))[: len(blocks)]
    found = tuple(ring(list(blocks), size, ident))
    held = lax.optimization_barrier(found + tuple(after))
    return held[: len(found)], held[len(found) :]


CORE = [(i, i ^ 1) for i in range(4)]
CHIP = [(i, i ^ 2) for i in range(4)]


def gather_start(own):
    near = lax.ppermute(own, "tensor", CORE)
    far = lax.ppermute(own, "tensor", CHIP)
    return near, far


def gather_end(own, near, far):
    last = lax.ppermute(far, "tensor", CORE)
    return jnp.concatenate([own, near, far, last], axis=0)


def gather_rows(own):
    return gather_end(own, *gather_start(own))


def scatter_start(partial):
    rows = partial.shape[0] // 4
    low = partial.astype(LOW)
    part = [low[b * rows : (b + 1) * rows] for b in range(4)]
    sent = lax.ppermute(jnp.concatenate([part[1], part[3]]), "tensor", CORE)
    here = part[0].astype(WIDE) + sent[:rows].astype(WIDE)
    return here, (part[2].astype(WIDE) + sent[rows:].astype(WIDE)).astype(LOW)


def scatter_rows(partial):
    here, there = scatter_start(partial)
    return here + lax.ppermute(there, "tensor", CHIP).astype(WIDE)


def head_lanes(head):
    lane = lax.broadcasted_iota(jnp.int32, (1, LANES), 1)
    return (lane < HEAD_DIM) if head == 0 else (lane >= HEAD_DIM)


def attend_pair(split, bias_ref, q_ref, k_ref, v_ref, out_ref, lse_ref):
    scale = HEAD_DIM ** (-0.5)
    bias = bias_ref[...]
    outs, totals = [], []
    for head in range(2):
        mine = head_lanes(head)
        queries = jnp.where(mine, q_ref[...] * scale, 0).astype(LOW)
        image = dot(queries, k_ref[:split], NT)
        text = dot(queries, k_ref[split:], NT) + bias
        top = jnp.maximum(
            jnp.max(image, axis=1, keepdims=True), jnp.max(text, axis=1, keepdims=True)
        )
        image = jnp.exp(image - top).astype(LOW)
        text = jnp.exp(text - top).astype(LOW)
        values = jnp.where(mine, v_ref[...], 1).astype(LOW)
        both = dot(image, values[:split], NN) + dot(text, values[split:], NN)
        sums = pltpu.roll(both, HEAD_DIM, 1)
        outs.append(both / sums)
        totals.append(top + jnp.log(sums))
    first = head_lanes(0)
    out_ref[...] = jnp.where(first, outs[0], outs[1]).astype(out_ref.dtype)
    flipped = jnp.where(first, totals[0], totals[1]).T
    lse_ref[0] = jnp.concatenate([flipped[:4], flipped[HEAD_DIM : HEAD_DIM + 4]], axis=0)


def attend_kernel(split, count, waits, *refs):
    bias_ref, q_ref, k_ref, v_ref = refs[:4]
    blocks, (out_ref, lse_ref) = refs[4 : 4 + count], refs[4 + count : 6 + count]
    at = pl.program_id(0) * pl.num_programs(1) + pl.program_id(1)
    if count:
        ring = GatherRing(blocks, refs[6 + count : 6 + 2 * count], refs[6 + 2 * count :])

        @pl.when(at == 0)
        def _():
            meet(ring.sides)
            ring.start()

        for step, when in enumerate(waits):

            @pl.when(at == when)
            def _():
                ring.step(step + 1)

    attend_pair(split, bias_ref, q_ref, k_ref, v_ref, out_ref, lse_ref)
    if count:

        @pl.when(at == pl.num_programs(0) * pl.num_programs(1) - 1)
        def _():
            for step in range(len(waits) + 1, ring.STEPS + 1):
                ring.step(step)
            ring.end()


def attend(joint, bias, split, heads, blocks, ident, waits):
    rows, pairs, count, block = joint.shape[0], heads // 2, len(blocks), joint.shape[0] // 2
    whole = lambda part: pl.BlockSpec((rows, LANES), lambda h, i: (0, part * pairs + h))
    extra = dict(collective_id=ident, has_side_effects=True) if count else {}
    found = pl.pallas_call(
        functools.partial(attend_kernel, split, count, waits),
        grid=(pairs, 2),
        in_specs=[
            pl.BlockSpec((1, rows - split), lambda h, i: (0, 0)),
            pl.BlockSpec((block, LANES), lambda h, i: (i, h)),
            whole(1),
            whole(2),
            *[ANY] * count,
        ],
        out_specs=[
            pl.BlockSpec((block, LANES), lambda h, i: (i, h)),
            pl.BlockSpec((1, 8, block), lambda h, i: (h, 0, i)),
            *[ANY] * count,
        ],
        out_shape=[
            jax.ShapeDtypeStruct((rows, heads * HEAD_DIM), LOW),
            jax.ShapeDtypeStruct((pairs, 8, rows), WIDE),
            *[jax.ShapeDtypeStruct((RING * b.shape[0], b.shape[1]), b.dtype) for b in blocks],
        ],
        scratch_shapes=GatherRing.scratch(count) if count else [],
        compiler_params=pltpu.CompilerParams(vmem_limit_bytes=VMEM_LIMIT, **extra),
        name="attend",
    )(bias, joint, joint, joint, *blocks)
    return found[0], found[1], found[2:]


def attend_back_pair(split, refs):
    (bias_ref, q_ref, k_ref, v_ref, o_ref, g_ref, lse_ref, dq_ref, dk_ref, dv_ref, dk_acc, dv_acc) = refs
    step = pl.program_id(1)
    scale = HEAD_DIM ** (-0.5)

    @pl.when(step == 0)
    def _():
        dk_acc[...] = jnp.zeros_like(dk_acc)
        dv_acc[...] = jnp.zeros_like(dv_acc)

    product = (g_ref[...].astype(WIDE) * o_ref[...].astype(WIDE)).T
    bias = bias_ref[...]
    dq = None
    for head in range(2):
        mine = head_lanes(head)
        queries = jnp.where(mine, q_ref[...] * scale, 0).astype(LOW)
        grads = jnp.where(mine, g_ref[...], 0).astype(LOW)
        keys = jnp.where(mine, k_ref[...], 0).astype(LOW)
        own = product[head * HEAD_DIM : (head + 1) * HEAD_DIM]
        delta = jnp.sum(own, axis=0, keepdims=True)
        total = lse_ref[0][4 * head : 4 * head + 1]
        for low, high in ((0, split), (split, k_ref.shape[0])):
            scores = dot(k_ref[low:high], queries, NT)
            if low:
                scores = scores + bias
            probs = jnp.exp(scores - total)
            grad_probs = dot(v_ref[low:high], grads, NT)
            grad_scores = (probs * (grad_probs - delta)).astype(LOW)
            dv_acc[low:high] += dot(probs.astype(LOW), grads, NN)
            dk_acc[low:high] += dot(grad_scores, queries, NN)
            part = dot(grad_scores, keys[low:high], TN)
            dq = part if dq is None else dq + part
    dq_ref[...] = (dq * scale).astype(LOW)

    @pl.when(step == pl.num_programs(1) - 1)
    def _():
        dk_ref[...] = dk_acc[...].astype(LOW)
        dv_ref[...] = dv_acc[...].astype(LOW)


def attend_back_kernel(split, count, waits, *refs):
    ins, rest = refs[:7], refs[7:]
    grads, outs, rest = rest[:count], rest[count : count + 3], rest[count + 3 :]
    sums, accs, rest = rest[:count], rest[count : count + 2], rest[count + 2 :]
    at = pl.program_id(0) * pl.num_programs(1) + pl.program_id(1)
    if count:
        ring = ScatterRing(grads, sums, rest)

        @pl.when(at == 0)
        def _():
            ring.load_all()
            meet(ring.sides)
            ring.start()

        for step, when in enumerate(waits):

            @pl.when(at == when)
            def _():
                ring.step(step + 1)

    attend_back_pair(split, (*ins, *outs, *accs))
    if count:

        @pl.when(at == pl.num_programs(0) * pl.num_programs(1) - 1)
        def _():
            for step in range(len(waits) + 1, ring.STEPS + 1):
                ring.step(step)
            ring.end()


def attend_back(joint, bias, mixed, grad, lse, split, heads, grads, ident, waits):
    rows, pairs, count, block = joint.shape[0], heads // 2, len(grads), joint.shape[0] // 2
    whole = lambda part: pl.BlockSpec((rows, LANES), lambda h, i: (0, part * pairs + h))
    some = pl.BlockSpec((block, LANES), lambda h, i: (i, h))
    extra = dict(collective_id=ident, has_side_effects=True) if count else {}
    found = pl.pallas_call(
        functools.partial(attend_back_kernel, split, count, waits),
        grid=(pairs, 2),
        in_specs=[
            pl.BlockSpec((rows - split, 1), lambda h, i: (0, 0)),
            some,
            whole(1),
            whole(2),
            some,
            some,
            pl.BlockSpec((1, 8, block), lambda h, i: (h, 0, i)),
            *[ANY] * count,
        ],
        out_specs=[some, whole(0), whole(0), *[WHOLE] * count],
        out_shape=[
            *[jax.ShapeDtypeStruct((rows, heads * HEAD_DIM), LOW)] * 3,
            *[jax.ShapeDtypeStruct((g.shape[0] // RING, g.shape[1]), WIDE) for g in grads],
        ],
        scratch_shapes=[
            *[pltpu.VMEM((rows, LANES), WIDE)] * 2,
            *(ScatterRing.scratch([g.shape for g in grads]) if count else []),
        ],
        compiler_params=pltpu.CompilerParams(vmem_limit_bytes=VMEM_LIMIT, **extra),
        name="attend_back",
    )(bias.T, joint, joint, joint, mixed, grad, lse, *grads)
    return found[:3], found[3:]


def local(size, image, text, cond, w_ada, w_qkv, w_out, w_up, w_down, grad_image, grad_text):
    index = lax.axis_index("tensor")
    seqs = size
    image_rows, width = image.shape[1], image.shape[2]
    text_tokens = text.shape[1]
    text_own = -(-text_tokens // 4)
    text_rows = -(-text_own // TEXT_TILE) * TEXT_TILE
    pool_rows = -(-text_own // POOL_TILE) * POOL_TILE
    width_here = w_ada.shape[-1]
    ada_rows = w_ada.shape[1]
    heads_here = w_qkv.shape[-1] // HEAD_DIM

    def blocks_of(weight):
        return [weight[stream].astype(LOW).reshape(weight.shape[1], -1) for stream in range(2)]

    up_blocks, down_blocks = blocks_of(w_up), blocks_of(w_down)

    units = up_blocks[1].shape[1] // size
    text_up = lax.all_to_all(
        up_blocks[1].reshape(-1, size, units), "dp", split_axis=1, concat_axis=0, tiled=True
    ).reshape(width, units)
    text_down = down_blocks[1]

    def pool_start(rows):
        copies = jnp.broadcast_to(rows[None, :pool_rows], (size, pool_rows, width))
        rows = lax.all_to_all(copies, "dp", split_axis=0, concat_axis=0, tiled=True)
        return rows.reshape(-1, width)

    def unpool_end(part):
        part = part.astype(LOW).reshape(size, pool_rows, width)
        part = lax.all_to_all(part, "dp", split_axis=0, concat_axis=0, tiled=True)
        total = jnp.sum(part.astype(WIDE), axis=0)
        return jnp.pad(total, ((0, text_rows - pool_rows), (0, 0)))

    cond_low = jax.nn.silu(cond).astype(LOW)
    cond_rows = lax.all_to_all(
        cond_low.reshape(seqs, ada_rows), "dp", split_axis=0, concat_axis=0, tiled=True
    )
    ada_low = w_ada.astype(LOW)
    mod_parts = jnp.einsum("nd,sdkf->nskf", cond_rows, ada_low, preferred_element_type=WIDE)
    mod_parts = lax.all_to_all(mod_parts, "dp", split_axis=0, concat_axis=0, tiled=True)
    modulation = lax.all_gather(jnp.sum(mod_parts, axis=0), "tensor", axis=2, tiled=True)

    def mod_row(stream, which):
        return modulation[stream, which][None, :]

    def own_text(rows):
        padded = jnp.pad(rows, ((0, 4 * text_own - text_tokens), (0, 0)))
        own = lax.dynamic_slice_in_dim(padded, index * text_own, text_own, 0)
        return jnp.pad(own, ((0, text_rows - text_own), (0, 0)))

    split_at = 4 * image_rows
    places = jnp.arange(4 * text_rows)
    token = ((places // text_rows) ^ index) * text_own + places % text_rows
    is_key = (places % text_rows < text_own) & (token < text_tokens)
    bias = jnp.where(is_key, 0.0, -1e30).astype(WIDE)[None, :]

    streams = [image[0].astype(WIDE), own_text(text[0]).astype(WIDE)]
    cotangent = [grad_image[0].astype(WIDE), own_text(grad_text[0]).astype(WIDE)]
    normed_in = [layer_norm(residual) for residual in streams]
    first_in = [
        (normed_in[s] * (1.0 + mod_row(s, 1)) + mod_row(s, 0)).astype(LOW) for s in range(2)
    ]
    ffn_grad = [(mod_row(s, 5) * cotangent[s]).astype(LOW) for s in range(2)]
    moved = [gather_start(first_in[s]) for s in range(2)]
    pooled_grad = pool_start(ffn_grad[1])
    ring = functools.partial(beside, gather_dp)
    found, held = ring(
        blocks_of(w_qkv) + blocks_of(w_out),
        size,
        1,
        first_in + [ffn_grad[1]],
        [*moved[0], *moved[1], pooled_grad, ffn_grad[0]],
    )
    qkv_full, out_full = found[:2], found[2:]
    pooled_grad, image_ffn_grad = held[4:]
    attn_rows = [
        gather_end(first_in[0], held[0], held[1]),
        gather_end(first_in[1], held[2], held[3]),
    ]
    joint = jnp.concatenate(
        [dot(attn_rows[s], qkv_full[s], NN).astype(LOW) for s in range(2)], axis=0
    )
    ffn_moved = gather_start(image_ffn_grad)
    text_ffn_moved = gather_start(pooled_grad)
    if size == RING:
        mixed, log_total, (up_full,) = attend(
            joint, bias, split_at, heads_here, [up_blocks[0]], 2, (4,)
        )
    else:
        mixed, log_total, _ = attend(joint, bias, split_at, heads_here, [], 0, ())
        (up_full,) = gather_dp([up_blocks[0]], size, 2)
    mixed, *ffn_moved = lax.optimization_barrier((mixed, *ffn_moved, *text_ffn_moved))
    mixed_rows = [mixed[:split_at], mixed[split_at:]]
    ffn_rows = gather_end(image_ffn_grad, *ffn_moved[:2])
    text_ffn_rows = gather_end(pooled_grad, *ffn_moved[2:])
    branches = [None, None]
    here, there = scatter_start(dot(mixed_rows[0], out_full[0], NN))
    branches[1] = scatter_rows(dot(mixed_rows[1], out_full[1], NN))
    far = lax.ppermute(there, "tensor", CHIP)
    branches[0] = here + far.astype(WIDE)
    middle = [streams[s] + mod_row(s, 2) * branches[s] for s in range(2)]
    normed_mid = [layer_norm(residual) for residual in middle]
    second_in = [
        (normed_mid[s] * (1.0 + mod_row(s, 4)) + mod_row(s, 3)).astype(LOW) for s in range(2)
    ]
    moved = gather_start(second_in[0])
    pooled_in = pool_start(second_in[1])
    (down_full,), (*moved, pooled_in) = ring(
        [down_blocks[0]], size, 3, second_in, [*moved, pooled_in]
    )
    mlp_rows = gather_end(second_in[0], *moved)
    text_moved = gather_start(pooled_in)

    def gelu_back(pre_act, hidden_grad):
        return jax.vjp(gelu_tanh, pre_act)[1](hidden_grad)[0].astype(LOW)

    pre_act = dot(mlp_rows, up_full, NN)
    hidden = gelu_tanh(pre_act).astype(LOW)
    pre_grad = gelu_back(pre_act, dot(ffn_rows, down_full, NT))
    here, there = scatter_start(dot(pre_grad, up_full, NT))
    far = lax.ppermute(there, "tensor", CHIP)
    down_grad = dot(hidden, ffn_rows, TN).astype(LOW)
    far, there, down_grad, *text_moved = lax.optimization_barrier(
        (far, there, down_grad, *text_moved)
    )
    second_grad, ffn = [None, None], [None, None]
    middle_grad, branch_grad = [None, None], [None, None]

    def middle_back(s):
        wide = second_grad[s] * (1.0 + mod_row(s, 4))
        middle_grad[s] = cotangent[s] + jax.vjp(layer_norm, middle[s])[1](wide)[0]
        branch_grad[s] = (mod_row(s, 2) * middle_grad[s]).astype(LOW)

    second_grad[0] = here + far.astype(WIDE)
    middle_back(0)
    moved = gather_start(branch_grad[0])
    text_mlp_rows = gather_end(pooled_in, *text_moved)
    text_pre_act = dot(text_mlp_rows, text_up, NN)
    text_hidden = gelu_tanh(text_pre_act).astype(LOW)
    text_pre_grad = gelu_back(text_pre_act, dot(text_ffn_rows, text_down, NT))
    text_here, text_there = scatter_start(dot(text_pre_grad, text_up, NT))
    text_far = lax.ppermute(text_there, "tensor", CHIP)
    up_grad = dot(mlp_rows, pre_grad, TN).astype(LOW)
    up_grad, text_far = lax.optimization_barrier((up_grad, text_far))
    second_grad[1] = unpool_end(text_here + text_far.astype(WIDE))
    here, there = scatter_start(dot(hidden, down_full, NN))
    moved = lax.optimization_barrier((*moved, there))[:2]
    branch_rows = [gather_end(branch_grad[0], *moved), None]
    middle_back(1)
    branch_rows[1] = gather_rows(branch_grad[1])
    far = lax.ppermute(there, "tensor", CHIP)
    text_here, text_there = scatter_start(dot(text_hidden, text_down, NN))
    text_far = lax.ppermute(text_there, "tensor", CHIP)
    mixed_grad = jnp.concatenate(
        [dot(branch_rows[s], out_full[s], NT).astype(LOW) for s in range(2)], axis=0
    )
    if size == RING:
        grads, (down_sum, up_sum) = attend_back(
            joint, bias, mixed, mixed_grad, log_total, split_at, heads_here,
            [down_grad, up_grad], 4, (3, 5),
        )
    else:
        grads, _ = attend_back(
            joint, bias, mixed, mixed_grad, log_total, split_at, heads_here, [], 0, ()
        )
        down_sum, up_sum = scatter_dp([down_grad, up_grad], size, 4)
    joint_grad = jnp.concatenate(grads, axis=1)
    joint_grad, far, text_far = lax.optimization_barrier((joint_grad, far, text_far))
    ffn[0] = here + far.astype(WIDE)
    ffn[1] = unpool_end(text_here + text_far.astype(WIDE))
    joint_rows = [joint_grad[:split_at], joint_grad[split_at:]]
    here, there = scatter_start(dot(joint_rows[0], qkv_full[0], NT))
    text_first = scatter_rows(dot(joint_rows[1], qkv_full[1], NT))
    far = lax.ppermute(there, "tensor", CHIP)
    qkv_grad = [dot(attn_rows[s], joint_rows[s], TN).astype(LOW) for s in range(2)]
    out_grad = [dot(mixed_rows[s], branch_rows[s], TN).astype(LOW) for s in range(2)]
    rest_sum, (far, text_first, ffn[1]) = beside(
        scatter_dp,
        qkv_grad + out_grad, size, 5, [there], [far, text_first, ffn[1]]
    )
    first_grad = [here + far.astype(WIDE), text_first]
    text_down_grad = dot(text_hidden, text_ffn_rows, TN)
    text_up_grad = lax.all_to_all(
        dot(text_mlp_rows, text_pre_grad, TN).astype(LOW).reshape(size, -1, units),
        "dp", split_axis=0, concat_axis=2, tiled=True,
    ).reshape(-1, size * units).astype(WIDE)
    results = [(middle[s] + mod_row(s, 5) * ffn[s]).astype(LOW) for s in range(2)]
    input_grad = [
        middle_grad[s]
        + jax.vjp(layer_norm, streams[s])[1](first_grad[s] * (1.0 + mod_row(s, 1)))[0]
        for s in range(2)
    ]
    mod_terms = jnp.stack(
        [
            jnp.stack(
                [
                    jnp.sum(first_grad[s], axis=0),
                    jnp.sum(first_grad[s] * normed_in[s], axis=0),
                    jnp.sum(middle_grad[s] * branches[s], axis=0),
                    jnp.sum(second_grad[s], axis=0),
                    jnp.sum(second_grad[s] * normed_mid[s], axis=0),
                    jnp.sum(cotangent[s] * ffn[s], axis=0),
                ]
            )
            for s in range(2)
        ]
    )
    mod_split = mod_terms.reshape(2, 6, 4, width_here).transpose(2, 0, 1, 3)
    mod_sum = jnp.sum(
        lax.all_to_all(mod_split, "tensor", split_axis=0, concat_axis=0, tiled=True), axis=0
    )
    shift_grad = mod_sum[:, 3]
    mod_low = jnp.broadcast_to(mod_sum.astype(LOW)[None], (seqs,) + mod_sum.shape)
    mod_grad = lax.all_to_all(mod_low, "dp", split_axis=0, concat_axis=0, tiled=True)
    ada_grad = jnp.einsum("nd,nskf->sdkf", cond_rows, mod_grad, preferred_element_type=WIDE)
    act_parts = jnp.einsum("nskf,sdkf->nd", mod_grad, ada_low, preferred_element_type=WIDE)
    act_parts = lax.all_to_all(act_parts, "dp", split_axis=0, concat_axis=0, tiled=True)
    act_grad = lax.psum(act_parts.reshape(1, width), "tensor")
    cond_grad = jax.vjp(jax.nn.silu, cond)[1](act_grad)[0]
    text_out, text_grad = results[1], input_grad[1]

    def whole_text(rows):
        blocks = lax.all_gather(rows, "tensor", axis=0)
        return blocks[:, :text_own].reshape(4 * text_own, width)[:text_tokens][None]

    down_sum = jnp.stack([down_sum, text_down_grad])
    up_sum = jnp.stack([up_sum, text_up_grad])
    qkv_sum, out_sum = jnp.stack(rest_sum[:2]), jnp.stack(rest_sum[2:])

    return (
        results[0][None],
        whole_text(text_out),
        input_grad[0][None],
        whole_text(text_grad),
        cond_grad,
        shift_grad[None],
        ada_grad,
        qkv_sum.reshape(w_qkv.shape),
        out_sum.reshape(w_out.shape),
        up_sum,
        down_sum,
    )


def solution(mesh):
    size = mesh.shape["dp"]

    def step(*args):
        return local(size, *args)

    return jax.shard_map(
        step,
        mesh=mesh,
        in_specs=(
            P("dp", "tensor", None),
            P("dp", None, None),
            P("dp", None),
            P(None, "dp", None, "tensor"),
            P(None, "dp", None, "tensor"),
            P(None, ("tensor", "dp"), None),
            P(None, "dp", "tensor"),
            P(None, ("tensor", "dp"), None),
            P("dp", "tensor", None),
            P("dp", None, None),
        ),
        out_specs=(
            P("dp", "tensor", None),
            P("dp", None, None),
            P("dp", "tensor", None),
            P("dp", None, None),
            P("dp", None),
            P("dp", None, "tensor"),
            P(None, "dp", None, "tensor"),
            P(None, "dp", None, "tensor"),
            P(None, ("tensor", "dp"), None),
            P(None, "dp", "tensor"),
            P(None, ("tensor", "dp"), None),
        ),
        check_vma=False,
    )
```

```python
import functools

import jax
import jax.numpy as jnp
from jax import lax
from jax.experimental import pallas as pl
from jax.experimental.pallas import tpu as pltpu
from jax.sharding import PartitionSpec as P

HEAD_DIM = 64
EPS = 1e-06
LOW = jnp.bfloat16
WIDE = jnp.float32
TEXT_TILE = 64
POOL_TILE = 8
LANES = 128
NT, NN, TN = ((1,), (1,)), ((1,), (0,)), ((0,), (0,))


def dot(left, right, dims):
    return lax.dot_general(left, right, (dims, ((), ())), preferred_element_type=WIDE)


def layer_norm(values):
    average = jnp.mean(values, axis=-1, keepdims=True)
    centred = values - average
    spread = jnp.mean(centred * centred, axis=-1, keepdims=True)
    return centred * lax.rsqrt(spread + EPS)


def gelu_tanh(values):
    return jax.nn.gelu(values, approximate=True)


MESH = pl.DeviceIdType.MESH
RING = 8


def ring_dp(place):
    place = place % RING
    return 2 * place + (place // (RING // 2)) * (2 * RING - 1 - 4 * place)


def ring_place():
    index = lax.axis_index("dp")
    return index // 2 + (index % 2) * (RING - 1 - 2 * (index // 2))


def ring_sides(place):
    tensor = lax.axis_index("tensor")
    return (ring_dp(place + 1), tensor), (ring_dp(place + RING - 1), tensor)


def meet(sides):
    barrier = pltpu.get_barrier_semaphore()
    for side in sides:
        pl.semaphore_signal(barrier, inc=1, device_id=side, device_id_type=MESH)
    pl.semaphore_wait(barrier, len(sides))


def half_of(rows, columns, way):
    if rows // 2 % 16 == 0:
        return way * (rows // 2), rows // 2, 0, columns
    return 0, rows, way * (columns // 2), columns // 2


class GatherRing:
    STEPS = RING // 2

    def __init__(self, blocks, fulls, sems):
        self.blocks, self.fulls = blocks, fulls
        self.own_sem, self.send_sem, self.recv_sem = sems
        self.place = ring_place()
        self.sides = ring_sides(self.place)

    @staticmethod
    def scratch(count):
        steps = RING // 2
        return [
            pltpu.SemaphoreType.DMA((count,)),
            pltpu.SemaphoreType.DMA((count, 2, steps)),
            pltpu.SemaphoreType.DMA((count, 2, steps)),
        ]

    def copy(self, i, way, step):
        rows, columns = self.blocks[i].shape
        at = self.place + (RING - step if way == 0 else step)
        top, high, left, wide = 0, rows, 0, columns
        if step == self.STEPS - 1:
            top, high, left, wide = half_of(rows, columns, way)
        there = self.fulls[i].at[pl.ds(ring_dp(at) * rows + top, high), pl.ds(left, wide)]
        here = there if step else self.blocks[i]
        return pltpu.make_async_remote_copy(
            src_ref=here,
            dst_ref=there,
            send_sem=self.send_sem.at[i, way, step],
            recv_sem=self.recv_sem.at[i, way, step],
            device_id=self.sides[way],
            device_id_type=MESH,
        )

    def own(self, i):
        rows = self.blocks[i].shape[0]
        start = ring_dp(self.place) * rows
        return pltpu.make_async_copy(
            self.blocks[i], self.fulls[i].at[pl.ds(start, rows)], self.own_sem.at[i]
        )

    def start(self):
        for i in range(len(self.blocks)):
            for way in range(2):
                self.copy(i, way, 0).start()
            self.own(i).start()

    def step(self, step):
        for i in range(len(self.blocks)):
            for way in range(2):
                self.copy(i, way, step - 1).wait_recv()
                if step < self.STEPS:
                    self.copy(i, way, step).start()

    def end(self):
        for i in range(len(self.blocks)):
            self.own(i).wait()
            for way in range(2):
                for step in range(self.STEPS):
                    self.copy(i, way, step).wait_send()


class ScatterRing:
    STEPS = RING - 1

    def __init__(self, grads, sums, scratch):
        self.grads, self.sums = grads, sums
        count = len(grads)
        self.mine, self.got = scratch[:count], scratch[count : 2 * count]
        self.mine_sem, self.send_sem, self.recv_sem = scratch[2 * count :]
        self.place = ring_place()
        self.sides = ring_sides(self.place)

    @staticmethod
    def scratch(shapes):
        sizes = [half_of(rows // RING, columns, 0) for rows, columns in shapes]
        halves = [(2, RING, high, wide) for _, high, _, wide in sizes]
        gots = [(2, RING - 1, high, wide) for _, high, _, wide in sizes]
        count = len(shapes)
        return [
            *[pltpu.VMEM(shape, LOW) for shape in halves],
            *[pltpu.VMEM(shape, LOW) for shape in gots],
            pltpu.SemaphoreType.DMA((count, 2, RING)),
            pltpu.SemaphoreType.DMA((count, 2, RING - 1)),
            pltpu.SemaphoreType.DMA((count, 2, RING - 1)),
        ]

    def load(self, i, way, step):
        rows, columns = self.grads[i].shape[0] // RING, self.grads[i].shape[1]
        at = self.place + (2 * RING - step - 1 if way == 0 else step + 1)
        top, high, left, wide = half_of(rows, columns, way)
        return pltpu.make_async_copy(
            self.grads[i].at[pl.ds(ring_dp(at) * rows + top, high), pl.ds(left, wide)],
            self.mine[i].at[way, step],
            self.mine_sem.at[i, way, step],
        )

    def copy(self, i, way, step):
        return pltpu.make_async_remote_copy(
            src_ref=self.mine[i].at[way, step],
            dst_ref=self.got[i].at[way, step],
            send_sem=self.send_sem.at[i, way, step],
            recv_sem=self.recv_sem.at[i, way, step],
            device_id=self.sides[way],
            device_id_type=MESH,
        )

    def load_all(self):
        for step in range(RING):
            for i in range(len(self.grads)):
                for way in range(2):
                    self.load(i, way, step).start()

    def start(self):
        for i in range(len(self.grads)):
            for way in range(2):
                self.load(i, way, 0).wait()
                self.copy(i, way, 0).start()

    def step(self, step):
        for i in range(len(self.grads)):
            rows, columns = self.grads[i].shape[0] // RING, self.grads[i].shape[1]
            for way in range(2):
                top, high, left, wide = half_of(rows, columns, way)
                self.load(i, way, step).wait()
                self.copy(i, way, step - 1).wait_recv()
                total = self.mine[i][way, step].astype(WIDE) + self.got[i][way, step - 1].astype(WIDE)
                if step < self.STEPS:
                    self.mine[i][way, step] = total.astype(LOW)
                    self.copy(i, way, step).start()
                else:
                    self.sums[i][pl.ds(top, high), pl.ds(left, wide)] = total

    def end(self):
        for i in range(len(self.grads)):
            for way in range(2):
                for step in range(self.STEPS):
                    self.copy(i, way, step).wait_send()


ANY = pl.BlockSpec(memory_space=pl.ANY)
WHOLE = pl.BlockSpec(memory_space=pltpu.VMEM)
VMEM_LIMIT = 56 << 20


def gather_kernel(count, *refs):
    ring = GatherRing(refs[:count], refs[count : 2 * count], refs[2 * count :])
    meet(ring.sides)
    ring.start()
    for step in range(1, ring.STEPS + 1):
        ring.step(step)
    ring.end()


def gather_ring(blocks, ident):
    count = len(blocks)
    return pl.pallas_call(
        functools.partial(gather_kernel, count),
        out_shape=[
            jax.ShapeDtypeStruct((RING * block.shape[0], block.shape[1]), block.dtype)
            for block in blocks
        ],
        in_specs=[ANY] * count,
        out_specs=[ANY] * count,
        scratch_shapes=GatherRing.scratch(count),
        compiler_params=pltpu.CompilerParams(
            collective_id=ident, has_side_effects=True, vmem_limit_bytes=VMEM_LIMIT
        ),
        name="gather_ring",
    )(*blocks)


def scatter_kernel(count, *refs):
    ring = ScatterRing(refs[:count], refs[count : 2 * count], refs[2 * count :])
    ring.load_all()
    meet(ring.sides)
    ring.start()
    for step in range(1, ring.STEPS + 1):
        ring.step(step)
    ring.end()


def scatter_ring(grads, ident):
    count = len(grads)
    return pl.pallas_call(
        functools.partial(scatter_kernel, count),
        out_shape=[
            jax.ShapeDtypeStruct((grad.shape[0] // RING, grad.shape[1]), WIDE) for grad in grads
        ],
        in_specs=[ANY] * count,
        out_specs=[WHOLE] * count,
        scratch_shapes=ScatterRing.scratch([grad.shape for grad in grads]),
        compiler_params=pltpu.CompilerParams(
            collective_id=ident, has_side_effects=True, vmem_limit_bytes=VMEM_LIMIT
        ),
        name="scatter_ring",
    )(*grads)


def gather_dp(blocks, size, ident):
    if size == RING:
        return gather_ring(blocks, ident)
    return [lax.all_gather(block, "dp", axis=0, tiled=True) for block in blocks]


def scatter_dp(grads, size, ident):
    if size == RING:
        return scatter_ring(grads, ident)
    return [
        lax.psum_scatter(grad, "dp", scatter_dimension=0, tiled=True).astype(WIDE)
        for grad in grads
    ]


def beside(ring, blocks, size, ident, before, after):
    blocks = lax.optimization_barrier(tuple(blocks) + tuple(before))[: len(blocks)]
    found = tuple(ring(list(blocks), size, ident))
    held = lax.optimization_barrier(found + tuple(after))
    return held[: len(found)], held[len(found) :]


def ring_to_dp(place, size):
    return jnp.where(place < size // 2, 2 * place, 2 * (size - 1 - place) + 1)


def dp_to_ring(index, size):
    return jnp.where(index % 2 == 0, index // 2, size - 1 - index // 2)


def ring_pairs(size, step):
    order = list(range(0, size, 2)) + list(range(size - 1, 0, -2))
    return [(order[p], order[(p + step) % size]) for p in range(size)]


class GatherSteps:
    def __init__(self, blocks, size):
        self.size, self.step = size, 0
        self.place = dp_to_ring(lax.axis_index("dp"), size)
        if size != 8:
            self.payload = ()
            self.fulls = [lax.all_gather(block, "dp", axis=0, tiled=True) for block in blocks]
            return
        self.fulls = [
            jnp.zeros((size * block.shape[0],) + block.shape[1:], block.dtype) for block in blocks
        ]
        self.payload = tuple(blocks) + tuple(blocks)
        for i, block in enumerate(blocks):
            self.put(i, block, self.place, 0)

    def put(self, i, piece, at, offset):
        rows = self.fulls[i].shape[0] // self.size
        start = ring_to_dp(at % self.size, self.size) * rows + offset
        self.fulls[i] = lax.dynamic_update_slice_in_dim(self.fulls[i], piece, start, 0)

    def launch(self, payload):
        self.step += 1
        count = len(payload) // 2
        if self.step == self.size // 2:
            payload = [piece[: piece.shape[0] // 2] for piece in payload[:count]] + [
                piece[piece.shape[0] // 2 :] for piece in payload[count:]
            ]
        return tuple(
            lax.ppermute(piece, "dp", ring_pairs(self.size, 1 if i < count else -1))
            for i, piece in enumerate(payload)
        )

    def land(self, got):
        count = len(got) // 2
        self.payload = got
        for i, piece in enumerate(got):
            direction = -1 if i < count else 1
            half = self.step == self.size // 2 and i >= count
            at = self.place + direction * self.step + self.size
            self.put(i % count, piece, at, piece.shape[0] if half else 0)


class Line:
    def __init__(self):
        self.jobs, self.flying, self.job = [], (), None

    def add(self, job, steps):
        if job.size == 8:
            self.jobs += [job] * steps

    def beat(self, *values):
        count, flown = len(values), len(self.flying)
        fresh = ()
        if self.jobs and self.jobs[0] is not self.job:
            fresh = tuple(self.jobs[0].payload)
        held = tuple(values) + tuple(self.flying) + fresh
        if held:
            held = lax.optimization_barrier(held)
        values = held[:count]
        if flown:
            self.job.land(held[count : count + flown])
        self.flying = ()
        if self.jobs:
            job = self.jobs.pop(0)
            self.flying = job.launch(job.payload if job is self.job else held[count + flown :])
            self.job = job
        return values[0] if count == 1 else values

    def finish(self, job):
        while job in self.jobs or (self.flying and self.job is job):
            self.beat()
        return job.fulls


CORE = [(i, i ^ 1) for i in range(4)]
CHIP = [(i, i ^ 2) for i in range(4)]


def gather_start(own):
    near = lax.ppermute(own, "tensor", CORE)
    far = lax.ppermute(own, "tensor", CHIP)
    return near, far


def gather_end(own, near, far):
    last = lax.ppermute(far, "tensor", CORE)
    return jnp.concatenate([own, near, far, last], axis=0)


def gather_rows(own):
    return gather_end(own, *gather_start(own))


def scatter_start(partial):
    rows = partial.shape[0] // 4
    low = partial.astype(LOW)
    part = [low[b * rows : (b + 1) * rows] for b in range(4)]
    sent = lax.ppermute(jnp.concatenate([part[1], part[3]]), "tensor", CORE)
    here = part[0].astype(WIDE) + sent[:rows].astype(WIDE)
    return here, (part[2].astype(WIDE) + sent[rows:].astype(WIDE)).astype(LOW)


def scatter_rows(partial):
    here, there = scatter_start(partial)
    return here + lax.ppermute(there, "tensor", CHIP).astype(WIDE)


def tensor_peer(hop):
    index = lax.axis_index("tensor")
    if hop == 1:
        return index + 1 - 2 * (index % 2)
    return (index + 2) % 4 if hop == 2 else 3 - index


def tail_kernel(columns, *refs):
    here, there, text_first, scale, other, x_image, x_text, mid_image, mid_text = refs[:9]
    grads, refs = refs[9:11], refs[11:]
    image_grad, text_grad, mod_sum, mod_all, *sums = refs[:6]
    far, terms, parts, low, slots, far_sem, part_sem, slot_sem = refs[6:14]
    ring = ScatterRing(grads, sums, refs[14:])
    me, index = lax.axis_index("dp"), lax.axis_index("tensor")
    far_copy = pltpu.make_async_remote_copy(
        src_ref=there, dst_ref=far, send_sem=far_sem.at[0], recv_sem=far_sem.at[1],
        device_id=(me, tensor_peer(2)), device_id_type=MESH,
    )

    def part_copy(hop):
        peer = tensor_peer(hop)
        start = pl.multiple_of(peer * columns, LANES)
        return pltpu.make_async_remote_copy(
            src_ref=terms.at[:, pl.ds(start, columns)], dst_ref=parts.at[hop - 1],
            send_sem=part_sem.at[0, hop - 1], recv_sem=part_sem.at[1, hop - 1],
            device_id=(me, peer), device_id_type=MESH,
        )

    def slot_copy(hop):
        return pltpu.make_async_remote_copy(
            src_ref=low, dst_ref=slots.at[me],
            send_sem=slot_sem.at[0, hop - 1], recv_sem=slot_sem.at[1, hop - 1],
            device_id=((me + hop) % RING, index), device_id_type=MESH,
        )

    def rows_back(first, x, middle, gain):
        x = x.astype(WIDE)
        centred = x - jnp.mean(x, axis=-1, keepdims=True)
        spread = lax.rsqrt(jnp.mean(centred * centred, axis=-1, keepdims=True) + EPS)
        normed = centred * spread
        wide = first * gain
        inner = jnp.mean(wide, axis=-1, keepdims=True)
        cross = jnp.mean(wide * normed, axis=-1, keepdims=True)
        sums = jnp.sum(first, axis=0, keepdims=True), jnp.sum(first * normed, axis=0, keepdims=True)
        return middle + (wide - inner - normed * cross) * spread, *sums

    ring.load_all()
    meet(
        [(me, tensor_peer(hop)) for hop in (1, 2, 3)]
        + [((me + hop) % RING, index) for hop in range(1, RING)]
    )
    far_copy.start()
    ring.start()
    ring.step(1)
    far_copy.wait()
    terms[...] = other[...]
    chunk = 64

    def image_chunk(at, totals):
        rows = pl.ds(pl.multiple_of(at * chunk, chunk), chunk)
        first = here[rows] + far[rows].astype(WIDE)
        out, shift, gain = rows_back(first, x_image[rows], mid_image[rows], scale[0:1])
        image_grad[rows] = out
        return totals[0] + shift, totals[1] + gain

    zero = jnp.zeros((1, here.shape[1]), WIDE)
    shift, gain = lax.fori_loop(0, here.shape[0] // chunk, image_chunk, (zero, zero))
    terms[0:1] = shift
    terms[1:2] = gain
    ring.step(2)
    out, shift, gain = rows_back(text_first[...], x_text[...], mid_text[...], scale[1:2])
    text_grad[...] = out
    terms[6:7] = shift
    terms[7:8] = gain
    for hop in (1, 2, 3):
        part_copy(hop).start()
    ring.step(3)
    for hop in (1, 2, 3):
        part_copy(hop).wait()
    own = terms[:, pl.ds(pl.multiple_of(index * columns, LANES), columns)]
    total = own + parts[0] + parts[1] + parts[2]
    mod_sum[...] = total
    low[...] = total.astype(LOW)
    slots[pl.ds(me, 1)] = total.astype(LOW)[None]
    for hop in range(1, RING):
        slot_copy(hop).start()
    ring.step(4)
    ring.step(5)
    for hop in range(1, RING):
        slot_copy(hop).wait()
    mod_all[...] = slots[...]
    ring.step(6)
    ring.step(7)
    ring.end()


def tail_ring(here, there, text_first, scale, other, x, middle, grads, columns, ident):
    width, shapes = here.shape[1], [grad.shape for grad in grads]
    rows, text_rows = here.shape[0], text_first.shape[0]
    found = pl.pallas_call(
        functools.partial(tail_kernel, columns),
        out_shape=[
            jax.ShapeDtypeStruct((rows, width), WIDE),
            jax.ShapeDtypeStruct((text_rows, width), WIDE),
            jax.ShapeDtypeStruct((16, columns), WIDE),
            jax.ShapeDtypeStruct((RING, 16, columns), LOW),
            *[jax.ShapeDtypeStruct((r // RING, c), WIDE) for r, c in shapes],
        ],
        in_specs=[WHOLE] * 9 + [ANY] * len(grads),
        out_specs=[WHOLE] * (4 + len(grads)),
        scratch_shapes=[
            pltpu.VMEM((rows, width), LOW),
            pltpu.VMEM((16, width), WIDE),
            pltpu.VMEM((3, 16, columns), WIDE),
            pltpu.VMEM((16, columns), LOW),
            pltpu.VMEM((RING, 16, columns), LOW),
            pltpu.SemaphoreType.DMA((2,)),
            pltpu.SemaphoreType.DMA((2, 3)),
            pltpu.SemaphoreType.DMA((2, RING - 1)),
            *ScatterRing.scratch(shapes),
        ],
        compiler_params=pltpu.CompilerParams(
            collective_id=ident, has_side_effects=True, vmem_limit_bytes=VMEM_LIMIT
        ),
        name="tail_ring",
    )(here, there, text_first, scale, other, *x, *middle, *grads)
    return found


def head_lanes(head):
    lane = lax.broadcasted_iota(jnp.int32, (1, LANES), 1)
    return (lane < HEAD_DIM) if head == 0 else (lane >= HEAD_DIM)


def attend_pair(split, bias_ref, q_ref, k_ref, v_ref, out_ref, lse_ref):
    scale = HEAD_DIM ** (-0.5)
    bias = bias_ref[...]
    outs, totals = [], []
    for head in range(2):
        mine = head_lanes(head)
        queries = jnp.where(mine, q_ref[...] * scale, 0).astype(LOW)
        image = dot(queries, k_ref[:split], NT)
        text = dot(queries, k_ref[split:], NT) + bias
        top = jnp.maximum(
            jnp.max(image, axis=1, keepdims=True), jnp.max(text, axis=1, keepdims=True)
        )
        image = jnp.exp(image - top).astype(LOW)
        text = jnp.exp(text - top).astype(LOW)
        values = jnp.where(mine, v_ref[...], 1).astype(LOW)
        both = dot(image, values[:split], NN) + dot(text, values[split:], NN)
        sums = pltpu.roll(both, HEAD_DIM, 1)
        outs.append(both / sums)
        totals.append(top + jnp.log(sums))
    first = head_lanes(0)
    out_ref[...] = jnp.where(first, outs[0], outs[1]).astype(out_ref.dtype)
    flipped = jnp.where(first, totals[0], totals[1]).T
    lse_ref[0] = jnp.concatenate([flipped[:4], flipped[HEAD_DIM : HEAD_DIM + 4]], axis=0)


def exchange_sums(part, sent, got, sems, me):
    copy = pltpu.make_async_remote_copy(
        src_ref=sent, dst_ref=got, send_sem=sems.at[0, 0], recv_sem=sems.at[1, 0],
        device_id=(me, tensor_peer(1)), device_id_type=MESH,
    )
    sent[0] = part(1).astype(LOW)
    sent[1] = part(3).astype(LOW)
    copy.start()
    return copy


def middle_kernel(split, chunk, *refs):
    bias_ref, q_ref, k_ref, v_ref, x_image, x_text, mods = refs[:7]
    out_blocks, ffn_blocks, refs = refs[7:9], refs[9:11], refs[11:]
    mixed, lse_ref, *wide_outs, text_in, image_in = refs[:8]
    branch_image, branch_text, mid_image, mid_text = wide_outs
    out_fulls, ffn_fulls, refs = refs[8:10], refs[10:12], refs[12:]
    weights, sent, got, far_sent, far_got, here, mine = refs[:7]
    sems, weight_sem, row_sem, own_sem = refs[7:11]
    first = GatherRing(out_blocks, out_fulls, refs[11:14])
    second = GatherRing(ffn_blocks, ffn_fulls, refs[14:17])
    me = lax.axis_index("dp")
    block = q_ref.shape[0]
    pair, at = pl.program_id(0), pl.program_id(0) * 2 + pl.program_id(1)
    rows = x_image.shape[0]

    @pl.when(at == 0)
    def _():
        meet([*first.sides, *[(me, tensor_peer(hop)) for hop in (1, 2)]])
        first.start()

    for step in range(1, 5):

        @pl.when(at == step)
        def _():
            first.step(step)

    weight_copies = [
        pltpu.make_async_copy(out_fulls[s], weights.at[s], weight_sem.at[s]) for s in range(2)
    ]

    @pl.when(at == 4)
    def _():
        first.end()
        second.start()
        for copy in weight_copies:
            copy.start()

    place = (
        pl.ds(pl.multiple_of(pl.program_id(1) * block, block), block),
        pl.ds(pl.multiple_of(pair * LANES, LANES), LANES),
    )
    attend_pair(split, bias_ref, q_ref, k_ref, v_ref, mixed.at[place], lse_ref)

    @pl.when(at == 2 * pl.num_programs(0) - 1)
    def _():
        for copy in weight_copies:
            copy.wait()
        text_rows = x_text.shape[0]

        def part(b):
            image = dot(mixed[b * rows : (b + 1) * rows], weights[0], NN)
            low = split + b * text_rows
            text = dot(mixed[low : low + text_rows], weights[1], NN)
            return jnp.concatenate([image, text], axis=0)

        near = exchange_sums(part, sent, got, sems, me)
        here[...] = part(0)
        far_sent[...] = part(2).astype(LOW)
        near.wait()
        far_sent[...] = (far_sent[...].astype(WIDE) + got[1].astype(WIDE)).astype(LOW)
        far = pltpu.make_async_remote_copy(
            src_ref=far_sent, dst_ref=far_got, send_sem=sems.at[0, 1], recv_sem=sems.at[1, 1],
            device_id=(me, tensor_peer(2)), device_id_type=MESH,
        )
        far.start()
        here[...] += got[0].astype(WIDE)
        second.step(1)
        far.wait()

        def norm_rows(x, branch, stream):
            middle = x.astype(WIDE) + mods[3 * stream : 3 * stream + 1] * branch
            centred = middle - jnp.mean(middle, axis=-1, keepdims=True)
            spread = lax.rsqrt(jnp.mean(centred * centred, axis=-1, keepdims=True) + EPS)
            gain, shift = mods[3 * stream + 1 : 3 * stream + 2], mods[3 * stream + 2 : 3 * stream + 3]
            return middle, (centred * spread * gain + shift).astype(LOW)

        def image_chunk(i, _):
            some = pl.ds(pl.multiple_of(i * chunk, chunk), chunk)
            branch = here[some] + far_got[some].astype(WIDE)
            branch_image[some] = branch
            middle, low = norm_rows(x_image[some], branch, 0)
            mid_image[some] = middle
            mine[some] = low
            return 0

        lax.fori_loop(0, rows // chunk, image_chunk, 0)

        def row_copy(source, slot, hop, sem):
            return pltpu.make_async_remote_copy(
                src_ref=source, dst_ref=image_in.at[pl.ds(slot * rows, rows)],
                send_sem=row_sem.at[0, sem], recv_sem=row_sem.at[1, sem],
                device_id=(me, tensor_peer(hop)), device_id_type=MESH,
            )

        own = pltpu.make_async_copy(mine, image_in.at[pl.ds(0, rows)], own_sem.at[0])
        to_far, to_near = row_copy(mine, 2, 2, 0), row_copy(mine, 1, 1, 1)
        to_far.start()
        to_near.start()
        own.start()
        branch = here[rows:] + far_got[rows:].astype(WIDE)
        branch_text[...] = branch
        middle, low = norm_rows(x_text[...], branch, 1)
        mid_text[...] = middle
        text_in[...] = low
        second.step(2)
        to_far.wait()
        last = row_copy(image_in.at[pl.ds(2 * rows, rows)], 3, 1, 2)
        last.start()
        second.step(3)
        own.wait()
        to_near.wait()
        last.wait()
        second.step(4)
        second.end()


def middle_ring(joint, bias, x, mods, split, heads, out_blocks, ffn_blocks, ident):
    rows, pairs, block = joint.shape[0], heads // 2, joint.shape[0] // 2
    whole = lambda part: pl.BlockSpec((rows, LANES), lambda h, i: (0, part * pairs + h))
    image_rows, width = x[0].shape
    text_rows = x[1].shape[0]
    both = image_rows + text_rows
    depth = heads * HEAD_DIM
    found = pl.pallas_call(
        functools.partial(middle_kernel, split, 64),
        grid=(pairs, 2),
        in_specs=[
            pl.BlockSpec((1, rows - split), lambda h, i: (0, 0)),
            pl.BlockSpec((block, LANES), lambda h, i: (i, h)),
            whole(1),
            whole(2),
            *[WHOLE] * 3,
            *[ANY] * 4,
        ],
        out_specs=[
            WHOLE,
            pl.BlockSpec((1, 8, block), lambda h, i: (h, 0, i)),
            *[WHOLE] * 5,
            *[ANY] * 5,
        ],
        out_shape=[
            jax.ShapeDtypeStruct((rows, depth), LOW),
            jax.ShapeDtypeStruct((pairs, 8, rows), WIDE),
            *[jax.ShapeDtypeStruct((n, width), WIDE) for n in (image_rows, text_rows) * 2],
            jax.ShapeDtypeStruct((text_rows, width), LOW),
            jax.ShapeDtypeStruct((4 * image_rows, width), LOW),
            *[
                jax.ShapeDtypeStruct((RING * b.shape[0], b.shape[1]), b.dtype)
                for b in (*out_blocks, *ffn_blocks)
            ],
        ],
        scratch_shapes=[
            pltpu.VMEM((2, depth, width), LOW),
            pltpu.VMEM((2, both, width), LOW),
            pltpu.VMEM((2, both, width), LOW),
            pltpu.VMEM((both, width), LOW),
            pltpu.VMEM((both, width), LOW),
            pltpu.VMEM((both, width), WIDE),
            pltpu.VMEM((image_rows, width), LOW),
            pltpu.SemaphoreType.DMA((2, 2)),
            pltpu.SemaphoreType.DMA((2,)),
            pltpu.SemaphoreType.DMA((2, 3)),
            pltpu.SemaphoreType.DMA((1,)),
            *GatherRing.scratch(2),
            *GatherRing.scratch(2),
        ],
        compiler_params=pltpu.CompilerParams(
            collective_id=ident, has_side_effects=True, vmem_limit_bytes=VMEM_LIMIT
        ),
        name="middle_ring",
    )(bias, joint, joint, joint, *x, mods, *out_blocks, *ffn_blocks)
    return found


def attend_kernel(split, count, waits, *refs):
    bias_ref, q_ref, k_ref, v_ref = refs[:4]
    blocks, (out_ref, lse_ref) = refs[4 : 4 + count], refs[4 + count : 6 + count]
    at = pl.program_id(0) * pl.num_programs(1) + pl.program_id(1)
    if count:
        ring = GatherRing(blocks, refs[6 + count : 6 + 2 * count], refs[6 + 2 * count :])

        @pl.when(at == 0)
        def _():
            meet(ring.sides)
            ring.start()

        for step, when in enumerate(waits):

            @pl.when(at == when)
            def _():
                ring.step(step + 1)

    attend_pair(split, bias_ref, q_ref, k_ref, v_ref, out_ref, lse_ref)
    if count:

        @pl.when(at == pl.num_programs(0) * pl.num_programs(1) - 1)
        def _():
            for step in range(len(waits) + 1, ring.STEPS + 1):
                ring.step(step)
            ring.end()


def attend(joint, bias, split, heads, blocks, ident, waits):
    rows, pairs, count, block = joint.shape[0], heads // 2, len(blocks), joint.shape[0] // 2
    whole = lambda part: pl.BlockSpec((rows, LANES), lambda h, i: (0, part * pairs + h))
    extra = dict(collective_id=ident, has_side_effects=True) if count else {}
    found = pl.pallas_call(
        functools.partial(attend_kernel, split, count, waits),
        grid=(pairs, 2),
        in_specs=[
            pl.BlockSpec((1, rows - split), lambda h, i: (0, 0)),
            pl.BlockSpec((block, LANES), lambda h, i: (i, h)),
            whole(1),
            whole(2),
            *[ANY] * count,
        ],
        out_specs=[
            pl.BlockSpec((block, LANES), lambda h, i: (i, h)),
            pl.BlockSpec((1, 8, block), lambda h, i: (h, 0, i)),
            *[ANY] * count,
        ],
        out_shape=[
            jax.ShapeDtypeStruct((rows, heads * HEAD_DIM), LOW),
            jax.ShapeDtypeStruct((pairs, 8, rows), WIDE),
            *[jax.ShapeDtypeStruct((RING * b.shape[0], b.shape[1]), b.dtype) for b in blocks],
        ],
        scratch_shapes=GatherRing.scratch(count) if count else [],
        compiler_params=pltpu.CompilerParams(vmem_limit_bytes=VMEM_LIMIT, **extra),
        name="attend",
    )(bias, joint, joint, joint, *blocks)
    return found[0], found[1], found[2:]


def attend_back_pair(split, refs):
    (bias_ref, q_ref, k_ref, v_ref, o_ref, g_ref, lse_ref, dq_ref, dk_ref, dv_ref, dk_acc, dv_acc) = refs
    step = pl.program_id(1)
    scale = HEAD_DIM ** (-0.5)

    @pl.when(step == 0)
    def _():
        dk_acc[...] = jnp.zeros_like(dk_acc)
        dv_acc[...] = jnp.zeros_like(dv_acc)

    product = (g_ref[...].astype(WIDE) * o_ref[...].astype(WIDE)).T
    bias = bias_ref[...]
    dq = None
    for head in range(2):
        mine = head_lanes(head)
        queries = jnp.where(mine, q_ref[...] * scale, 0).astype(LOW)
        grads = jnp.where(mine, g_ref[...], 0).astype(LOW)
        keys = jnp.where(mine, k_ref[...], 0).astype(LOW)
        own = product[head * HEAD_DIM : (head + 1) * HEAD_DIM]
        delta = jnp.sum(own, axis=0, keepdims=True)
        total = lse_ref[0][4 * head : 4 * head + 1]
        for low, high in ((0, split), (split, k_ref.shape[0])):
            scores = dot(k_ref[low:high], queries, NT)
            if low:
                scores = scores + bias
            probs = jnp.exp(scores - total)
            grad_probs = dot(v_ref[low:high], grads, NT)
            grad_scores = (probs * (grad_probs - delta)).astype(LOW)
            dv_acc[low:high] += dot(probs.astype(LOW), grads, NN)
            dk_acc[low:high] += dot(grad_scores, queries, NN)
            part = dot(grad_scores, keys[low:high], TN)
            dq = part if dq is None else dq + part
    dq_ref[...] = (dq * scale).astype(LOW)

    @pl.when(step == pl.num_programs(1) - 1)
    def _():
        dk_ref[...] = dk_acc[...].astype(LOW)
        dv_ref[...] = dv_acc[...].astype(LOW)


def attend_back_kernel(split, count, waits, *refs):
    ins, rest = refs[:7], refs[7:]
    grads, outs, rest = rest[:count], rest[count : count + 3], rest[count + 3 :]
    sums, accs, rest = rest[:count], rest[count : count + 2], rest[count + 2 :]
    at = pl.program_id(0) * pl.num_programs(1) + pl.program_id(1)
    if count:
        ring = ScatterRing(grads, sums, rest)

        @pl.when(at == 0)
        def _():
            ring.load_all()
            meet(ring.sides)
            ring.start()

        for step, when in enumerate(waits):

            @pl.when(at == when)
            def _():
                ring.step(step + 1)

    attend_back_pair(split, (*ins, *outs, *accs))
    if count:

        @pl.when(at == pl.num_programs(0) * pl.num_programs(1) - 1)
        def _():
            for step in range(len(waits) + 1, ring.STEPS + 1):
                ring.step(step)
            ring.end()


def attend_back(joint, bias, mixed, grad, lse, split, heads, grads, ident, waits):
    rows, pairs, count, block = joint.shape[0], heads // 2, len(grads), joint.shape[0] // 2
    whole = lambda part: pl.BlockSpec((rows, LANES), lambda h, i: (0, part * pairs + h))
    some = pl.BlockSpec((block, LANES), lambda h, i: (i, h))
    extra = dict(collective_id=ident, has_side_effects=True) if count else {}
    found = pl.pallas_call(
        functools.partial(attend_back_kernel, split, count, waits),
        grid=(pairs, 2),
        in_specs=[
            pl.BlockSpec((rows - split, 1), lambda h, i: (0, 0)),
            some,
            whole(1),
            whole(2),
            some,
            some,
            pl.BlockSpec((1, 8, block), lambda h, i: (h, 0, i)),
            *[ANY] * count,
        ],
        out_specs=[some, whole(0), whole(0), *[WHOLE] * count],
        out_shape=[
            *[jax.ShapeDtypeStruct((rows, heads * HEAD_DIM), LOW)] * 3,
            *[jax.ShapeDtypeStruct((g.shape[0] // RING, g.shape[1]), WIDE) for g in grads],
        ],
        scratch_shapes=[
            *[pltpu.VMEM((rows, LANES), WIDE)] * 2,
            *(ScatterRing.scratch([g.shape for g in grads]) if count else []),
        ],
        compiler_params=pltpu.CompilerParams(vmem_limit_bytes=VMEM_LIMIT, **extra),
        name="attend_back",
    )(bias.T, joint, joint, joint, mixed, grad, lse, *grads)
    return found[:3], found[3:]


def local(size, image, text, cond, w_ada, w_qkv, w_out, w_up, w_down, grad_image, grad_text):
    index = lax.axis_index("tensor")
    seqs = size
    image_rows, width = image.shape[1], image.shape[2]
    text_tokens = text.shape[1]
    text_own = -(-text_tokens // 4)
    text_rows = -(-text_own // TEXT_TILE) * TEXT_TILE
    pool_rows = -(-text_own // POOL_TILE) * POOL_TILE
    width_here = w_ada.shape[-1]
    ada_rows = w_ada.shape[1]
    heads_here = w_qkv.shape[-1] // HEAD_DIM

    def blocks_of(weight):
        return [weight[stream].astype(LOW).reshape(weight.shape[1], -1) for stream in range(2)]

    up_blocks, down_blocks = blocks_of(w_up), blocks_of(w_down)

    units = up_blocks[1].shape[1] // size
    text_up = lax.all_to_all(
        up_blocks[1].reshape(-1, size, units), "dp", split_axis=1, concat_axis=0, tiled=True
    ).reshape(width, units)
    text_down = down_blocks[1]

    def pool_start(rows):
        copies = jnp.broadcast_to(rows[None, :pool_rows], (size, pool_rows, width))
        rows = lax.all_to_all(copies, "dp", split_axis=0, concat_axis=0, tiled=True)
        return rows.reshape(-1, width)

    def unpool_end(part):
        part = part.astype(LOW).reshape(size, pool_rows, width)
        part = lax.all_to_all(part, "dp", split_axis=0, concat_axis=0, tiled=True)
        total = jnp.sum(part.astype(WIDE), axis=0)
        return jnp.pad(total, ((0, text_rows - pool_rows), (0, 0)))

    line = Line()
    qkv_steps = GatherSteps(blocks_of(w_qkv), size)
    line.add(qkv_steps, size // 2)
    line.beat()

    cond_low = jax.nn.silu(cond).astype(LOW)
    cond_rows = lax.all_to_all(
        cond_low.reshape(seqs, ada_rows), "dp", split_axis=0, concat_axis=0, tiled=True
    )
    cond_rows = line.beat(cond_rows)
    ada_low = w_ada.astype(LOW)
    mod_parts = jnp.einsum("nd,sdkf->nskf", cond_rows, ada_low, preferred_element_type=WIDE)
    mod_parts = lax.all_to_all(mod_parts, "dp", split_axis=0, concat_axis=0, tiled=True)
    modulation = lax.all_gather(jnp.sum(mod_parts, axis=0), "tensor", axis=2, tiled=True)

    def mod_row(stream, which):
        return modulation[stream, which][None, :]

    def own_text(rows):
        padded = jnp.pad(rows, ((0, 4 * text_own - text_tokens), (0, 0)))
        own = lax.dynamic_slice_in_dim(padded, index * text_own, text_own, 0)
        return jnp.pad(own, ((0, text_rows - text_own), (0, 0)))

    split_at = 4 * image_rows
    places = jnp.arange(4 * text_rows)
    token = ((places // text_rows) ^ index) * text_own + places % text_rows
    is_key = (places % text_rows < text_own) & (token < text_tokens)
    bias = jnp.where(is_key, 0.0, -1e30).astype(WIDE)[None, :]

    streams = [image[0].astype(WIDE), own_text(text[0]).astype(WIDE)]
    cotangent = [grad_image[0].astype(WIDE), own_text(grad_text[0]).astype(WIDE)]
    normed_in = [layer_norm(residual) for residual in streams]
    first_in = [
        (normed_in[s] * (1.0 + mod_row(s, 1)) + mod_row(s, 0)).astype(LOW) for s in range(2)
    ]
    ffn_grad = [(mod_row(s, 5) * cotangent[s]).astype(LOW) for s in range(2)]
    first_in = line.beat(*first_in)
    moved = [gather_start(first_in[s]) for s in range(2)]
    *image_moved, text_near, text_far = line.beat(*moved[0], *moved[1])
    pooled_grad = pool_start(ffn_grad[1])
    attn_rows = [
        gather_end(first_in[0], *image_moved),
        gather_end(first_in[1], text_near, text_far),
    ]
    qkv_full = line.finish(qkv_steps)
    attn_rows = line.beat(*attn_rows)
    joint = jnp.concatenate(
        [dot(attn_rows[s], qkv_full[s], NN).astype(LOW) for s in range(2)], axis=0
    )
    image_ffn_grad = ffn_grad[0]
    ffn_moved = gather_start(image_ffn_grad)
    text_ffn_moved = gather_start(pooled_grad)
    ffn_blocks = [up_blocks[0], down_blocks[0]]
    x_rows = [image[0], own_text(text[0])]
    if size == RING:
        mods = jnp.concatenate(
            [row for s in range(2) for row in (mod_row(s, 2), 1.0 + mod_row(s, 4), mod_row(s, 3))]
            + [jnp.zeros((2, width), WIDE)],
            axis=0,
        )
        found = middle_ring(
            joint, bias, x_rows, mods, split_at, heads_here, blocks_of(w_out), ffn_blocks, 2
        )
        mixed, log_total, *found = found
        branches, middle, text_in, mlp_rows = found[:2], found[2:4], found[4], found[5]
        out_full, up_full, down_full = found[6:8], found[8], found[9]
    else:
        mixed, log_total, _ = attend(joint, bias, split_at, heads_here, [], 0, ())
        *out_full, up_full, down_full = gather_dp(blocks_of(w_out) + ffn_blocks, size, 2)
        branches = [
            scatter_rows(dot(mixed[:split_at], out_full[0], NN)),
            scatter_rows(dot(mixed[split_at:], out_full[1], NN)),
        ]
        middle = [streams[s] + mod_row(s, 2) * branches[s] for s in range(2)]
        second_in = [
            (layer_norm(middle[s]) * (1.0 + mod_row(s, 4)) + mod_row(s, 3)).astype(LOW)
            for s in range(2)
        ]
        mlp_rows, text_in = gather_rows(second_in[0]), second_in[1]
    mixed, *ffn_moved = lax.optimization_barrier((mixed, *ffn_moved, *text_ffn_moved))
    mixed_rows = [mixed[:split_at], mixed[split_at:]]
    ffn_rows = gather_end(image_ffn_grad, *ffn_moved[:2])
    text_ffn_rows = gather_end(pooled_grad, *ffn_moved[2:])
    normed_mid = [layer_norm(residual) for residual in middle]
    pooled_in = pool_start(text_in)
    text_moved = gather_start(pooled_in)

    def gelu_back(pre_act, hidden_grad):
        return jax.vjp(gelu_tanh, pre_act)[1](hidden_grad)[0].astype(LOW)

    pre_act = dot(mlp_rows, up_full, NN)
    hidden = gelu_tanh(pre_act).astype(LOW)
    pre_grad = gelu_back(pre_act, dot(ffn_rows, down_full, NT))
    here, there = scatter_start(dot(pre_grad, up_full, NT))
    far = lax.ppermute(there, "tensor", CHIP)
    down_grad = dot(hidden, ffn_rows, TN).astype(LOW)
    there, down_grad, *text_moved = lax.optimization_barrier((there, down_grad, *text_moved))
    text_mlp_rows = gather_end(pooled_in, *text_moved)
    text_pre_act = dot(text_mlp_rows, text_up, NN)
    text_hidden = gelu_tanh(text_pre_act).astype(LOW)
    text_pre_grad = gelu_back(text_pre_act, dot(text_ffn_rows, text_down, NT))
    text_here, text_there = scatter_start(dot(text_pre_grad, text_up, NT))
    text_far = lax.ppermute(text_there, "tensor", CHIP)
    (down_sum,), (far, text_far) = beside(
        scatter_dp, [down_grad], size, 4, [there, text_there], [far, text_far]
    )
    second_grad, ffn = [None, None], [None, None]
    middle_grad, branch_grad = [None, None], [None, None]

    def middle_back(s):
        wide = second_grad[s] * (1.0 + mod_row(s, 4))
        middle_grad[s] = cotangent[s] + jax.vjp(layer_norm, middle[s])[1](wide)[0]
        branch_grad[s] = (mod_row(s, 2) * middle_grad[s]).astype(LOW)

    second_grad[1] = unpool_end(text_here + text_far.astype(WIDE))
    second_grad[0] = here + far.astype(WIDE)
    middle_back(0)
    moved = gather_start(branch_grad[0])
    up_grad = dot(mlp_rows, pre_grad, TN).astype(LOW)
    here, there = scatter_start(dot(hidden, down_full, NN))
    up_grad, there, second_grad[1], *moved = lax.optimization_barrier(
        (up_grad, there, second_grad[1], *moved)
    )
    middle_back(1)
    text_moved = gather_start(branch_grad[1])
    branch_rows = [gather_end(branch_grad[0], *moved), gather_end(branch_grad[1], *text_moved)]
    out_grad = [dot(mixed_rows[s], branch_rows[s], TN).astype(LOW) for s in range(2)]
    far = lax.ppermute(there, "tensor", CHIP)
    text_here, text_there = scatter_start(dot(text_hidden, text_down, NN))
    text_far = lax.ppermute(text_there, "tensor", CHIP)
    mixed_grad = jnp.concatenate(
        [dot(branch_rows[s], out_full[s], NT).astype(LOW) for s in range(2)], axis=0
    )
    if size == RING:
        grads, (up_sum, *out_sum) = attend_back(
            joint, bias, mixed, mixed_grad, log_total, split_at, heads_here,
            [up_grad] + out_grad, 5, (2, 4),
        )
    else:
        grads, _ = attend_back(
            joint, bias, mixed, mixed_grad, log_total, split_at, heads_here, [], 0, ()
        )
        up_sum, *out_sum = scatter_dp([up_grad] + out_grad, size, 5)
    joint_grad = jnp.concatenate(grads, axis=1)
    joint_grad, far, text_far = lax.optimization_barrier((joint_grad, far, text_far))
    ffn[0] = here + far.astype(WIDE)
    ffn[1] = unpool_end(text_here + text_far.astype(WIDE))
    joint_rows = [joint_grad[:split_at], joint_grad[split_at:]]
    qkv_grad = [dot(attn_rows[s], joint_rows[s], TN).astype(LOW) for s in range(2)]
    here, there = scatter_start(dot(joint_rows[0], qkv_full[0], NT))
    text_first = scatter_rows(dot(joint_rows[1], qkv_full[1], NT))
    results = [(middle[s] + mod_row(s, 5) * ffn[s]).astype(LOW) for s in range(2)]
    text_down_grad = dot(text_hidden, text_ffn_rows, TN)
    text_up_grad = lax.all_to_all(
        dot(text_mlp_rows, text_pre_grad, TN).astype(LOW).reshape(size, -1, units),
        "dp", split_axis=0, concat_axis=2, tiled=True,
    )
    other = []
    for s in range(2):
        other += [
            jnp.zeros((2, width), WIDE),
            jnp.sum(middle_grad[s] * branches[s], axis=0)[None],
            jnp.sum(second_grad[s], axis=0)[None],
            jnp.sum(second_grad[s] * normed_mid[s], axis=0)[None],
            jnp.sum(cotangent[s] * ffn[s], axis=0)[None],
        ]
    other = jnp.concatenate(other + [jnp.zeros((4, width), WIDE)], axis=0)
    if size == RING:
        scale = jnp.concatenate([1.0 + mod_row(s, 1) for s in range(2)], axis=0)
        *input_grad, mod_sum, mod_grad, qkv_image, qkv_text = tail_ring(
            here, there, text_first, scale, other, x_rows, middle_grad, qkv_grad, width_here, 6
        )
        qkv_sums = [qkv_image, qkv_text]
        mod_sum = mod_sum[:12].reshape(2, 6, width_here)
        mod_grad = mod_grad[:, :12].reshape(seqs, 2, 6, width_here)
        mod_grad, text_up_grad = lax.optimization_barrier((mod_grad, text_up_grad))
    else:
        qkv_sums = scatter_dp(qkv_grad, size, 6)
        far = lax.ppermute(there, "tensor", CHIP)
        first_grad = [here + far.astype(WIDE), text_first]
        input_grad, first_terms = [None, None], []
        for s in range(2):
            wide = first_grad[s] * (1.0 + mod_row(s, 1))
            input_grad[s] = middle_grad[s] + jax.vjp(layer_norm, streams[s])[1](wide)[0]
            shift = jnp.sum(first_grad[s], axis=0)
            gain = jnp.sum(first_grad[s] * normed_in[s], axis=0)
            first_terms.append(jnp.stack([shift, gain]))
        mod_terms = other[:12].reshape(2, 6, width).at[:, :2].set(jnp.stack(first_terms))
        mod_split = mod_terms.reshape(2, 6, 4, width_here).transpose(2, 0, 1, 3)
        mod_sum = jnp.sum(
            lax.all_to_all(mod_split, "tensor", split_axis=0, concat_axis=0, tiled=True), axis=0
        )
        mod_low = jnp.broadcast_to(mod_sum.astype(LOW)[None], (seqs,) + mod_sum.shape)
        mod_grad = lax.all_to_all(mod_low, "dp", split_axis=0, concat_axis=0, tiled=True)
    shift_grad = mod_sum[:, 3]
    text_up_grad = text_up_grad.reshape(-1, size * units).astype(WIDE)
    ada_grad = jnp.einsum("nd,nskf->sdkf", cond_rows, mod_grad, preferred_element_type=WIDE)
    act_parts = jnp.einsum("nskf,sdkf->nd", mod_grad, ada_low, preferred_element_type=WIDE)
    act_parts = lax.all_to_all(act_parts, "dp", split_axis=0, concat_axis=0, tiled=True)
    act_grad = lax.psum(act_parts.reshape(1, width), "tensor")
    cond_grad = jax.vjp(jax.nn.silu, cond)[1](act_grad)[0]
    text_out, text_grad = results[1], input_grad[1]

    def whole_text(rows):
        blocks = lax.all_gather(rows, "tensor", axis=0)
        return blocks[:, :text_own].reshape(4 * text_own, width)[:text_tokens][None]

    down_sum = jnp.stack([down_sum, text_down_grad])
    up_sum = jnp.stack([up_sum, text_up_grad])
    qkv_sum, out_sum = jnp.stack(qkv_sums), jnp.stack(out_sum)

    return (
        results[0][None],
        whole_text(text_out),
        input_grad[0][None],
        whole_text(text_grad),
        cond_grad,
        shift_grad[None],
        ada_grad,
        qkv_sum.reshape(w_qkv.shape),
        out_sum.reshape(w_out.shape),
        up_sum,
        down_sum,
    )


def solution(mesh):
    size = mesh.shape["dp"]

    def step(*args):
        return local(size, *args)

    return jax.shard_map(
        step,
        mesh=mesh,
        in_specs=(
            P("dp", "tensor", None),
            P("dp", None, None),
            P("dp", None),
            P(None, "dp", None, "tensor"),
            P(None, "dp", None, "tensor"),
            P(None, ("tensor", "dp"), None),
            P(None, "dp", "tensor"),
            P(None, ("tensor", "dp"), None),
            P("dp", "tensor", None),
            P("dp", None, None),
        ),
        out_specs=(
            P("dp", "tensor", None),
            P("dp", None, None),
            P("dp", "tensor", None),
            P("dp", None, None),
            P("dp", None),
            P("dp", None, "tensor"),
            P(None, "dp", None, "tensor"),
            P(None, "dp", None, "tensor"),
            P(None, ("tensor", "dp"), None),
            P(None, "dp", "tensor"),
            P(None, ("tensor", "dp"), None),
        ),
        check_vma=False,
    )
```

```python
import functools

import jax
import jax.numpy as jnp
from jax import lax
from jax.experimental import pallas as pl
from jax.experimental.pallas import tpu as pltpu
from jax.sharding import PartitionSpec as P

HEAD_DIM = 64
EPS = 1e-06
LOW = jnp.bfloat16
WIDE = jnp.float32
TEXT_TILE = 64
POOL_TILE = 16
LANES = 128
NT, NN, TN = ((1,), (1,)), ((1,), (0,)), ((0,), (0,))


def dot(left, right, dims):
    return lax.dot_general(left, right, (dims, ((), ())), preferred_element_type=WIDE)


def layer_norm(values):
    average = jnp.mean(values, axis=-1, keepdims=True)
    centred = values - average
    spread = jnp.mean(centred * centred, axis=-1, keepdims=True)
    return centred * lax.rsqrt(spread + EPS)


def gelu_tanh(values):
    return jax.nn.gelu(values, approximate=True)


MESH = pl.DeviceIdType.MESH
RING = 8


def ring_dp(place):
    place = place % RING
    return 2 * place + (place // (RING // 2)) * (2 * RING - 1 - 4 * place)


def ring_place():
    index = lax.axis_index("dp")
    return index // 2 + (index % 2) * (RING - 1 - 2 * (index // 2))


def ring_sides(place):
    tensor = lax.axis_index("tensor")
    return (ring_dp(place + 1), tensor), (ring_dp(place + RING - 1), tensor)


def meet(sides):
    barrier = pltpu.get_barrier_semaphore()
    for side in sides:
        pl.semaphore_signal(barrier, inc=1, device_id=side, device_id_type=MESH)
    pl.semaphore_wait(barrier, len(sides))


def half_of(rows, columns, way):
    if rows // 2 % 16 == 0:
        return way * (rows // 2), rows // 2, 0, columns
    return 0, rows, way * (columns // 2), columns // 2


class GatherRing:
    STEPS = RING // 2

    def __init__(self, blocks, fulls, sems):
        self.blocks, self.fulls = blocks, fulls
        self.own_sem, self.send_sem, self.recv_sem = sems
        self.place = ring_place()
        self.sides = ring_sides(self.place)

    @staticmethod
    def scratch(count):
        steps = RING // 2
        return [
            pltpu.SemaphoreType.DMA((count,)),
            pltpu.SemaphoreType.DMA((count, 2, steps)),
            pltpu.SemaphoreType.DMA((count, 2, steps)),
        ]

    def copy(self, i, way, step):
        rows, columns = self.blocks[i].shape
        at = self.place + (RING - step if way == 0 else step)
        top, high, left, wide = 0, rows, 0, columns
        if step == self.STEPS - 1:
            top, high, left, wide = half_of(rows, columns, way)
        there = self.fulls[i].at[pl.ds(ring_dp(at) * rows + top, high), pl.ds(left, wide)]
        here = there if step else self.blocks[i]
        return pltpu.make_async_remote_copy(
            src_ref=here,
            dst_ref=there,
            send_sem=self.send_sem.at[i, way, step],
            recv_sem=self.recv_sem.at[i, way, step],
            device_id=self.sides[way],
            device_id_type=MESH,
        )

    def own(self, i):
        rows = self.blocks[i].shape[0]
        start = ring_dp(self.place) * rows
        return pltpu.make_async_copy(
            self.blocks[i], self.fulls[i].at[pl.ds(start, rows)], self.own_sem.at[i]
        )

    def start(self):
        for i in range(len(self.blocks)):
            for way in range(2):
                self.copy(i, way, 0).start()
            self.own(i).start()

    def step(self, step):
        for i in range(len(self.blocks)):
            for way in range(2):
                self.copy(i, way, step - 1).wait_recv()
                if step < self.STEPS:
                    self.copy(i, way, step).start()

    def end(self):
        for i in range(len(self.blocks)):
            self.own(i).wait()
            for way in range(2):
                for step in range(self.STEPS):
                    self.copy(i, way, step).wait_send()


class ScatterRing:
    STEPS = RING - 1

    def __init__(self, grads, sums, scratch):
        self.grads, self.sums = grads, sums
        count = len(grads)
        self.mine, self.got = scratch[:count], scratch[count : 2 * count]
        self.mine_sem, self.send_sem, self.recv_sem = scratch[2 * count :]
        self.place = ring_place()
        self.sides = ring_sides(self.place)

    @staticmethod
    def scratch(shapes):
        sizes = [half_of(rows // RING, columns, 0) for rows, columns in shapes]
        halves = [(2, RING, high, wide) for _, high, _, wide in sizes]
        gots = [(2, RING - 1, high, wide) for _, high, _, wide in sizes]
        count = len(shapes)
        return [
            *[pltpu.VMEM(shape, LOW) for shape in halves],
            *[pltpu.VMEM(shape, LOW) for shape in gots],
            pltpu.SemaphoreType.DMA((count, 2, RING)),
            pltpu.SemaphoreType.DMA((count, 2, RING - 1)),
            pltpu.SemaphoreType.DMA((count, 2, RING - 1)),
        ]

    def load(self, i, way, step):
        rows, columns = self.grads[i].shape[0] // RING, self.grads[i].shape[1]
        at = self.place + (2 * RING - step - 1 if way == 0 else step + 1)
        top, high, left, wide = half_of(rows, columns, way)
        return pltpu.make_async_copy(
            self.grads[i].at[pl.ds(ring_dp(at) * rows + top, high), pl.ds(left, wide)],
            self.mine[i].at[way, step],
            self.mine_sem.at[i, way, step],
        )

    def copy(self, i, way, step):
        return pltpu.make_async_remote_copy(
            src_ref=self.mine[i].at[way, step],
            dst_ref=self.got[i].at[way, step],
            send_sem=self.send_sem.at[i, way, step],
            recv_sem=self.recv_sem.at[i, way, step],
            device_id=self.sides[way],
            device_id_type=MESH,
        )

    def load_all(self):
        for step in range(RING):
            for i in range(len(self.grads)):
                for way in range(2):
                    self.load(i, way, step).start()

    def start(self):
        for i in range(len(self.grads)):
            for way in range(2):
                self.load(i, way, 0).wait()
                self.copy(i, way, 0).start()

    def step(self, step):
        for i in range(len(self.grads)):
            rows, columns = self.grads[i].shape[0] // RING, self.grads[i].shape[1]
            for way in range(2):
                top, high, left, wide = half_of(rows, columns, way)
                self.load(i, way, step).wait()
                self.copy(i, way, step - 1).wait_recv()
                total = self.mine[i][way, step].astype(WIDE) + self.got[i][way, step - 1].astype(WIDE)
                if step < self.STEPS:
                    self.mine[i][way, step] = total.astype(LOW)
                    self.copy(i, way, step).start()
                else:
                    self.sums[i][pl.ds(top, high), pl.ds(left, wide)] = total

    def end(self):
        for i in range(len(self.grads)):
            for way in range(2):
                for step in range(self.STEPS):
                    self.copy(i, way, step).wait_send()


ANY = pl.BlockSpec(memory_space=pl.ANY)
WHOLE = pl.BlockSpec(memory_space=pltpu.VMEM)
VMEM_LIMIT = 56 << 20


def gather_kernel(count, *refs):
    ring = GatherRing(refs[:count], refs[count : 2 * count], refs[2 * count :])
    meet(ring.sides)
    ring.start()
    for step in range(1, ring.STEPS + 1):
        ring.step(step)
    ring.end()


def gather_ring(blocks, ident):
    count = len(blocks)
    return pl.pallas_call(
        functools.partial(gather_kernel, count),
        out_shape=[
            jax.ShapeDtypeStruct((RING * block.shape[0], block.shape[1]), block.dtype)
            for block in blocks
        ],
        in_specs=[ANY] * count,
        out_specs=[ANY] * count,
        scratch_shapes=GatherRing.scratch(count),
        compiler_params=pltpu.CompilerParams(
            collective_id=ident, has_side_effects=True, vmem_limit_bytes=VMEM_LIMIT
        ),
        name="gather_ring",
    )(*blocks)


def scatter_kernel(count, *refs):
    ring = ScatterRing(refs[:count], refs[count : 2 * count], refs[2 * count :])
    ring.load_all()
    meet(ring.sides)
    ring.start()
    for step in range(1, ring.STEPS + 1):
        ring.step(step)
    ring.end()


def scatter_ring(grads, ident):
    count = len(grads)
    return pl.pallas_call(
        functools.partial(scatter_kernel, count),
        out_shape=[
            jax.ShapeDtypeStruct((grad.shape[0] // RING, grad.shape[1]), WIDE) for grad in grads
        ],
        in_specs=[ANY] * count,
        out_specs=[WHOLE] * count,
        scratch_shapes=ScatterRing.scratch([grad.shape for grad in grads]),
        compiler_params=pltpu.CompilerParams(
            collective_id=ident, has_side_effects=True, vmem_limit_bytes=VMEM_LIMIT
        ),
        name="scatter_ring",
    )(*grads)


def gather_dp(blocks, size, ident):
    if size == RING:
        return gather_ring(blocks, ident)
    return [lax.all_gather(block, "dp", axis=0, tiled=True) for block in blocks]


def scatter_dp(grads, size, ident):
    if size == RING:
        return scatter_ring(grads, ident)
    return [
        lax.psum_scatter(grad, "dp", scatter_dimension=0, tiled=True).astype(WIDE)
        for grad in grads
    ]


def beside(ring, blocks, size, ident, before, after):
    blocks = lax.optimization_barrier(tuple(blocks) + tuple(before))[: len(blocks)]
    found = tuple(ring(list(blocks), size, ident))
    held = lax.optimization_barrier(found + tuple(after))
    return held[: len(found)], held[len(found) :]


CORE = [(i, i ^ 1) for i in range(4)]
CHIP = [(i, i ^ 2) for i in range(4)]


def gather_start(own):
    near = lax.ppermute(own, "tensor", CORE)
    far = lax.ppermute(own, "tensor", CHIP)
    return near, far


def gather_end(own, near, far):
    last = lax.ppermute(far, "tensor", CORE)
    return jnp.concatenate([own, near, far, last], axis=0)


def gather_rows(own):
    return gather_end(own, *gather_start(own))


def scatter_start(partial):
    rows = partial.shape[0] // 4
    low = partial.astype(LOW)
    part = [low[b * rows : (b + 1) * rows] for b in range(4)]
    sent = lax.ppermute(jnp.concatenate([part[1], part[3]]), "tensor", CORE)
    here = part[0].astype(WIDE) + sent[:rows].astype(WIDE)
    return here, (part[2].astype(WIDE) + sent[rows:].astype(WIDE)).astype(LOW)


def scatter_rows(partial):
    here, there = scatter_start(partial)
    return here + lax.ppermute(there, "tensor", CHIP).astype(WIDE)


def tensor_peer(hop):
    index = lax.axis_index("tensor")
    if hop == 1:
        return index + 1 - 2 * (index % 2)
    return (index + 2) % 4 if hop == 2 else 3 - index


def tail_kernel(columns, count, *refs):
    here, there, scale, other, x_image, x_text, mid_image, mid_text, text_out = refs[:9]
    grads, refs = refs[9 : 9 + count], refs[9 + count :]
    image_grad, mod_sum, mod_all, *wholes = refs[:5]
    sums, refs = refs[5 : 5 + count], refs[5 + count :]
    far, text_grad, terms, parts, low, slots, far_sem, part_sem, slot_sem, text_sem = refs[:10]
    ring = ScatterRing(grads, sums, refs[10:])
    me, index = lax.axis_index("dp"), lax.axis_index("tensor")
    far_copy = pltpu.make_async_remote_copy(
        src_ref=there, dst_ref=far, send_sem=far_sem.at[0], recv_sem=far_sem.at[1],
        device_id=(me, tensor_peer(2)), device_id_type=MESH,
    )

    def part_copy(hop):
        peer = tensor_peer(hop)
        start = pl.multiple_of(peer * columns, LANES)
        return pltpu.make_async_remote_copy(
            src_ref=terms.at[:, pl.ds(start, columns)], dst_ref=parts.at[hop - 1],
            send_sem=part_sem.at[0, hop - 1], recv_sem=part_sem.at[1, hop - 1],
            device_id=(me, peer), device_id_type=MESH,
        )

    def slot_copy(hop):
        return pltpu.make_async_remote_copy(
            src_ref=low, dst_ref=slots.at[me],
            send_sem=slot_sem.at[0, hop - 1], recv_sem=slot_sem.at[1, hop - 1],
            device_id=((me + hop) % RING, index), device_id_type=MESH,
        )

    def text_copy(i, hop):
        source = (text_out, text_grad)[i]
        return pltpu.make_async_remote_copy(
            src_ref=source, dst_ref=wholes[i].at[index],
            send_sem=text_sem.at[i, 0, hop], recv_sem=text_sem.at[i, 1, hop],
            device_id=(me, tensor_peer(hop)), device_id_type=MESH,
        )

    def text_own(i):
        source = (text_out, text_grad)[i]
        return pltpu.make_async_copy(source, wholes[i].at[index], text_sem.at[i, 0, 0])

    def rows_back(first, x, middle, gain):
        x = x.astype(WIDE)
        centred = x - jnp.mean(x, axis=-1, keepdims=True)
        spread = lax.rsqrt(jnp.mean(centred * centred, axis=-1, keepdims=True) + EPS)
        normed = centred * spread
        wide = first * gain
        inner = jnp.mean(wide, axis=-1, keepdims=True)
        cross = jnp.mean(wide * normed, axis=-1, keepdims=True)
        sums = jnp.sum(first, axis=0, keepdims=True), jnp.sum(first * normed, axis=0, keepdims=True)
        return middle + (wide - inner - normed * cross) * spread, *sums

    ring.load_all()
    meet(
        [(me, tensor_peer(hop)) for hop in (1, 2, 3)]
        + [((me + hop) % RING, index) for hop in range(1, RING)]
    )
    far_copy.start()
    ring.start()
    ring.step(1)
    far_copy.wait()
    terms[...] = other[...]
    chunk = 64

    def image_chunk(at, totals):
        rows = pl.ds(pl.multiple_of(at * chunk, chunk), chunk)
        first = here[rows] + far[rows].astype(WIDE)
        out, shift, gain = rows_back(first, x_image[rows], mid_image[rows], scale[0:1])
        image_grad[rows] = out
        return totals[0] + shift, totals[1] + gain

    zero = jnp.zeros((1, here.shape[1]), WIDE)
    image_rows = x_image.shape[0]
    shift, gain = lax.fori_loop(0, image_rows // chunk, image_chunk, (zero, zero))
    terms[0:1] = shift
    terms[1:2] = gain
    ring.step(2)
    text_first = here[image_rows:] + far[image_rows:].astype(WIDE)
    out, shift, gain = rows_back(text_first, x_text[...], mid_text[...], scale[1:2])
    text_grad[...] = out
    for i in range(2):
        text_own(i).start()
        for hop in (1, 2, 3):
            text_copy(i, hop).start()
    terms[6:7] = shift
    terms[7:8] = gain
    for hop in (1, 2, 3):
        part_copy(hop).start()
    ring.step(3)
    for hop in (1, 2, 3):
        part_copy(hop).wait()
    own = terms[:, pl.ds(pl.multiple_of(index * columns, LANES), columns)]
    total = own + parts[0] + parts[1] + parts[2]
    mod_sum[...] = total
    low[...] = total.astype(LOW)
    slots[pl.ds(me, 1)] = total.astype(LOW)[None]
    for hop in range(1, RING):
        slot_copy(hop).start()
    ring.step(4)
    ring.step(5)
    for hop in range(1, RING):
        slot_copy(hop).wait()
    mod_all[...] = slots[...]
    ring.step(6)
    for i in range(2):
        text_own(i).wait()
        for hop in (1, 2, 3):
            text_copy(i, hop).wait()
    ring.step(7)
    ring.end()


def tail_ring(here, there, scale, other, x, middle, text_out, grads, columns, ident):
    width, shapes = here.shape[1], [grad.shape for grad in grads]
    rows, text_rows = x[0].shape[0], x[1].shape[0]
    found = pl.pallas_call(
        functools.partial(tail_kernel, columns, len(grads)),
        out_shape=[
            jax.ShapeDtypeStruct((rows, width), WIDE),
            jax.ShapeDtypeStruct((16, columns), WIDE),
            jax.ShapeDtypeStruct((RING, 16, columns), LOW),
            jax.ShapeDtypeStruct((4, text_rows, width), LOW),
            jax.ShapeDtypeStruct((4, text_rows, width), WIDE),
            *[jax.ShapeDtypeStruct((r // RING, c), WIDE) for r, c in shapes],
        ],
        in_specs=[WHOLE] * 9 + [ANY] * len(grads),
        out_specs=[WHOLE] * 3 + [ANY] * 2 + [WHOLE] * len(grads),
        scratch_shapes=[
            pltpu.VMEM((rows + text_rows, width), LOW),
            pltpu.VMEM((text_rows, width), WIDE),
            pltpu.VMEM((16, width), WIDE),
            pltpu.VMEM((3, 16, columns), WIDE),
            pltpu.VMEM((16, columns), LOW),
            pltpu.VMEM((RING, 16, columns), LOW),
            pltpu.SemaphoreType.DMA((2,)),
            pltpu.SemaphoreType.DMA((2, 3)),
            pltpu.SemaphoreType.DMA((2, RING - 1)),
            pltpu.SemaphoreType.DMA((2, 2, 4)),
            *ScatterRing.scratch(shapes),
        ],
        compiler_params=pltpu.CompilerParams(
            collective_id=ident, has_side_effects=True, vmem_limit_bytes=VMEM_LIMIT
        ),
        name="tail_ring",
    )(here, there, scale, other, *x, *middle, text_out, *grads)
    return found


def head_lanes(head):
    lane = lax.broadcasted_iota(jnp.int32, (1, LANES), 1)
    return (lane < HEAD_DIM) if head == 0 else (lane >= HEAD_DIM)


def attend_pair(split, bias_ref, q_ref, k_ref, v_ref, out_ref, lse_ref):
    scale = HEAD_DIM ** (-0.5)
    bias = bias_ref[...]
    outs, totals = [], []
    for head in range(2):
        mine = head_lanes(head)
        queries = jnp.where(mine, q_ref[...] * scale, 0).astype(LOW)
        image = dot(queries, k_ref[:split], NT)
        text = dot(queries, k_ref[split:], NT) + bias
        top = jnp.maximum(
            jnp.max(image, axis=1, keepdims=True), jnp.max(text, axis=1, keepdims=True)
        )
        image = jnp.exp(image - top).astype(LOW)
        text = jnp.exp(text - top).astype(LOW)
        values = jnp.where(mine, v_ref[...], 1).astype(LOW)
        both = dot(image, values[:split], NN) + dot(text, values[split:], NN)
        sums = pltpu.roll(both, HEAD_DIM, 1)
        outs.append(both / sums)
        totals.append(top + jnp.log(sums))
    first = head_lanes(0)
    out_ref[...] = jnp.where(first, outs[0], outs[1]).astype(out_ref.dtype)
    flipped = jnp.where(first, totals[0], totals[1]).T
    lse_ref[0] = jnp.concatenate([flipped[:4], flipped[HEAD_DIM : HEAD_DIM + 4]], axis=0)


def first_kernel(chunk, *refs):
    x_image, x_text, cot_image, cot_text, mods, *blocks = refs[:7]
    outs, fulls, refs = refs[7:10], refs[10:13], refs[13:]
    mines, pooled, (row_sem, own_sem) = refs[:3], refs[3], refs[4:6]
    ring = GatherRing([*blocks, pooled], fulls, refs[6:])
    me = lax.axis_index("dp")

    def row_copy(i, source, slot, hop, sem):
        rows = mines[i].shape[0]
        return pltpu.make_async_remote_copy(
            src_ref=source, dst_ref=outs[i].at[pl.ds(slot * rows, rows)],
            send_sem=row_sem.at[i, 0, sem], recv_sem=row_sem.at[i, 1, sem],
            device_id=(me, tensor_peer(hop)), device_id_type=MESH,
        )

    def own(i):
        rows = mines[i].shape[0]
        return pltpu.make_async_copy(mines[i], outs[i].at[pl.ds(0, rows)], own_sem.at[i])

    def to_far(i):
        return row_copy(i, mines[i], 2, 2, 0)

    def to_near(i):
        return row_copy(i, mines[i], 1, 1, 1)

    def forward(i):
        rows = mines[i].shape[0]
        return row_copy(i, outs[i].at[pl.ds(2 * rows, rows)], 3, 1, 2)

    def send(i):
        to_far(i).start()
        to_near(i).start()
        own(i).start()

    def norm_rows(x, stream):
        x = x.astype(WIDE)
        centred = x - jnp.mean(x, axis=-1, keepdims=True)
        spread = lax.rsqrt(jnp.mean(centred * centred, axis=-1, keepdims=True) + EPS)
        gain, shift = mods[2 * stream : 2 * stream + 1], mods[2 * stream + 1 : 2 * stream + 2]
        return (centred * spread * gain + shift).astype(LOW)

    def over_chunks(body):
        def step(i, _):
            body(pl.ds(pl.multiple_of(i * chunk, chunk), chunk))
            return 0

        lax.fori_loop(0, x_image.shape[0] // chunk, step, 0)

    meet([*ring.sides, *[(me, tensor_peer(hop)) for hop in (1, 2)]])
    pooled[...] = (mods[5:6] * cot_text[: pooled.shape[0]].astype(WIDE)).astype(LOW)
    ring.start()

    def norm_chunk(some):
        mines[0][some] = norm_rows(x_image[some], 0)

    def grad_chunk(some):
        mines[2][some] = (mods[4:5] * cot_image[some].astype(WIDE)).astype(LOW)

    over_chunks(norm_chunk)
    send(0)
    mines[1][...] = norm_rows(x_text[...], 1)
    send(1)
    over_chunks(grad_chunk)
    send(2)
    ring.step(1)
    for i in range(2):
        to_far(i).wait()
        forward(i).start()
    ring.step(2)
    to_far(2).wait()
    forward(2).start()
    ring.step(3)
    for i in range(3):
        own(i).wait()
        to_near(i).wait()
        forward(i).wait()
    ring.step(4)
    ring.end()


def first_ring(x, cotangent, mods, blocks, pool_rows, ident):
    width = mods.shape[1]
    rows = [x[0].shape[0], x[1].shape[0], x[0].shape[0]]
    fulls = [block.shape for block in blocks] + [(pool_rows, width)]
    found = pl.pallas_call(
        functools.partial(first_kernel, 64),
        in_specs=[WHOLE] * 5 + [ANY] * 2,
        out_specs=[ANY] * 6,
        out_shape=[
            *[jax.ShapeDtypeStruct((4 * n, width), LOW) for n in rows],
            *[jax.ShapeDtypeStruct((RING * n, columns), LOW) for n, columns in fulls],
        ],
        scratch_shapes=[
            *[pltpu.VMEM((n, width), LOW) for n in rows],
            pltpu.VMEM((pool_rows, width), LOW),
            pltpu.SemaphoreType.DMA((3, 2, 3)),
            pltpu.SemaphoreType.DMA((3,)),
            *GatherRing.scratch(3),
        ],
        compiler_params=pltpu.CompilerParams(
            collective_id=ident, has_side_effects=True, vmem_limit_bytes=VMEM_LIMIT
        ),
        name="first_ring",
    )(*x, *cotangent, mods, *blocks)
    return found[:2], found[2], found[3:5], found[5]


def exchange_sums(part, sent, got, sems, me):
    copy = pltpu.make_async_remote_copy(
        src_ref=sent, dst_ref=got, send_sem=sems.at[0, 0], recv_sem=sems.at[1, 0],
        device_id=(me, tensor_peer(1)), device_id_type=MESH,
    )
    sent[0] = part(1).astype(LOW)
    sent[1] = part(3).astype(LOW)
    copy.start()
    return copy


def middle_kernel(split, chunk, *refs):
    bias_ref, q_ref, k_ref, v_ref, x_image, x_text, mods = refs[:7]
    out_blocks, ffn_blocks, refs = refs[7:9], refs[9:11], refs[11:]
    mixed, lse_ref, *wide_outs, text_in, image_in = refs[:8]
    branch_image, branch_text, mid_image, mid_text = wide_outs
    out_fulls, ffn_fulls, refs = refs[8:10], refs[10:12], refs[12:]
    weights, sent, got, far_sent, far_got, here, mine = refs[:7]
    sems, weight_sem, row_sem, own_sem = refs[7:11]
    first = GatherRing(out_blocks, out_fulls, refs[11:14])
    second = GatherRing(ffn_blocks, ffn_fulls, refs[14:17])
    me = lax.axis_index("dp")
    block = q_ref.shape[0]
    pair, at = pl.program_id(0), pl.program_id(0) * 2 + pl.program_id(1)
    rows = x_image.shape[0]

    @pl.when(at == 0)
    def _():
        meet([*first.sides, *[(me, tensor_peer(hop)) for hop in (1, 2)]])
        first.start()

    for step in range(1, 5):

        @pl.when(at == step)
        def _():
            first.step(step)

    weight_copies = [
        pltpu.make_async_copy(out_fulls[s], weights.at[s], weight_sem.at[s]) for s in range(2)
    ]

    @pl.when(at == 4)
    def _():
        first.end()
        second.start()
        for copy in weight_copies:
            copy.start()

    place = (
        pl.ds(pl.multiple_of(pl.program_id(1) * block, block), block),
        pl.ds(pl.multiple_of(pair * LANES, LANES), LANES),
    )
    attend_pair(split, bias_ref, q_ref, k_ref, v_ref, mixed.at[place], lse_ref)

    @pl.when(at == 2 * pl.num_programs(0) - 1)
    def _():
        for copy in weight_copies:
            copy.wait()
        text_rows = x_text.shape[0]

        def part(b):
            image = dot(mixed[b * rows : (b + 1) * rows], weights[0], NN)
            low = split + b * text_rows
            text = dot(mixed[low : low + text_rows], weights[1], NN)
            return jnp.concatenate([image, text], axis=0)

        near = exchange_sums(part, sent, got, sems, me)
        here[...] = part(0)
        far_sent[...] = part(2).astype(LOW)
        near.wait()
        far_sent[...] = (far_sent[...].astype(WIDE) + got[1].astype(WIDE)).astype(LOW)
        far = pltpu.make_async_remote_copy(
            src_ref=far_sent, dst_ref=far_got, send_sem=sems.at[0, 1], recv_sem=sems.at[1, 1],
            device_id=(me, tensor_peer(2)), device_id_type=MESH,
        )
        far.start()
        here[...] += got[0].astype(WIDE)
        second.step(1)
        far.wait()

        def norm_rows(x, branch, stream):
            middle = x.astype(WIDE) + mods[3 * stream : 3 * stream + 1] * branch
            centred = middle - jnp.mean(middle, axis=-1, keepdims=True)
            spread = lax.rsqrt(jnp.mean(centred * centred, axis=-1, keepdims=True) + EPS)
            gain, shift = mods[3 * stream + 1 : 3 * stream + 2], mods[3 * stream + 2 : 3 * stream + 3]
            return middle, (centred * spread * gain + shift).astype(LOW)

        def image_chunk(i, _):
            some = pl.ds(pl.multiple_of(i * chunk, chunk), chunk)
            branch = here[some] + far_got[some].astype(WIDE)
            branch_image[some] = branch
            middle, low = norm_rows(x_image[some], branch, 0)
            mid_image[some] = middle
            mine[some] = low
            return 0

        lax.fori_loop(0, rows // chunk, image_chunk, 0)

        def row_copy(source, slot, hop, sem):
            return pltpu.make_async_remote_copy(
                src_ref=source, dst_ref=image_in.at[pl.ds(slot * rows, rows)],
                send_sem=row_sem.at[0, sem], recv_sem=row_sem.at[1, sem],
                device_id=(me, tensor_peer(hop)), device_id_type=MESH,
            )

        own = pltpu.make_async_copy(mine, image_in.at[pl.ds(0, rows)], own_sem.at[0])
        to_far, to_near = row_copy(mine, 2, 2, 0), row_copy(mine, 1, 1, 1)
        to_far.start()
        to_near.start()
        own.start()
        branch = here[rows:] + far_got[rows:].astype(WIDE)
        branch_text[...] = branch
        middle, low = norm_rows(x_text[...], branch, 1)
        mid_text[...] = middle
        text_in[...] = low
        second.step(2)
        to_far.wait()
        last = row_copy(image_in.at[pl.ds(2 * rows, rows)], 3, 1, 2)
        last.start()
        second.step(3)
        own.wait()
        to_near.wait()
        last.wait()
        second.step(4)
        second.end()


def middle_ring(joint, bias, x, mods, split, heads, out_blocks, ffn_blocks, ident):
    rows, pairs, block = joint.shape[0], heads // 2, joint.shape[0] // 2
    whole = lambda part: pl.BlockSpec((rows, LANES), lambda h, i: (0, part * pairs + h))
    image_rows, width = x[0].shape
    text_rows = x[1].shape[0]
    both = image_rows + text_rows
    depth = heads * HEAD_DIM
    found = pl.pallas_call(
        functools.partial(middle_kernel, split, 64),
        grid=(pairs, 2),
        in_specs=[
            pl.BlockSpec((1, rows - split), lambda h, i: (0, 0)),
            pl.BlockSpec((block, LANES), lambda h, i: (i, h)),
            whole(1),
            whole(2),
            *[WHOLE] * 3,
            *[ANY] * 4,
        ],
        out_specs=[
            WHOLE,
            pl.BlockSpec((1, 8, block), lambda h, i: (h, 0, i)),
            *[WHOLE] * 5,
            *[ANY] * 5,
        ],
        out_shape=[
            jax.ShapeDtypeStruct((rows, depth), LOW),
            jax.ShapeDtypeStruct((pairs, 8, rows), WIDE),
            *[jax.ShapeDtypeStruct((n, width), WIDE) for n in (image_rows, text_rows) * 2],
            jax.ShapeDtypeStruct((text_rows, width), LOW),
            jax.ShapeDtypeStruct((4 * image_rows, width), LOW),
            *[
                jax.ShapeDtypeStruct((RING * b.shape[0], b.shape[1]), b.dtype)
                for b in (*out_blocks, *ffn_blocks)
            ],
        ],
        scratch_shapes=[
            pltpu.VMEM((2, depth, width), LOW),
            pltpu.VMEM((2, both, width), LOW),
            pltpu.VMEM((2, both, width), LOW),
            pltpu.VMEM((both, width), LOW),
            pltpu.VMEM((both, width), LOW),
            pltpu.VMEM((both, width), WIDE),
            pltpu.VMEM((image_rows, width), LOW),
            pltpu.SemaphoreType.DMA((2, 2)),
            pltpu.SemaphoreType.DMA((2,)),
            pltpu.SemaphoreType.DMA((2, 3)),
            pltpu.SemaphoreType.DMA((1,)),
            *GatherRing.scratch(2),
            *GatherRing.scratch(2),
        ],
        compiler_params=pltpu.CompilerParams(
            collective_id=ident, has_side_effects=True, vmem_limit_bytes=VMEM_LIMIT
        ),
        name="middle_ring",
    )(bias, joint, joint, joint, *x, mods, *out_blocks, *ffn_blocks)
    return found


def back_kernel(split, chunk, *refs):
    bias_ref, q_ref, k_ref, v_ref, o_ref, lse_ref = refs[:6]
    text_second, mid_image, mid_text, cot_image, cot_text, mods = refs[6:12]
    partial, out_weights, grads, theirs, refs = refs[12], refs[13:15], refs[15:17], refs[17:19], refs[19:]
    dq_ref, dk_ref, dv_ref, image_second, image_grad, text_grad = refs[:6]
    image_rows, text_rows, *fars = refs[6:10]
    sums, refs = refs[10:12], refs[12:]
    dk_acc, dv_acc, weights, parts, got, far_sent, far_got, rows_in, mixed_grad = refs[:9]
    part_sem, sems, row_sem, weight_sem, rows_sem, far_sem = refs[9:15]
    ring = ScatterRing(grads, sums, refs[15:])
    me = lax.axis_index("dp")
    rows, texts = mid_image.shape[0], mid_text.shape[0]
    block = q_ref.shape[0]
    at = pl.program_id(0) * pl.num_programs(1) + pl.program_id(1)
    last = pl.num_programs(0) * pl.num_programs(1) - 1

    def part_of(b):
        return partial.at[pl.ds(b * rows, rows)]

    def keep(i):
        return pltpu.make_async_copy(part_of(2 * i), parts.at[i], part_sem.at[i])

    def near(i):
        return pltpu.make_async_remote_copy(
            src_ref=part_of(2 * i + 1), dst_ref=got.at[i],
            send_sem=sems.at[0, i], recv_sem=sems.at[1, i],
            device_id=(me, tensor_peer(1)), device_id_type=MESH,
        )

    def row_copy(source, slot, hop, sem):
        return pltpu.make_async_remote_copy(
            src_ref=source, dst_ref=rows_in.at[slot],
            send_sem=row_sem.at[0, sem], recv_sem=row_sem.at[1, sem],
            device_id=(me, tensor_peer(hop)), device_id_type=MESH,
        )

    def weight(s):
        return pltpu.make_async_copy(out_weights[s], weights.at[s], weight_sem.at[s])

    def save(b, s):
        low, high, whole = ((0, rows, image_rows), (rows, texts, text_rows))[s]
        return pltpu.make_async_copy(
            rows_in.at[b, pl.ds(low, high)], whole.at[pl.ds(b * high, high)], rows_sem.at[s, b]
        )

    def rows_back(second, middle, cotangent, stream):
        centred = middle - jnp.mean(middle, axis=-1, keepdims=True)
        spread = lax.rsqrt(jnp.mean(centred * centred, axis=-1, keepdims=True) + EPS)
        normed = centred * spread
        wide = second * mods[2 * stream + 1 : 2 * stream + 2]
        inner = jnp.mean(wide, axis=-1, keepdims=True)
        cross = jnp.mean(wide * normed, axis=-1, keepdims=True)
        grad = cotangent.astype(WIDE) + (wide - inner - normed * cross) * spread
        return grad, (mods[2 * stream : 2 * stream + 1] * grad).astype(LOW)

    @pl.when(at == 0)
    def _():
        for i in range(2):
            keep(i).start()
            weight(i).start()
        ring.load_all()
        meet([*ring.sides, *[(me, tensor_peer(hop)) for hop in (1, 2)]])
        for i in range(2):
            near(i).start()
        ring.start()
        for i in range(2):
            keep(i).wait()
            near(i).wait()
        far_sent[...] = (parts[1].astype(WIDE) + got[1].astype(WIDE)).astype(LOW)
        far = pltpu.make_async_remote_copy(
            src_ref=far_sent, dst_ref=far_got, send_sem=sems.at[0, 2], recv_sem=sems.at[1, 2],
            device_id=(me, tensor_peer(2)), device_id_type=MESH,
        )
        far.start()
        grad, low = rows_back(text_second[...], mid_text[...], cot_text[...], 1)
        text_grad[...] = grad
        rows_in[0, rows:] = low
        ring.step(1)
        far.wait()

        def image_chunk(i, _):
            some = pl.ds(pl.multiple_of(i * chunk, chunk), chunk)
            second = parts[0, some].astype(WIDE) + got[0, some].astype(WIDE)
            second = second + far_got[some].astype(WIDE)
            image_second[some] = second
            grad, low = rows_back(second, mid_image[some], cot_image[some], 0)
            image_grad[some] = grad
            rows_in[0, some] = low
            return 0

        lax.fori_loop(0, rows // chunk, image_chunk, 0)
        to_far = row_copy(rows_in.at[0], 2, 2, 0)
        to_near = row_copy(rows_in.at[0], 1, 1, 1)
        to_far.start()
        to_near.start()
        ring.step(2)
        to_far.wait()
        forward = row_copy(rows_in.at[2], 3, 1, 2)
        forward.start()
        for i in range(2):
            weight(i).wait()
        to_near.wait()

        def through(b):
            image = dot(rows_in[b, :rows], weights[0], NT).astype(LOW)
            mixed_grad[b * rows : (b + 1) * rows] = image
            text = dot(rows_in[b, rows:], weights[1], NT).astype(LOW)
            mixed_grad[split + b * texts : split + (b + 1) * texts] = text

        for b in range(3):
            through(b)
        ring.step(3)
        forward.wait()
        through(3)
        for b in range(4):
            for s in range(2):
                save(b, s).start()

    far_copies = [
        pltpu.make_async_remote_copy(
            src_ref=theirs[s], dst_ref=fars[s], send_sem=far_sem.at[0, s], recv_sem=far_sem.at[1, s],
            device_id=(me, tensor_peer(2)), device_id_type=MESH,
        )
        for s in range(2)
    ]

    @pl.when(at == 1)
    def _():
        for copy in far_copies:
            copy.start()

    for step, when in ((4, 3), (5, 8), (6, 13)):

        @pl.when(at == when)
        def _():
            ring.step(step)

    place = (
        pl.ds(pl.multiple_of(pl.program_id(1) * block, block), block),
        pl.ds(pl.multiple_of(pl.program_id(0) * LANES, LANES), LANES),
    )
    attend_back_pair(
        split,
        (bias_ref, q_ref, k_ref, v_ref, o_ref, mixed_grad.at[place], lse_ref)
        + (dq_ref, dk_ref, dv_ref, dk_acc, dv_acc),
    )

    @pl.when(at == last)
    def _():
        ring.step(7)
        ring.end()
        for copy in far_copies:
            copy.wait()
        for b in range(4):
            for s in range(2):
                save(b, s).wait()


def back_ring(
    joint, bias, mixed, lse, split, heads, text_second, middle, cotangent, mods, partial,
    out_weights, grads, theirs, ident, block=256,
):
    rows, pairs = joint.shape[0], heads // 2
    whole = lambda part: pl.BlockSpec((rows, LANES), lambda h, i: (0, part * pairs + h))
    some = pl.BlockSpec((block, LANES), lambda h, i: (i, h))
    image_rows, width = middle[0].shape
    texts = middle[1].shape[0]
    depth = heads * HEAD_DIM
    found = pl.pallas_call(
        functools.partial(back_kernel, split, 64),
        grid=(pairs, rows // block),
        in_specs=[
            pl.BlockSpec((rows - split, 1), lambda h, i: (0, 0)),
            some,
            whole(1),
            whole(2),
            some,
            pl.BlockSpec((1, 8, block), lambda h, i: (h, 0, i)),
            *[WHOLE] * 6,
            *[ANY] * 7,
        ],
        out_specs=[some, whole(0), whole(0), *[WHOLE] * 3, *[ANY] * 4, WHOLE, WHOLE],
        out_shape=[
            *[jax.ShapeDtypeStruct((rows, depth), LOW)] * 3,
            *[jax.ShapeDtypeStruct((n, width), WIDE) for n in (image_rows, image_rows, texts)],
            *[jax.ShapeDtypeStruct((4 * n, width), LOW) for n in (image_rows, texts)],
            *[jax.ShapeDtypeStruct(t.shape, t.dtype) for t in theirs],
            *[jax.ShapeDtypeStruct((g.shape[0] // RING, g.shape[1]), WIDE) for g in grads],
        ],
        scratch_shapes=[
            *[pltpu.VMEM((rows, LANES), WIDE)] * 2,
            pltpu.VMEM((2, depth, width), LOW),
            *[pltpu.VMEM((2, image_rows, width), LOW)] * 2,
            *[pltpu.VMEM((image_rows, width), LOW)] * 2,
            pltpu.VMEM((4, image_rows + texts, width), LOW),
            pltpu.VMEM((rows, depth), LOW),
            pltpu.SemaphoreType.DMA((2,)),
            pltpu.SemaphoreType.DMA((2, 3)),
            pltpu.SemaphoreType.DMA((2, 3)),
            pltpu.SemaphoreType.DMA((2,)),
            pltpu.SemaphoreType.DMA((2, 4)),
            pltpu.SemaphoreType.DMA((2, 2)),
            *ScatterRing.scratch([g.shape for g in grads]),
        ],
        compiler_params=pltpu.CompilerParams(
            collective_id=ident, has_side_effects=True, vmem_limit_bytes=VMEM_LIMIT
        ),
        name="back_ring",
    )(
        bias.T, joint, joint, joint, mixed, lse, text_second, *middle, *cotangent, mods,
        partial, *out_weights, *grads, *theirs,
    )
    return found


def attend_kernel(split, count, waits, *refs):
    bias_ref, q_ref, k_ref, v_ref = refs[:4]
    blocks, (out_ref, lse_ref) = refs[4 : 4 + count], refs[4 + count : 6 + count]
    at = pl.program_id(0) * pl.num_programs(1) + pl.program_id(1)
    if count:
        ring = GatherRing(blocks, refs[6 + count : 6 + 2 * count], refs[6 + 2 * count :])

        @pl.when(at == 0)
        def _():
            meet(ring.sides)
            ring.start()

        for step, when in enumerate(waits):

            @pl.when(at == when)
            def _():
                ring.step(step + 1)

    attend_pair(split, bias_ref, q_ref, k_ref, v_ref, out_ref, lse_ref)
    if count:

        @pl.when(at == pl.num_programs(0) * pl.num_programs(1) - 1)
        def _():
            for step in range(len(waits) + 1, ring.STEPS + 1):
                ring.step(step)
            ring.end()


def attend(joint, bias, split, heads, blocks, ident, waits):
    rows, pairs, count, block = joint.shape[0], heads // 2, len(blocks), joint.shape[0] // 2
    whole = lambda part: pl.BlockSpec((rows, LANES), lambda h, i: (0, part * pairs + h))
    extra = dict(collective_id=ident, has_side_effects=True) if count else {}
    found = pl.pallas_call(
        functools.partial(attend_kernel, split, count, waits),
        grid=(pairs, 2),
        in_specs=[
            pl.BlockSpec((1, rows - split), lambda h, i: (0, 0)),
            pl.BlockSpec((block, LANES), lambda h, i: (i, h)),
            whole(1),
            whole(2),
            *[ANY] * count,
        ],
        out_specs=[
            pl.BlockSpec((block, LANES), lambda h, i: (i, h)),
            pl.BlockSpec((1, 8, block), lambda h, i: (h, 0, i)),
            *[ANY] * count,
        ],
        out_shape=[
            jax.ShapeDtypeStruct((rows, heads * HEAD_DIM), LOW),
            jax.ShapeDtypeStruct((pairs, 8, rows), WIDE),
            *[jax.ShapeDtypeStruct((RING * b.shape[0], b.shape[1]), b.dtype) for b in blocks],
        ],
        scratch_shapes=GatherRing.scratch(count) if count else [],
        compiler_params=pltpu.CompilerParams(vmem_limit_bytes=VMEM_LIMIT, **extra),
        name="attend",
    )(bias, joint, joint, joint, *blocks)
    return found[0], found[1], found[2:]


def attend_back_pair(split, refs):
    (bias_ref, q_ref, k_ref, v_ref, o_ref, g_ref, lse_ref, dq_ref, dk_ref, dv_ref, dk_acc, dv_acc) = refs
    step = pl.program_id(1)
    scale = HEAD_DIM ** (-0.5)

    @pl.when(step == 0)
    def _():
        dk_acc[...] = jnp.zeros_like(dk_acc)
        dv_acc[...] = jnp.zeros_like(dv_acc)

    product = (g_ref[...].astype(WIDE) * o_ref[...].astype(WIDE)).T
    bias = bias_ref[...]
    dq = None
    for head in range(2):
        mine = head_lanes(head)
        queries = jnp.where(mine, q_ref[...] * scale, 0).astype(LOW)
        grads = jnp.where(mine, g_ref[...], 0).astype(LOW)
        keys = jnp.where(mine, k_ref[...], 0).astype(LOW)
        own = product[head * HEAD_DIM : (head + 1) * HEAD_DIM]
        delta = jnp.sum(own, axis=0, keepdims=True)
        total = lse_ref[0][4 * head : 4 * head + 1]
        for low, high in ((0, split), (split, k_ref.shape[0])):
            scores = dot(k_ref[low:high], queries, NT)
            if low:
                scores = scores + bias
            probs = jnp.exp(scores - total)
            grad_probs = dot(v_ref[low:high], grads, NT)
            grad_scores = (probs * (grad_probs - delta)).astype(LOW)
            dv_acc[low:high] += dot(probs.astype(LOW), grads, NN)
            dk_acc[low:high] += dot(grad_scores, queries, NN)
            part = dot(grad_scores, keys[low:high], TN)
            dq = part if dq is None else dq + part
    dq_ref[...] = (dq * scale).astype(LOW)

    @pl.when(step == pl.num_programs(1) - 1)
    def _():
        dk_ref[...] = dk_acc[...].astype(LOW)
        dv_ref[...] = dv_acc[...].astype(LOW)


def attend_back_kernel(split, count, waits, *refs):
    ins, rest = refs[:7], refs[7:]
    grads, outs, rest = rest[:count], rest[count : count + 3], rest[count + 3 :]
    sums, accs, rest = rest[:count], rest[count : count + 2], rest[count + 2 :]
    at = pl.program_id(0) * pl.num_programs(1) + pl.program_id(1)
    if count:
        ring = ScatterRing(grads, sums, rest)

        @pl.when(at == 0)
        def _():
            ring.load_all()
            meet(ring.sides)
            ring.start()

        for step, when in enumerate(waits):

            @pl.when(at == when)
            def _():
                ring.step(step + 1)

    attend_back_pair(split, (*ins, *outs, *accs))
    if count:

        @pl.when(at == pl.num_programs(0) * pl.num_programs(1) - 1)
        def _():
            for step in range(len(waits) + 1, ring.STEPS + 1):
                ring.step(step)
            ring.end()


def attend_back(joint, bias, mixed, grad, lse, split, heads, grads, ident, waits):
    rows, pairs, count, block = joint.shape[0], heads // 2, len(grads), joint.shape[0] // 2
    whole = lambda part: pl.BlockSpec((rows, LANES), lambda h, i: (0, part * pairs + h))
    some = pl.BlockSpec((block, LANES), lambda h, i: (i, h))
    extra = dict(collective_id=ident, has_side_effects=True) if count else {}
    found = pl.pallas_call(
        functools.partial(attend_back_kernel, split, count, waits),
        grid=(pairs, 2),
        in_specs=[
            pl.BlockSpec((rows - split, 1), lambda h, i: (0, 0)),
            some,
            whole(1),
            whole(2),
            some,
            some,
            pl.BlockSpec((1, 8, block), lambda h, i: (h, 0, i)),
            *[ANY] * count,
        ],
        out_specs=[some, whole(0), whole(0), *[WHOLE] * count],
        out_shape=[
            *[jax.ShapeDtypeStruct((rows, heads * HEAD_DIM), LOW)] * 3,
            *[jax.ShapeDtypeStruct((g.shape[0] // RING, g.shape[1]), WIDE) for g in grads],
        ],
        scratch_shapes=[
            *[pltpu.VMEM((rows, LANES), WIDE)] * 2,
            *(ScatterRing.scratch([g.shape for g in grads]) if count else []),
        ],
        compiler_params=pltpu.CompilerParams(vmem_limit_bytes=VMEM_LIMIT, **extra),
        name="attend_back",
    )(bias.T, joint, joint, joint, mixed, grad, lse, *grads)
    return found[:3], found[3:]


def local(size, image, text, cond, w_ada, w_qkv, w_out, w_up, w_down, grad_image, grad_text):
    index = lax.axis_index("tensor")
    seqs = size
    image_rows, width = image.shape[1], image.shape[2]
    text_tokens = text.shape[1]
    text_own = -(-text_tokens // 4)
    text_rows = -(-text_own // TEXT_TILE) * TEXT_TILE
    pool_rows = -(-text_own // POOL_TILE) * POOL_TILE
    width_here = w_ada.shape[-1]
    ada_rows = w_ada.shape[1]
    heads_here = w_qkv.shape[-1] // HEAD_DIM

    def blocks_of(weight):
        return [weight[stream].astype(LOW).reshape(weight.shape[1], -1) for stream in range(2)]

    up_blocks, down_blocks = blocks_of(w_up), blocks_of(w_down)

    units = up_blocks[1].shape[1] // size
    text_up = lax.all_to_all(
        up_blocks[1].reshape(-1, size, units), "dp", split_axis=1, concat_axis=0, tiled=True
    ).reshape(width, units)
    text_down = down_blocks[1]

    def pool_start(rows):
        copies = jnp.broadcast_to(rows[None, :pool_rows], (size, pool_rows, width))
        rows = lax.all_to_all(copies, "dp", split_axis=0, concat_axis=0, tiled=True)
        return rows.reshape(-1, width)

    def unpool_end(here, far):
        part = (here + far.astype(WIDE)).astype(LOW).reshape(size, pool_rows, width)
        part = lax.all_to_all(part, "dp", split_axis=0, concat_axis=0, tiled=True)
        total = jnp.sum(part.astype(WIDE), axis=0)
        return jnp.pad(total, ((0, text_rows - pool_rows), (0, 0)))


    cond_low = jax.nn.silu(cond).astype(LOW)
    cond_rows = lax.all_to_all(
        cond_low.reshape(seqs, ada_rows), "dp", split_axis=0, concat_axis=0, tiled=True
    )
    ada_low = w_ada.astype(LOW)
    mod_parts = jnp.einsum("nd,sdkf->nskf", cond_rows, ada_low, preferred_element_type=WIDE)
    mod_parts = lax.all_to_all(mod_parts, "dp", split_axis=0, concat_axis=0, tiled=True)
    modulation = lax.all_gather(jnp.sum(mod_parts, axis=0), "tensor", axis=2, tiled=True)

    def mod_row(stream, which):
        return modulation[stream, which][None, :]

    def own_text(rows):
        padded = jnp.pad(rows, ((0, 4 * text_own - text_tokens), (0, 0)))
        own = lax.dynamic_slice_in_dim(padded, index * text_own, text_own, 0)
        return jnp.pad(own, ((0, text_rows - text_own), (0, 0)))

    split_at = 4 * image_rows
    places = jnp.arange(4 * text_rows)
    token = ((places // text_rows) ^ index) * text_own + places % text_rows
    is_key = (places % text_rows < text_own) & (token < text_tokens)
    bias = jnp.where(is_key, 0.0, -1e30).astype(WIDE)[None, :]

    streams = [image[0].astype(WIDE), own_text(text[0]).astype(WIDE)]
    cotangent = [grad_image[0].astype(WIDE), own_text(grad_text[0]).astype(WIDE)]
    normed_in = [layer_norm(residual) for residual in streams]
    first_in = [
        (normed_in[s] * (1.0 + mod_row(s, 1)) + mod_row(s, 0)).astype(LOW) for s in range(2)
    ]
    ffn_grad = [(mod_row(s, 5) * cotangent[s]).astype(LOW) for s in range(2)]
    cot_rows = [grad_image[0], own_text(grad_text[0])]
    x_rows = [image[0], own_text(text[0])]
    if size == RING:
        mods = [1.0 + mod_row(0, 1), mod_row(0, 0), 1.0 + mod_row(1, 1), mod_row(1, 0)]
        mods += [mod_row(0, 5), mod_row(1, 5), jnp.zeros((2, width), WIDE)]
        attn_rows, ffn_rows, qkv_full, pooled_grad = first_ring(
            x_rows, cot_rows, jnp.concatenate(mods, axis=0), blocks_of(w_qkv), pool_rows, 1
        )
    else:
        attn_rows = [gather_rows(rows) for rows in first_in]
        ffn_rows, pooled_grad = gather_rows(ffn_grad[0]), pool_start(ffn_grad[1])
        qkv_full = gather_dp(blocks_of(w_qkv), size, 1)
    joint = jnp.concatenate(
        [dot(attn_rows[s], qkv_full[s], NN).astype(LOW) for s in range(2)], axis=0
    )
    text_ffn_moved = gather_start(pooled_grad)
    ffn_blocks = [up_blocks[0], down_blocks[0]]
    if size == RING:
        mods = jnp.concatenate(
            [row for s in range(2) for row in (mod_row(s, 2), 1.0 + mod_row(s, 4), mod_row(s, 3))]
            + [jnp.zeros((2, width), WIDE)],
            axis=0,
        )
        found = middle_ring(
            joint, bias, x_rows, mods, split_at, heads_here, blocks_of(w_out), ffn_blocks, 2
        )
        mixed, log_total, *found = found
        branches, middle, text_in, mlp_rows = found[:2], found[2:4], found[4], found[5]
        out_full, up_full, down_full = found[6:8], found[8], found[9]
    else:
        mixed, log_total, _ = attend(joint, bias, split_at, heads_here, [], 0, ())
        *out_full, up_full, down_full = gather_dp(blocks_of(w_out) + ffn_blocks, size, 2)
        branches = [
            scatter_rows(dot(mixed[:split_at], out_full[0], NN)),
            scatter_rows(dot(mixed[split_at:], out_full[1], NN)),
        ]
        middle = [streams[s] + mod_row(s, 2) * branches[s] for s in range(2)]
        second_in = [
            (layer_norm(middle[s]) * (1.0 + mod_row(s, 4)) + mod_row(s, 3)).astype(LOW)
            for s in range(2)
        ]
        mlp_rows, text_in = gather_rows(second_in[0]), second_in[1]
    mixed, *text_ffn_moved = lax.optimization_barrier((mixed, *text_ffn_moved))
    text_ffn_rows = gather_end(pooled_grad, *text_ffn_moved)
    mixed_rows = [mixed[:split_at], mixed[split_at:]]
    normed_mid = [layer_norm(residual) for residual in middle]

    def gelu_back(pre_act, hidden_grad):
        return jax.vjp(gelu_tanh, pre_act)[1](hidden_grad)[0].astype(LOW)

    pooled_in = pool_start(text_in)
    pre_act = dot(mlp_rows, up_full, NN)
    hidden = gelu_tanh(pre_act).astype(LOW)
    hidden, pre_act, pooled_in = lax.optimization_barrier((hidden, pre_act, pooled_in))
    text_moved = gather_start(pooled_in)
    pre_grad = gelu_back(pre_act, dot(ffn_rows, down_full, NT))
    second_part = dot(pre_grad, up_full, NT).astype(LOW)
    down_grad = dot(hidden, ffn_rows, TN).astype(LOW)
    second_part, down_grad, *text_moved = lax.optimization_barrier(
        (second_part, down_grad, *text_moved)
    )
    text_mlp_rows = gather_end(pooled_in, *text_moved)
    text_pre_act = dot(text_mlp_rows, text_up, NN)
    text_hidden = gelu_tanh(text_pre_act).astype(LOW)
    text_pre_grad = gelu_back(text_pre_act, dot(text_ffn_rows, text_down, NT))
    text_here, text_there = scatter_start(dot(text_pre_grad, text_up, NT))
    text_far = lax.ppermute(text_there, "tensor", CHIP)
    pre_grad, text_there = lax.optimization_barrier((pre_grad, text_there))
    up_grad = dot(mlp_rows, pre_grad, TN).astype(LOW)
    here, there = scatter_start(dot(hidden, down_full, NN))
    up_grad, there, text_far = lax.optimization_barrier((up_grad, there, text_far))
    second_grad, ffn = [None, None], [None, None]
    second_grad[1] = unpool_end(text_here, text_far)
    text_here, text_there = scatter_start(dot(text_hidden, text_down, NN))
    text_down_grad = dot(text_hidden, text_ffn_rows, TN)
    text_up_grad = dot(text_mlp_rows, text_pre_grad, TN)
    second_part, second_grad[1], text_there, text_down_grad, text_up_grad = (
        lax.optimization_barrier(
            (second_part, second_grad[1], text_there, text_down_grad, text_up_grad)
        )
    )
    if size == RING:
        mods = jnp.concatenate(
            [row for s in range(2) for row in (mod_row(s, 2), 1.0 + mod_row(s, 4))]
            + [jnp.zeros((4, width), WIDE)],
            axis=0,
        )
        found = back_ring(
            joint, bias, mixed, log_total, split_at, heads_here, second_grad[1], middle,
            cot_rows, mods, second_part, out_full,
            [down_grad, up_grad], [there, text_there], 5,
        )
        *grads, second_grad[0], image_middle, text_middle = found[:6]
        middle_grad, branch_rows = [image_middle, text_middle], found[6:8]
        far, text_far, down_sum, up_sum = found[8:]
    else:
        second_grad[0] = scatter_rows(second_part)
        middle_grad, branch_rows = [None, None], [None, None]
        for s in range(2):
            wide = second_grad[s] * (1.0 + mod_row(s, 4))
            middle_grad[s] = cotangent[s] + jax.vjp(layer_norm, middle[s])[1](wide)[0]
            branch_rows[s] = gather_rows((mod_row(s, 2) * middle_grad[s]).astype(LOW))
        mixed_grad = jnp.concatenate(
            [dot(branch_rows[s], out_full[s], NT).astype(LOW) for s in range(2)], axis=0
        )
        grads = attend_back(
            joint, bias, mixed, mixed_grad, log_total, split_at, heads_here, [], 0, ()
        )[0]
        grads = list(grads)
        down_sum, up_sum = scatter_dp([down_grad, up_grad], size, 5)
        far = lax.ppermute(there, "tensor", CHIP)
        text_far = lax.ppermute(text_there, "tensor", CHIP)
    ffn[0], ffn[1] = here + far.astype(WIDE), unpool_end(text_here, text_far)
    results = [(middle[s] + mod_row(s, 5) * ffn[s]).astype(LOW) for s in range(2)]
    gate_terms = [jnp.sum(cotangent[s] * ffn[s], axis=0)[None] for s in range(2)]
    out_grad = [dot(mixed_rows[s], branch_rows[s], TN).astype(LOW) for s in range(2)]
    text_up_grad, grads[0] = lax.optimization_barrier((text_up_grad, grads[0]))
    text_up_grad = lax.all_to_all(
        text_up_grad.astype(LOW).reshape(size, -1, units),
        "dp", split_axis=0, concat_axis=2, tiled=True,
    )
    joint_grad = jnp.concatenate(grads, axis=1)
    joint_rows = [joint_grad[:split_at], joint_grad[split_at:]]
    qkv_grad = [dot(attn_rows[s], joint_rows[s], TN).astype(LOW) for s in range(2)]
    first_parts = [dot(joint_rows[s], qkv_full[s], NT).astype(LOW) for s in range(2)]
    here, there = scatter_start(
        jnp.concatenate(
            [
                part[b * (part.shape[0] // 4) : (b + 1) * (part.shape[0] // 4)]
                for b in range(4)
                for part in first_parts
            ]
        )
    )
    other = []
    for s in range(2):
        other += [
            jnp.zeros((2, width), WIDE),
            jnp.sum(middle_grad[s] * branches[s], axis=0)[None],
            jnp.sum(second_grad[s], axis=0)[None],
            jnp.sum(second_grad[s] * normed_mid[s], axis=0)[None],
            gate_terms[s],
        ]
    other = jnp.concatenate(other + [jnp.zeros((4, width), WIDE)], axis=0)
    if size == RING:
        scale = jnp.concatenate([1.0 + mod_row(s, 1) for s in range(2)], axis=0)
        image_input, mod_sum, mod_grad, text_out, text_grad, *found = tail_ring(
            here, there, scale, other, x_rows, middle_grad, results[1], qkv_grad + out_grad,
            width_here, 6,
        )
        qkv_image, qkv_text, out_image, out_text = found
        qkv_sums, out_sum = [qkv_image, qkv_text], [out_image, out_text]
        mod_sum = mod_sum[:12].reshape(2, 6, width_here)
        mod_grad = mod_grad[:, :12].reshape(seqs, 2, 6, width_here)
        mod_grad, text_up_grad = lax.optimization_barrier((mod_grad, text_up_grad))
    else:
        *qkv_sums, out_image, out_text = scatter_dp(qkv_grad + out_grad, size, 6)
        out_sum = [out_image, out_text]
        far = lax.ppermute(there, "tensor", CHIP)
        first_rows = here + far.astype(WIDE)
        first_grad = [first_rows[:image_rows], first_rows[image_rows:]]
        input_grad, first_terms = [None, None], []
        for s in range(2):
            wide = first_grad[s] * (1.0 + mod_row(s, 1))
            input_grad[s] = middle_grad[s] + jax.vjp(layer_norm, streams[s])[1](wide)[0]
            shift = jnp.sum(first_grad[s], axis=0)
            gain = jnp.sum(first_grad[s] * normed_in[s], axis=0)
            first_terms.append(jnp.stack([shift, gain]))
        image_input = input_grad[0]
        text_out = lax.all_gather(results[1], "tensor", axis=0)
        text_grad = lax.all_gather(input_grad[1], "tensor", axis=0)
        mod_terms = other[:12].reshape(2, 6, width).at[:, :2].set(jnp.stack(first_terms))
        mod_split = mod_terms.reshape(2, 6, 4, width_here).transpose(2, 0, 1, 3)
        mod_sum = jnp.sum(
            lax.all_to_all(mod_split, "tensor", split_axis=0, concat_axis=0, tiled=True), axis=0
        )
        mod_low = jnp.broadcast_to(mod_sum.astype(LOW)[None], (seqs,) + mod_sum.shape)
        mod_grad = lax.all_to_all(mod_low, "dp", split_axis=0, concat_axis=0, tiled=True)
    shift_grad = mod_sum[:, 3]
    text_up_grad = text_up_grad.reshape(-1, size * units).astype(WIDE)
    ada_grad = jnp.einsum("nd,nskf->sdkf", cond_rows, mod_grad, preferred_element_type=WIDE)
    act_parts = jnp.einsum("nskf,sdkf->nd", mod_grad, ada_low, preferred_element_type=WIDE)
    act_parts = lax.all_to_all(act_parts, "dp", split_axis=0, concat_axis=0, tiled=True)
    act_grad = lax.psum(act_parts.reshape(1, width), "tensor")
    cond_grad = jax.vjp(jax.nn.silu, cond)[1](act_grad)[0]

    def whole_text(blocks):
        return blocks[:, :text_own].reshape(4 * text_own, width)[:text_tokens][None]

    down_sum = jnp.stack([down_sum, text_down_grad])
    up_sum = jnp.stack([up_sum, text_up_grad])
    qkv_sum, out_sum = jnp.stack(qkv_sums), jnp.stack(out_sum)

    return (
        results[0][None],
        whole_text(text_out),
        image_input[None],
        whole_text(text_grad),
        cond_grad,
        shift_grad[None],
        ada_grad,
        qkv_sum.reshape(w_qkv.shape),
        out_sum.reshape(w_out.shape),
        up_sum,
        down_sum,
    )


def solution(mesh):
    size = mesh.shape["dp"]

    def step(*args):
        return local(size, *args)

    return jax.shard_map(
        step,
        mesh=mesh,
        in_specs=(
            P("dp", "tensor", None),
            P("dp", None, None),
            P("dp", None),
            P(None, "dp", None, "tensor"),
            P(None, "dp", None, "tensor"),
            P(None, ("tensor", "dp"), None),
            P(None, "dp", "tensor"),
            P(None, ("tensor", "dp"), None),
            P("dp", "tensor", None),
            P("dp", None, None),
        ),
        out_specs=(
            P("dp", "tensor", None),
            P("dp", None, None),
            P("dp", "tensor", None),
            P("dp", None, None),
            P("dp", None),
            P("dp", None, "tensor"),
            P(None, "dp", None, "tensor"),
            P(None, "dp", None, "tensor"),
            P(None, ("tensor", "dp"), None),
            P(None, "dp", "tensor"),
            P(None, ("tensor", "dp"), None),
        ),
        check_vma=False,
    )
```

```python
import functools

import jax
import jax.numpy as jnp
from jax import lax
from jax.experimental import pallas as pl
from jax.experimental.pallas import tpu as pltpu
from jax.sharding import PartitionSpec as P

HEAD_DIM = 64
EPS = 1e-06
LOW = jnp.bfloat16
WIDE = jnp.float32
TEXT_TILE = 64
POOL_TILE = 16
LANES = 128
NT, NN, TN = ((1,), (1,)), ((1,), (0,)), ((0,), (0,))


def dot(left, right, dims):
    return lax.dot_general(left, right, (dims, ((), ())), preferred_element_type=WIDE)


def layer_norm(values):
    average = jnp.mean(values, axis=-1, keepdims=True)
    centred = values - average
    spread = jnp.mean(centred * centred, axis=-1, keepdims=True)
    return centred * lax.rsqrt(spread + EPS)


def gelu_tanh(values):
    return jax.nn.gelu(values, approximate=True)


MESH = pl.DeviceIdType.MESH
RING = 8


def ring_dp(place):
    place = place % RING
    return 2 * place + (place // (RING // 2)) * (2 * RING - 1 - 4 * place)


def ring_place():
    index = lax.axis_index("dp")
    return index // 2 + (index % 2) * (RING - 1 - 2 * (index // 2))


def ring_sides(place):
    tensor = lax.axis_index("tensor")
    return (ring_dp(place + 1), tensor), (ring_dp(place + RING - 1), tensor)


def meet(sides):
    barrier = pltpu.get_barrier_semaphore()
    for side in sides:
        pl.semaphore_signal(barrier, inc=1, device_id=side, device_id_type=MESH)
    pl.semaphore_wait(barrier, len(sides))


def half_of(rows, columns, way):
    if rows // 2 % 16 == 0:
        return way * (rows // 2), rows // 2, 0, columns
    return 0, rows, way * (columns // 2), columns // 2


class GatherRing:
    STEPS = RING // 2

    def __init__(self, blocks, fulls, sems):
        self.blocks, self.fulls = blocks, fulls
        self.own_sem, self.send_sem, self.recv_sem = sems
        self.place = ring_place()
        self.sides = ring_sides(self.place)

    @staticmethod
    def scratch(count):
        steps = RING // 2
        return [
            pltpu.SemaphoreType.DMA((count,)),
            pltpu.SemaphoreType.DMA((count, 2, steps)),
            pltpu.SemaphoreType.DMA((count, 2, steps)),
        ]

    def copy(self, i, way, step):
        rows, columns = self.blocks[i].shape
        at = self.place + (RING - step if way == 0 else step)
        top, high, left, wide = 0, rows, 0, columns
        if step == self.STEPS - 1:
            top, high, left, wide = half_of(rows, columns, way)
        there = self.fulls[i].at[pl.ds(ring_dp(at) * rows + top, high), pl.ds(left, wide)]
        here = there if step else self.blocks[i]
        return pltpu.make_async_remote_copy(
            src_ref=here,
            dst_ref=there,
            send_sem=self.send_sem.at[i, way, step],
            recv_sem=self.recv_sem.at[i, way, step],
            device_id=self.sides[way],
            device_id_type=MESH,
        )

    def own(self, i):
        rows = self.blocks[i].shape[0]
        start = ring_dp(self.place) * rows
        return pltpu.make_async_copy(
            self.blocks[i], self.fulls[i].at[pl.ds(start, rows)], self.own_sem.at[i]
        )

    def start(self):
        for i in range(len(self.blocks)):
            for way in range(2):
                self.copy(i, way, 0).start()
            self.own(i).start()

    def step(self, step):
        for i in range(len(self.blocks)):
            for way in range(2):
                self.copy(i, way, step - 1).wait_recv()
                if step < self.STEPS:
                    self.copy(i, way, step).start()

    def end(self):
        for i in range(len(self.blocks)):
            self.own(i).wait()
            for way in range(2):
                for step in range(self.STEPS):
                    self.copy(i, way, step).wait_send()


class ScatterRing:
    STEPS = RING - 1

    def __init__(self, grads, sums, scratch):
        self.grads, self.sums = grads, sums
        count = len(grads)
        self.mine, self.got = scratch[:count], scratch[count : 2 * count]
        self.mine_sem, self.send_sem, self.recv_sem = scratch[2 * count :]
        self.place = ring_place()
        self.sides = ring_sides(self.place)

    @staticmethod
    def scratch(shapes):
        sizes = [half_of(rows // RING, columns, 0) for rows, columns in shapes]
        halves = [(2, RING, high, wide) for _, high, _, wide in sizes]
        gots = [(2, RING - 1, high, wide) for _, high, _, wide in sizes]
        count = len(shapes)
        return [
            *[pltpu.VMEM(shape, LOW) for shape in halves],
            *[pltpu.VMEM(shape, LOW) for shape in gots],
            pltpu.SemaphoreType.DMA((count, 2, RING)),
            pltpu.SemaphoreType.DMA((count, 2, RING - 1)),
            pltpu.SemaphoreType.DMA((count, 2, RING - 1)),
        ]

    def load(self, i, way, step):
        rows, columns = self.grads[i].shape[0] // RING, self.grads[i].shape[1]
        at = self.place + (2 * RING - step - 1 if way == 0 else step + 1)
        top, high, left, wide = half_of(rows, columns, way)
        return pltpu.make_async_copy(
            self.grads[i].at[pl.ds(ring_dp(at) * rows + top, high), pl.ds(left, wide)],
            self.mine[i].at[way, step],
            self.mine_sem.at[i, way, step],
        )

    def copy(self, i, way, step):
        return pltpu.make_async_remote_copy(
            src_ref=self.mine[i].at[way, step],
            dst_ref=self.got[i].at[way, step],
            send_sem=self.send_sem.at[i, way, step],
            recv_sem=self.recv_sem.at[i, way, step],
            device_id=self.sides[way],
            device_id_type=MESH,
        )

    def load_all(self):
        for step in range(RING):
            for i in range(len(self.grads)):
                for way in range(2):
                    self.load(i, way, step).start()

    def start(self):
        for i in range(len(self.grads)):
            for way in range(2):
                self.load(i, way, 0).wait()
                self.copy(i, way, 0).start()

    def step(self, step):
        for i in range(len(self.grads)):
            rows, columns = self.grads[i].shape[0] // RING, self.grads[i].shape[1]
            for way in range(2):
                top, high, left, wide = half_of(rows, columns, way)
                self.load(i, way, step).wait()
                self.copy(i, way, step - 1).wait_recv()
                total = self.mine[i][way, step].astype(WIDE) + self.got[i][way, step - 1].astype(WIDE)
                if step < self.STEPS:
                    self.mine[i][way, step] = total.astype(LOW)
                    self.copy(i, way, step).start()
                else:
                    self.sums[i][pl.ds(top, high), pl.ds(left, wide)] = total

    def end(self):
        for i in range(len(self.grads)):
            for way in range(2):
                for step in range(self.STEPS):
                    self.copy(i, way, step).wait_send()


ANY = pl.BlockSpec(memory_space=pl.ANY)
WHOLE = pl.BlockSpec(memory_space=pltpu.VMEM)
VMEM_LIMIT = 56 << 20


def gather_kernel(count, *refs):
    ring = GatherRing(refs[:count], refs[count : 2 * count], refs[2 * count :])
    meet(ring.sides)
    ring.start()
    for step in range(1, ring.STEPS + 1):
        ring.step(step)
    ring.end()


def gather_ring(blocks, ident):
    count = len(blocks)
    return pl.pallas_call(
        functools.partial(gather_kernel, count),
        out_shape=[
            jax.ShapeDtypeStruct((RING * block.shape[0], block.shape[1]), block.dtype)
            for block in blocks
        ],
        in_specs=[ANY] * count,
        out_specs=[ANY] * count,
        scratch_shapes=GatherRing.scratch(count),
        compiler_params=pltpu.CompilerParams(
            collective_id=ident, has_side_effects=True, vmem_limit_bytes=VMEM_LIMIT
        ),
        name="gather_ring",
    )(*blocks)


def scatter_kernel(count, *refs):
    ring = ScatterRing(refs[:count], refs[count : 2 * count], refs[2 * count :])
    ring.load_all()
    meet(ring.sides)
    ring.start()
    for step in range(1, ring.STEPS + 1):
        ring.step(step)
    ring.end()


def scatter_ring(grads, ident):
    count = len(grads)
    return pl.pallas_call(
        functools.partial(scatter_kernel, count),
        out_shape=[
            jax.ShapeDtypeStruct((grad.shape[0] // RING, grad.shape[1]), WIDE) for grad in grads
        ],
        in_specs=[ANY] * count,
        out_specs=[WHOLE] * count,
        scratch_shapes=ScatterRing.scratch([grad.shape for grad in grads]),
        compiler_params=pltpu.CompilerParams(
            collective_id=ident, has_side_effects=True, vmem_limit_bytes=VMEM_LIMIT
        ),
        name="scatter_ring",
    )(*grads)


def gather_dp(blocks, size, ident):
    if size == RING:
        return gather_ring(blocks, ident)
    return [lax.all_gather(block, "dp", axis=0, tiled=True) for block in blocks]


def scatter_dp(grads, size, ident):
    if size == RING:
        return scatter_ring(grads, ident)
    return [
        lax.psum_scatter(grad, "dp", scatter_dimension=0, tiled=True).astype(WIDE)
        for grad in grads
    ]


def beside(ring, blocks, size, ident, before, after):
    blocks = lax.optimization_barrier(tuple(blocks) + tuple(before))[: len(blocks)]
    found = tuple(ring(list(blocks), size, ident))
    held = lax.optimization_barrier(found + tuple(after))
    return held[: len(found)], held[len(found) :]


CORE = [(i, i ^ 1) for i in range(4)]
CHIP = [(i, i ^ 2) for i in range(4)]


def gather_start(own):
    near = lax.ppermute(own, "tensor", CORE)
    far = lax.ppermute(own, "tensor", CHIP)
    return near, far


def gather_end(own, near, far):
    last = lax.ppermute(far, "tensor", CORE)
    return jnp.concatenate([own, near, far, last], axis=0)


def gather_rows(own):
    return gather_end(own, *gather_start(own))


def scatter_start(partial):
    rows = partial.shape[0] // 4
    low = partial.astype(LOW)
    part = [low[b * rows : (b + 1) * rows] for b in range(4)]
    sent = lax.ppermute(jnp.concatenate([part[1], part[3]]), "tensor", CORE)
    here = part[0].astype(WIDE) + sent[:rows].astype(WIDE)
    return here, (part[2].astype(WIDE) + sent[rows:].astype(WIDE)).astype(LOW)


def scatter_rows(partial):
    here, there = scatter_start(partial)
    return here + lax.ppermute(there, "tensor", CHIP).astype(WIDE)


def tensor_peer(hop):
    index = lax.axis_index("tensor")
    if hop == 1:
        return index + 1 - 2 * (index % 2)
    return (index + 2) % 4 if hop == 2 else 3 - index


def tail_kernel(columns, count, *refs):
    here, there, scale, other, x_image, x_text, mid_image, mid_text, text_out = refs[:9]
    grads, refs = refs[9 : 9 + count], refs[9 + count :]
    image_grad, mod_sum, mod_all, *wholes = refs[:5]
    sums, refs = refs[5 : 5 + count], refs[5 + count :]
    far, text_grad, terms, parts, low, slots, far_sem, part_sem, slot_sem, text_sem = refs[:10]
    ring = ScatterRing(grads, sums, refs[10:])
    me, index = lax.axis_index("dp"), lax.axis_index("tensor")
    far_copy = pltpu.make_async_remote_copy(
        src_ref=there, dst_ref=far, send_sem=far_sem.at[0], recv_sem=far_sem.at[1],
        device_id=(me, tensor_peer(2)), device_id_type=MESH,
    )

    def part_copy(hop):
        peer = tensor_peer(hop)
        start = pl.multiple_of(peer * columns, LANES)
        return pltpu.make_async_remote_copy(
            src_ref=terms.at[:, pl.ds(start, columns)], dst_ref=parts.at[hop - 1],
            send_sem=part_sem.at[0, hop - 1], recv_sem=part_sem.at[1, hop - 1],
            device_id=(me, peer), device_id_type=MESH,
        )

    def slot_copy(hop):
        return pltpu.make_async_remote_copy(
            src_ref=low, dst_ref=slots.at[me],
            send_sem=slot_sem.at[0, hop - 1], recv_sem=slot_sem.at[1, hop - 1],
            device_id=((me + hop) % RING, index), device_id_type=MESH,
        )

    def text_copy(i, hop):
        source = (text_out, text_grad)[i]
        return pltpu.make_async_remote_copy(
            src_ref=source, dst_ref=wholes[i].at[index],
            send_sem=text_sem.at[i, 0, hop], recv_sem=text_sem.at[i, 1, hop],
            device_id=(me, tensor_peer(hop)), device_id_type=MESH,
        )

    def text_own(i):
        source = (text_out, text_grad)[i]
        return pltpu.make_async_copy(source, wholes[i].at[index], text_sem.at[i, 0, 0])

    def rows_back(first, x, middle, gain):
        x = x.astype(WIDE)
        centred = x - jnp.mean(x, axis=-1, keepdims=True)
        spread = lax.rsqrt(jnp.mean(centred * centred, axis=-1, keepdims=True) + EPS)
        normed = centred * spread
        wide = first * gain
        inner = jnp.mean(wide, axis=-1, keepdims=True)
        cross = jnp.mean(wide * normed, axis=-1, keepdims=True)
        sums = jnp.sum(first, axis=0, keepdims=True), jnp.sum(first * normed, axis=0, keepdims=True)
        return middle + (wide - inner - normed * cross) * spread, *sums

    ring.load_all()
    meet(
        [(me, tensor_peer(hop)) for hop in (1, 2, 3)]
        + [((me + hop) % RING, index) for hop in range(1, RING)]
    )
    far_copy.start()
    ring.start()
    ring.step(1)
    far_copy.wait()
    terms[...] = other[...]
    chunk = 64

    def image_chunk(at, totals):
        rows = pl.ds(pl.multiple_of(at * chunk, chunk), chunk)
        first = here[rows] + far[rows].astype(WIDE)
        out, shift, gain = rows_back(first, x_image[rows], mid_image[rows], scale[0:1])
        image_grad[rows] = out
        return totals[0] + shift, totals[1] + gain

    zero = jnp.zeros((1, here.shape[1]), WIDE)
    image_rows = x_image.shape[0]
    shift, gain = lax.fori_loop(0, image_rows // chunk, image_chunk, (zero, zero))
    terms[0:1] = shift
    terms[1:2] = gain
    ring.step(2)
    text_first = here[image_rows:] + far[image_rows:].astype(WIDE)
    out, shift, gain = rows_back(text_first, x_text[...], mid_text[...], scale[1:2])
    text_grad[...] = out
    for i in range(2):
        text_own(i).start()
        for hop in (1, 2, 3):
            text_copy(i, hop).start()
    terms[6:7] = shift
    terms[7:8] = gain
    for hop in (1, 2, 3):
        part_copy(hop).start()
    ring.step(3)
    for hop in (1, 2, 3):
        part_copy(hop).wait()
    own = terms[:, pl.ds(pl.multiple_of(index * columns, LANES), columns)]
    total = own + parts[0] + parts[1] + parts[2]
    mod_sum[...] = total
    low[...] = total.astype(LOW)
    slots[pl.ds(me, 1)] = total.astype(LOW)[None]
    for hop in range(1, RING):
        slot_copy(hop).start()
    ring.step(4)
    ring.step(5)
    for hop in range(1, RING):
        slot_copy(hop).wait()
    mod_all[...] = slots[...]
    ring.step(6)
    for i in range(2):
        text_own(i).wait()
        for hop in (1, 2, 3):
            text_copy(i, hop).wait()
    ring.step(7)
    ring.end()


def tail_ring(here, there, scale, other, x, middle, text_out, grads, columns, ident):
    width, shapes = here.shape[1], [grad.shape for grad in grads]
    rows, text_rows = x[0].shape[0], x[1].shape[0]
    found = pl.pallas_call(
        functools.partial(tail_kernel, columns, len(grads)),
        out_shape=[
            jax.ShapeDtypeStruct((rows, width), WIDE),
            jax.ShapeDtypeStruct((16, columns), WIDE),
            jax.ShapeDtypeStruct((RING, 16, columns), LOW),
            jax.ShapeDtypeStruct((4, text_rows, width), LOW),
            jax.ShapeDtypeStruct((4, text_rows, width), WIDE),
            *[jax.ShapeDtypeStruct((r // RING, c), WIDE) for r, c in shapes],
        ],
        in_specs=[WHOLE] * 9 + [ANY] * len(grads),
        out_specs=[WHOLE] * 3 + [ANY] * 2 + [WHOLE] * len(grads),
        scratch_shapes=[
            pltpu.VMEM((rows + text_rows, width), LOW),
            pltpu.VMEM((text_rows, width), WIDE),
            pltpu.VMEM((16, width), WIDE),
            pltpu.VMEM((3, 16, columns), WIDE),
            pltpu.VMEM((16, columns), LOW),
            pltpu.VMEM((RING, 16, columns), LOW),
            pltpu.SemaphoreType.DMA((2,)),
            pltpu.SemaphoreType.DMA((2, 3)),
            pltpu.SemaphoreType.DMA((2, RING - 1)),
            pltpu.SemaphoreType.DMA((2, 2, 4)),
            *ScatterRing.scratch(shapes),
        ],
        compiler_params=pltpu.CompilerParams(
            collective_id=ident, has_side_effects=True, vmem_limit_bytes=VMEM_LIMIT
        ),
        name="tail_ring",
    )(here, there, scale, other, *x, *middle, text_out, *grads)
    return found


def head_lanes(head):
    lane = lax.broadcasted_iota(jnp.int32, (1, LANES), 1)
    return (lane < HEAD_DIM) if head == 0 else (lane >= HEAD_DIM)


def attend_pair(split, bias_ref, q_ref, k_ref, v_ref, out_ref, lse_ref):
    scale = HEAD_DIM ** (-0.5)
    bias = bias_ref[...]
    outs, totals = [], []
    for head in range(2):
        mine = head_lanes(head)
        queries = jnp.where(mine, q_ref[...] * scale, 0).astype(LOW)
        image = dot(queries, k_ref[:split], NT)
        text = dot(queries, k_ref[split:], NT) + bias
        top = jnp.maximum(
            jnp.max(image, axis=1, keepdims=True), jnp.max(text, axis=1, keepdims=True)
        )
        image = jnp.exp(image - top).astype(LOW)
        text = jnp.exp(text - top).astype(LOW)
        values = jnp.where(mine, v_ref[...], 1).astype(LOW)
        both = dot(image, values[:split], NN) + dot(text, values[split:], NN)
        sums = pltpu.roll(both, HEAD_DIM, 1)
        outs.append(both / sums)
        totals.append(top + jnp.log(sums))
    first = head_lanes(0)
    out_ref[...] = jnp.where(first, outs[0], outs[1]).astype(out_ref.dtype)
    flipped = jnp.where(first, totals[0], totals[1]).T
    lse_ref[0] = jnp.concatenate([flipped[:4], flipped[HEAD_DIM : HEAD_DIM + 4]], axis=0)


def first_kernel(chunk, *refs):
    x_image, x_text, cot_image, cot_text, cond, ada, *blocks = refs[:8]
    outs, fulls, pool, (mods, conds), refs = refs[8:11], refs[11:13], refs[13:14], refs[14:16], refs[16:]
    mines, pooled, (row_sem, own_sem) = refs[:3], refs[3], refs[4:6]
    cond_got, parts, got, cond_sem, part_sem, mod_sem = refs[6:12]
    ring = GatherRing(blocks, fulls, refs[12:15])
    text_ring = GatherRing([pooled], pool, refs[15:18])
    me, index = lax.axis_index("dp"), lax.axis_index("tensor")
    width, columns = mods.shape[1], ada.shape[2]

    def dp_copy(hop, source, target, sem):
        peer = (me + hop) % RING
        return pltpu.make_async_remote_copy(
            src_ref=source.at[peer], dst_ref=target.at[me],
            send_sem=sem.at[0, hop - 1], recv_sem=sem.at[1, hop - 1],
            device_id=(peer, index), device_id_type=MESH,
        )

    def mod_copy(hop):
        here = mods.at[:, pl.ds(pl.multiple_of(index * columns, LANES), columns)]
        return pltpu.make_async_remote_copy(
            src_ref=here, dst_ref=here,
            send_sem=mod_sem.at[0, hop - 1], recv_sem=mod_sem.at[1, hop - 1],
            device_id=(me, tensor_peer(hop)), device_id_type=MESH,
        )

    def row_copy(i, source, slot, hop, sem):
        rows = mines[i].shape[0]
        return pltpu.make_async_remote_copy(
            src_ref=source, dst_ref=outs[i].at[pl.ds(slot * rows, rows)],
            send_sem=row_sem.at[i, 0, sem], recv_sem=row_sem.at[i, 1, sem],
            device_id=(me, tensor_peer(hop)), device_id_type=MESH,
        )

    def own(i):
        rows = mines[i].shape[0]
        return pltpu.make_async_copy(mines[i], outs[i].at[pl.ds(0, rows)], own_sem.at[i])

    def to_far(i):
        return row_copy(i, mines[i], 2, 2, 0)

    def to_near(i):
        return row_copy(i, mines[i], 1, 1, 1)

    def forward(i):
        rows = mines[i].shape[0]
        return row_copy(i, outs[i].at[pl.ds(2 * rows, rows)], 3, 1, 2)

    def send(i):
        to_far(i).start()
        to_near(i).start()
        own(i).start()

    def norm_rows(x, stream):
        x = x.astype(WIDE)
        centred = x - jnp.mean(x, axis=-1, keepdims=True)
        spread = lax.rsqrt(jnp.mean(centred * centred, axis=-1, keepdims=True) + EPS)
        gain, shift = 1.0 + mods[6 * stream + 1 : 6 * stream + 2], mods[6 * stream : 6 * stream + 1]
        return (centred * spread * gain + shift).astype(LOW)

    def over_chunks(body):
        def step(i, _):
            body(pl.ds(pl.multiple_of(i * chunk, chunk), chunk))
            return 0

        lax.fori_loop(0, x_image.shape[0] // chunk, step, 0)

    meet(
        [(me, tensor_peer(hop)) for hop in (1, 2, 3)]
        + [((me + hop) % RING, index) for hop in range(1, RING)]
    )
    for hop in range(1, RING):
        dp_copy(hop, cond, cond_got, cond_sem).start()
    cond_got[pl.ds(me, 1)] = cond[pl.ds(me, 1)]
    parts[...] = jnp.zeros_like(parts)
    for hop in range(1, RING):
        dp_copy(hop, cond, cond_got, cond_sem).wait()
    rows = jnp.concatenate([cond_got[n, 0:1] for n in range(RING)], axis=0)
    conds[...] = rows
    rows = rows.astype(LOW)
    for which in range(12):
        part = dot(rows, ada[which], NN)
        for n in range(RING):
            parts[n, which : which + 1] = part[n : n + 1]
    for hop in range(1, RING):
        dp_copy(hop, parts, got, part_sem).start()
    ring.start()
    got[pl.ds(me, 1)] = parts[pl.ds(me, 1)]
    for hop in range(1, RING):
        dp_copy(hop, parts, got, part_sem).wait()
    mods[:, pl.ds(pl.multiple_of(index * columns, LANES), columns)] = jnp.sum(got[...], axis=0)
    for hop in (1, 2, 3):
        mod_copy(hop).start()
    for hop in (1, 2, 3):
        mod_copy(hop).wait()
    pooled[...] = (mods[11:12] * cot_text[: pooled.shape[0]].astype(WIDE)).astype(LOW)
    text_ring.start()

    def norm_chunk(some):
        mines[0][some] = norm_rows(x_image[some], 0)

    def grad_chunk(some):
        mines[2][some] = (mods[5:6] * cot_image[some].astype(WIDE)).astype(LOW)

    over_chunks(norm_chunk)
    send(0)
    mines[1][...] = norm_rows(x_text[...], 1)
    send(1)
    over_chunks(grad_chunk)
    send(2)
    ring.step(1)
    text_ring.step(1)
    for i in range(2):
        to_far(i).wait()
        forward(i).start()
    ring.step(2)
    text_ring.step(2)
    to_far(2).wait()
    forward(2).start()
    ring.step(3)
    text_ring.step(3)
    for i in range(3):
        own(i).wait()
        to_near(i).wait()
        forward(i).wait()
    text_ring.step(4)
    ring.step(4)
    text_ring.end()
    ring.end()


def first_ring(x, cotangent, cond, ada, blocks, pool_rows, ident):
    width, columns, depth = x[0].shape[1], ada.shape[2], ada.shape[1]
    rows = [x[0].shape[0], x[1].shape[0], x[0].shape[0]]
    fulls = [block.shape for block in blocks] + [(pool_rows, width)]
    cond = jnp.broadcast_to(cond.astype(WIDE)[:, None], (RING, 8, depth))
    found = pl.pallas_call(
        functools.partial(first_kernel, 64),
        in_specs=[WHOLE] * 6 + [ANY] * 2,
        out_specs=[ANY] * 6 + [WHOLE] * 2,
        out_shape=[
            *[jax.ShapeDtypeStruct((4 * n, width), LOW) for n in rows],
            *[jax.ShapeDtypeStruct((RING * n, wide), LOW) for n, wide in fulls],
            jax.ShapeDtypeStruct((16, width), WIDE),
            jax.ShapeDtypeStruct((RING, depth), WIDE),
        ],
        scratch_shapes=[
            *[pltpu.VMEM((n, width), LOW) for n in rows],
            pltpu.VMEM((pool_rows, width), LOW),
            pltpu.SemaphoreType.DMA((3, 2, 3)),
            pltpu.SemaphoreType.DMA((3,)),
            pltpu.VMEM((RING, 8, depth), WIDE),
            *[pltpu.VMEM((RING, 16, columns), WIDE)] * 2,
            *[pltpu.SemaphoreType.DMA((2, RING - 1))] * 2,
            pltpu.SemaphoreType.DMA((2, 3)),
            *GatherRing.scratch(2),
            *GatherRing.scratch(1),
        ],
        compiler_params=pltpu.CompilerParams(
            collective_id=ident, has_side_effects=True, vmem_limit_bytes=VMEM_LIMIT
        ),
        name="first_ring",
    )(*x, *cotangent, cond, ada, *blocks)
    return found[:2], found[2], found[3:5], found[5], found[6][:12], found[7]


def exchange_sums(part, sent, got, sems, me):
    copy = pltpu.make_async_remote_copy(
        src_ref=sent, dst_ref=got, send_sem=sems.at[0, 0], recv_sem=sems.at[1, 0],
        device_id=(me, tensor_peer(1)), device_id_type=MESH,
    )
    sent[0] = part(1).astype(LOW)
    sent[1] = part(3).astype(LOW)
    copy.start()
    return copy


def middle_kernel(split, chunk, *refs):
    bias_ref, q_ref, k_ref, v_ref, x_image, x_text, mods = refs[:7]
    out_blocks, ffn_blocks, refs = refs[7:9], refs[9:11], refs[11:]
    mixed, lse_ref, *wide_outs, text_in, image_in = refs[:8]
    branch_image, branch_text, mid_image, mid_text = wide_outs
    pool, out_fulls, ffn_fulls, refs = refs[8:9], refs[9:11], refs[11:13], refs[13:]
    weights, sent, got, far_sent, far_got, here, mine = refs[:7]
    sems, weight_sem, row_sem, own_sem = refs[7:11]
    first = GatherRing(out_blocks, out_fulls, refs[11:14])
    second = GatherRing(ffn_blocks, ffn_fulls, refs[14:17])
    third = GatherRing([text_in.at[pl.ds(0, pool[0].shape[0] // RING)]], pool, refs[17:20])
    me = lax.axis_index("dp")
    block = q_ref.shape[0]
    pair, at = pl.program_id(0), pl.program_id(0) * 2 + pl.program_id(1)
    rows = x_image.shape[0]

    @pl.when(at == 0)
    def _():
        meet([*first.sides, *[(me, tensor_peer(hop)) for hop in (1, 2)]])
        first.start()

    for step in range(1, 5):

        @pl.when(at == step)
        def _():
            first.step(step)

    weight_copies = [
        pltpu.make_async_copy(out_fulls[s], weights.at[s], weight_sem.at[s]) for s in range(2)
    ]

    @pl.when(at == 4)
    def _():
        first.end()
        second.start()
        for copy in weight_copies:
            copy.start()

    place = (
        pl.ds(pl.multiple_of(pl.program_id(1) * block, block), block),
        pl.ds(pl.multiple_of(pair * LANES, LANES), LANES),
    )
    attend_pair(split, bias_ref, q_ref, k_ref, v_ref, mixed.at[place], lse_ref)

    @pl.when(at == 2 * pl.num_programs(0) - 1)
    def _():
        for copy in weight_copies:
            copy.wait()
        text_rows = x_text.shape[0]

        def part(b):
            image = dot(mixed[b * rows : (b + 1) * rows], weights[0], NN)
            low = split + b * text_rows
            text = dot(mixed[low : low + text_rows], weights[1], NN)
            return jnp.concatenate([image, text], axis=0)

        near = exchange_sums(part, sent, got, sems, me)
        here[...] = part(0)
        far_sent[...] = part(2).astype(LOW)
        near.wait()
        far_sent[...] = (far_sent[...].astype(WIDE) + got[1].astype(WIDE)).astype(LOW)
        far = pltpu.make_async_remote_copy(
            src_ref=far_sent, dst_ref=far_got, send_sem=sems.at[0, 1], recv_sem=sems.at[1, 1],
            device_id=(me, tensor_peer(2)), device_id_type=MESH,
        )
        far.start()
        here[...] += got[0].astype(WIDE)
        second.step(1)
        far.wait()

        def norm_rows(x, branch, stream):
            middle = x.astype(WIDE) + mods[3 * stream : 3 * stream + 1] * branch
            centred = middle - jnp.mean(middle, axis=-1, keepdims=True)
            spread = lax.rsqrt(jnp.mean(centred * centred, axis=-1, keepdims=True) + EPS)
            gain, shift = mods[3 * stream + 1 : 3 * stream + 2], mods[3 * stream + 2 : 3 * stream + 3]
            return middle, (centred * spread * gain + shift).astype(LOW)

        def image_chunk(i, _):
            some = pl.ds(pl.multiple_of(i * chunk, chunk), chunk)
            branch = here[some] + far_got[some].astype(WIDE)
            branch_image[some] = branch
            middle, low = norm_rows(x_image[some], branch, 0)
            mid_image[some] = middle
            mine[some] = low
            return 0

        lax.fori_loop(0, rows // chunk, image_chunk, 0)

        def row_copy(source, slot, hop, sem):
            return pltpu.make_async_remote_copy(
                src_ref=source, dst_ref=image_in.at[pl.ds(slot * rows, rows)],
                send_sem=row_sem.at[0, sem], recv_sem=row_sem.at[1, sem],
                device_id=(me, tensor_peer(hop)), device_id_type=MESH,
            )

        own = pltpu.make_async_copy(mine, image_in.at[pl.ds(0, rows)], own_sem.at[0])
        to_far, to_near = row_copy(mine, 2, 2, 0), row_copy(mine, 1, 1, 1)
        to_far.start()
        to_near.start()
        own.start()
        branch = here[rows:] + far_got[rows:].astype(WIDE)
        branch_text[...] = branch
        middle, low = norm_rows(x_text[...], branch, 1)
        mid_text[...] = middle
        text_in[...] = low
        third.start()
        second.step(2)
        third.step(1)
        to_far.wait()
        last = row_copy(image_in.at[pl.ds(2 * rows, rows)], 3, 1, 2)
        last.start()
        third.step(2)
        second.step(3)
        third.step(3)
        own.wait()
        to_near.wait()
        last.wait()
        third.step(4)
        second.step(4)
        second.end()
        third.end()


def middle_ring(joint, bias, x, mods, split, heads, out_blocks, ffn_blocks, pool_rows, ident):
    rows, pairs, block = joint.shape[0], heads // 2, joint.shape[0] // 2
    whole = lambda part: pl.BlockSpec((rows, LANES), lambda h, i: (0, part * pairs + h))
    image_rows, width = x[0].shape
    text_rows = x[1].shape[0]
    both = image_rows + text_rows
    depth = heads * HEAD_DIM
    found = pl.pallas_call(
        functools.partial(middle_kernel, split, 64),
        grid=(pairs, 2),
        in_specs=[
            pl.BlockSpec((1, rows - split), lambda h, i: (0, 0)),
            pl.BlockSpec((block, LANES), lambda h, i: (i, h)),
            whole(1),
            whole(2),
            *[WHOLE] * 3,
            *[ANY] * 4,
        ],
        out_specs=[
            WHOLE,
            pl.BlockSpec((1, 8, block), lambda h, i: (h, 0, i)),
            *[WHOLE] * 5,
            *[ANY] * 6,
        ],
        out_shape=[
            jax.ShapeDtypeStruct((rows, depth), LOW),
            jax.ShapeDtypeStruct((pairs, 8, rows), WIDE),
            *[jax.ShapeDtypeStruct((n, width), WIDE) for n in (image_rows, text_rows) * 2],
            jax.ShapeDtypeStruct((text_rows, width), LOW),
            jax.ShapeDtypeStruct((4 * image_rows, width), LOW),
            jax.ShapeDtypeStruct((RING * pool_rows, width), LOW),
            *[
                jax.ShapeDtypeStruct((RING * b.shape[0], b.shape[1]), b.dtype)
                for b in (*out_blocks, *ffn_blocks)
            ],
        ],
        scratch_shapes=[
            pltpu.VMEM((2, depth, width), LOW),
            pltpu.VMEM((2, both, width), LOW),
            pltpu.VMEM((2, both, width), LOW),
            pltpu.VMEM((both, width), LOW),
            pltpu.VMEM((both, width), LOW),
            pltpu.VMEM((both, width), WIDE),
            pltpu.VMEM((image_rows, width), LOW),
            pltpu.SemaphoreType.DMA((2, 2)),
            pltpu.SemaphoreType.DMA((2,)),
            pltpu.SemaphoreType.DMA((2, 3)),
            pltpu.SemaphoreType.DMA((1,)),
            *GatherRing.scratch(2),
            *GatherRing.scratch(2),
            *GatherRing.scratch(1),
        ],
        compiler_params=pltpu.CompilerParams(
            collective_id=ident, has_side_effects=True, vmem_limit_bytes=VMEM_LIMIT
        ),
        name="middle_ring",
    )(bias, joint, joint, joint, *x, mods, *out_blocks, *ffn_blocks)
    return found


def back_kernel(split, chunk, *refs):
    bias_ref, q_ref, k_ref, v_ref, o_ref, lse_ref = refs[:6]
    mid_image, mid_text, cot_image, cot_text, mods, text_part = refs[6:12]
    partial, out_weights, grads, theirs, refs = refs[12], refs[13:15], refs[15:17], refs[17:19], refs[19:]
    dq_ref, dk_ref, dv_ref, image_second, image_grad, text_grad = refs[:6]
    image_rows, text_rows, *fars = refs[6:10]
    sums, text_second, refs = refs[10:12], refs[12], refs[13:]
    dk_acc, dv_acc, weights, parts, got, far_sent, far_got, rows_in, mixed_grad = refs[:9]
    part_sem, sems, row_sem, weight_sem, rows_sem, far_sem, text_sum = refs[9:16]
    ring = ScatterRing(grads, sums, refs[16:23])
    text_ring = ScatterRing([text_part], [text_sum], refs[23:])
    me = lax.axis_index("dp")
    rows, texts = mid_image.shape[0], mid_text.shape[0]
    block = q_ref.shape[0]
    at = pl.program_id(0) * pl.num_programs(1) + pl.program_id(1)
    last = pl.num_programs(0) * pl.num_programs(1) - 1

    def part_of(b):
        return partial.at[pl.ds(b * rows, rows)]

    def keep(i):
        return pltpu.make_async_copy(part_of(2 * i), parts.at[i], part_sem.at[i])

    def near(i):
        return pltpu.make_async_remote_copy(
            src_ref=part_of(2 * i + 1), dst_ref=got.at[i],
            send_sem=sems.at[0, i], recv_sem=sems.at[1, i],
            device_id=(me, tensor_peer(1)), device_id_type=MESH,
        )

    def row_copy(source, slot, hop, sem):
        return pltpu.make_async_remote_copy(
            src_ref=source, dst_ref=rows_in.at[slot],
            send_sem=row_sem.at[0, sem], recv_sem=row_sem.at[1, sem],
            device_id=(me, tensor_peer(hop)), device_id_type=MESH,
        )

    def weight(s):
        return pltpu.make_async_copy(out_weights[s], weights.at[s], weight_sem.at[s])

    def save(b, s):
        low, high, whole = ((0, rows, image_rows), (rows, texts, text_rows))[s]
        return pltpu.make_async_copy(
            rows_in.at[b, pl.ds(low, high)], whole.at[pl.ds(b * high, high)], rows_sem.at[s, b]
        )

    def rows_back(second, middle, cotangent, stream):
        centred = middle - jnp.mean(middle, axis=-1, keepdims=True)
        spread = lax.rsqrt(jnp.mean(centred * centred, axis=-1, keepdims=True) + EPS)
        normed = centred * spread
        wide = second * mods[2 * stream + 1 : 2 * stream + 2]
        inner = jnp.mean(wide, axis=-1, keepdims=True)
        cross = jnp.mean(wide * normed, axis=-1, keepdims=True)
        grad = cotangent.astype(WIDE) + (wide - inner - normed * cross) * spread
        return grad, (mods[2 * stream : 2 * stream + 1] * grad).astype(LOW)

    @pl.when(at == 0)
    def _():
        for i in range(2):
            keep(i).start()
            weight(i).start()
        text_ring.load_all()
        ring.load_all()
        meet([*ring.sides, *[(me, tensor_peer(hop)) for hop in (1, 2)]])
        for i in range(2):
            near(i).start()
        text_ring.start()
        ring.start()
        for i in range(2):
            keep(i).wait()
            near(i).wait()
        far_sent[...] = (parts[1].astype(WIDE) + got[1].astype(WIDE)).astype(LOW)
        far = pltpu.make_async_remote_copy(
            src_ref=far_sent, dst_ref=far_got, send_sem=sems.at[0, 2], recv_sem=sems.at[1, 2],
            device_id=(me, tensor_peer(2)), device_id_type=MESH,
        )
        far.start()
        for step in range(1, 4):
            text_ring.step(step)
        ring.step(1)
        far.wait()

        def image_chunk(i, _):
            some = pl.ds(pl.multiple_of(i * chunk, chunk), chunk)
            second = parts[0, some].astype(WIDE) + got[0, some].astype(WIDE)
            second = second + far_got[some].astype(WIDE)
            image_second[some] = second
            grad, low = rows_back(second, mid_image[some], cot_image[some], 0)
            image_grad[some] = grad
            rows_in[0, some] = low
            return 0

        text_ring.step(4)
        lax.fori_loop(0, rows // chunk, image_chunk, 0)
        for step in range(5, 8):
            text_ring.step(step)
        pooled = text_sum.shape[0]
        text_second[...] = jnp.zeros_like(text_second)
        text_second[:pooled] = text_sum[...]
        grad, low = rows_back(text_second[...], mid_text[...], cot_text[...], 1)
        text_grad[...] = grad
        rows_in[0, rows:] = low
        to_far = row_copy(rows_in.at[0], 2, 2, 0)
        to_near = row_copy(rows_in.at[0], 1, 1, 1)
        to_far.start()
        to_near.start()
        ring.step(2)
        to_far.wait()
        forward = row_copy(rows_in.at[2], 3, 1, 2)
        forward.start()
        for i in range(2):
            weight(i).wait()
        to_near.wait()

        def through(b):
            image = dot(rows_in[b, :rows], weights[0], NT).astype(LOW)
            mixed_grad[b * rows : (b + 1) * rows] = image
            text = dot(rows_in[b, rows:], weights[1], NT).astype(LOW)
            mixed_grad[split + b * texts : split + (b + 1) * texts] = text

        for b in range(3):
            through(b)
        ring.step(3)
        forward.wait()
        through(3)
        for b in range(4):
            for s in range(2):
                save(b, s).start()

    far_copies = [
        pltpu.make_async_remote_copy(
            src_ref=theirs[s], dst_ref=fars[s], send_sem=far_sem.at[0, s], recv_sem=far_sem.at[1, s],
            device_id=(me, tensor_peer(2)), device_id_type=MESH,
        )
        for s in range(2)
    ]

    @pl.when(at == 1)
    def _():
        for copy in far_copies:
            copy.start()

    for step, when in ((4, 3), (5, 8), (6, 13)):

        @pl.when(at == when)
        def _():
            ring.step(step)

    place = (
        pl.ds(pl.multiple_of(pl.program_id(1) * block, block), block),
        pl.ds(pl.multiple_of(pl.program_id(0) * LANES, LANES), LANES),
    )
    attend_back_pair(
        split,
        (bias_ref, q_ref, k_ref, v_ref, o_ref, mixed_grad.at[place], lse_ref)
        + (dq_ref, dk_ref, dv_ref, dk_acc, dv_acc),
    )

    @pl.when(at == last)
    def _():
        ring.step(7)
        ring.end()
        text_ring.end()
        for copy in far_copies:
            copy.wait()
        for b in range(4):
            for s in range(2):
                save(b, s).wait()


def back_ring(
    joint, bias, mixed, lse, split, heads, text_part, middle, cotangent, mods, partial,
    out_weights, grads, theirs, ident, block=256,
):
    rows, pairs = joint.shape[0], heads // 2
    whole = lambda part: pl.BlockSpec((rows, LANES), lambda h, i: (0, part * pairs + h))
    some = pl.BlockSpec((block, LANES), lambda h, i: (i, h))
    image_rows, width = middle[0].shape
    texts = middle[1].shape[0]
    depth, pooled = heads * HEAD_DIM, text_part.shape[0] // RING
    found = pl.pallas_call(
        functools.partial(back_kernel, split, 64),
        grid=(pairs, rows // block),
        in_specs=[
            pl.BlockSpec((rows - split, 1), lambda h, i: (0, 0)),
            some,
            whole(1),
            whole(2),
            some,
            pl.BlockSpec((1, 8, block), lambda h, i: (h, 0, i)),
            *[WHOLE] * 5,
            *[ANY] * 8,
        ],
        out_specs=[some, whole(0), whole(0), *[WHOLE] * 3, *[ANY] * 4, *[WHOLE] * 3],
        out_shape=[
            *[jax.ShapeDtypeStruct((rows, depth), LOW)] * 3,
            *[jax.ShapeDtypeStruct((n, width), WIDE) for n in (image_rows, image_rows, texts)],
            *[jax.ShapeDtypeStruct((4 * n, width), LOW) for n in (image_rows, texts)],
            *[jax.ShapeDtypeStruct(t.shape, t.dtype) for t in theirs],
            *[jax.ShapeDtypeStruct((g.shape[0] // RING, g.shape[1]), WIDE) for g in grads],
            jax.ShapeDtypeStruct((texts, width), WIDE),
        ],
        scratch_shapes=[
            *[pltpu.VMEM((rows, LANES), WIDE)] * 2,
            pltpu.VMEM((2, depth, width), LOW),
            *[pltpu.VMEM((2, image_rows, width), LOW)] * 2,
            *[pltpu.VMEM((image_rows, width), LOW)] * 2,
            pltpu.VMEM((4, image_rows + texts, width), LOW),
            pltpu.VMEM((rows, depth), LOW),
            pltpu.SemaphoreType.DMA((2,)),
            pltpu.SemaphoreType.DMA((2, 3)),
            pltpu.SemaphoreType.DMA((2, 3)),
            pltpu.SemaphoreType.DMA((2,)),
            pltpu.SemaphoreType.DMA((2, 4)),
            pltpu.SemaphoreType.DMA((2, 2)),
            pltpu.VMEM((pooled, width), WIDE),
            *ScatterRing.scratch([g.shape for g in grads]),
            *ScatterRing.scratch([text_part.shape]),
        ],
        compiler_params=pltpu.CompilerParams(
            collective_id=ident, has_side_effects=True, vmem_limit_bytes=VMEM_LIMIT
        ),
        name="back_ring",
    )(
        bias.T, joint, joint, joint, mixed, lse, *middle, *cotangent, mods, text_part,
        partial, *out_weights, *grads, *theirs,
    )
    return found


def attend_kernel(split, count, waits, *refs):
    bias_ref, q_ref, k_ref, v_ref = refs[:4]
    blocks, (out_ref, lse_ref) = refs[4 : 4 + count], refs[4 + count : 6 + count]
    at = pl.program_id(0) * pl.num_programs(1) + pl.program_id(1)
    if count:
        ring = GatherRing(blocks, refs[6 + count : 6 + 2 * count], refs[6 + 2 * count :])

        @pl.when(at == 0)
        def _():
            meet(ring.sides)
            ring.start()

        for step, when in enumerate(waits):

            @pl.when(at == when)
            def _():
                ring.step(step + 1)

    attend_pair(split, bias_ref, q_ref, k_ref, v_ref, out_ref, lse_ref)
    if count:

        @pl.when(at == pl.num_programs(0) * pl.num_programs(1) - 1)
        def _():
            for step in range(len(waits) + 1, ring.STEPS + 1):
                ring.step(step)
            ring.end()


def attend(joint, bias, split, heads, blocks, ident, waits):
    rows, pairs, count, block = joint.shape[0], heads // 2, len(blocks), joint.shape[0] // 2
    whole = lambda part: pl.BlockSpec((rows, LANES), lambda h, i: (0, part * pairs + h))
    extra = dict(collective_id=ident, has_side_effects=True) if count else {}
    found = pl.pallas_call(
        functools.partial(attend_kernel, split, count, waits),
        grid=(pairs, 2),
        in_specs=[
            pl.BlockSpec((1, rows - split), lambda h, i: (0, 0)),
            pl.BlockSpec((block, LANES), lambda h, i: (i, h)),
            whole(1),
            whole(2),
            *[ANY] * count,
        ],
        out_specs=[
            pl.BlockSpec((block, LANES), lambda h, i: (i, h)),
            pl.BlockSpec((1, 8, block), lambda h, i: (h, 0, i)),
            *[ANY] * count,
        ],
        out_shape=[
            jax.ShapeDtypeStruct((rows, heads * HEAD_DIM), LOW),
            jax.ShapeDtypeStruct((pairs, 8, rows), WIDE),
            *[jax.ShapeDtypeStruct((RING * b.shape[0], b.shape[1]), b.dtype) for b in blocks],
        ],
        scratch_shapes=GatherRing.scratch(count) if count else [],
        compiler_params=pltpu.CompilerParams(vmem_limit_bytes=VMEM_LIMIT, **extra),
        name="attend",
    )(bias, joint, joint, joint, *blocks)
    return found[0], found[1], found[2:]


def attend_back_pair(split, refs):
    (bias_ref, q_ref, k_ref, v_ref, o_ref, g_ref, lse_ref, dq_ref, dk_ref, dv_ref, dk_acc, dv_acc) = refs
    step = pl.program_id(1)
    scale = HEAD_DIM ** (-0.5)

    @pl.when(step == 0)
    def _():
        dk_acc[...] = jnp.zeros_like(dk_acc)
        dv_acc[...] = jnp.zeros_like(dv_acc)

    product = (g_ref[...].astype(WIDE) * o_ref[...].astype(WIDE)).T
    bias = bias_ref[...]
    dq = None
    for head in range(2):
        mine = head_lanes(head)
        queries = jnp.where(mine, q_ref[...] * scale, 0).astype(LOW)
        grads = jnp.where(mine, g_ref[...], 0).astype(LOW)
        keys = jnp.where(mine, k_ref[...], 0).astype(LOW)
        own = product[head * HEAD_DIM : (head + 1) * HEAD_DIM]
        delta = jnp.sum(own, axis=0, keepdims=True)
        total = lse_ref[0][4 * head : 4 * head + 1]
        for low, high in ((0, split), (split, k_ref.shape[0])):
            scores = dot(k_ref[low:high], queries, NT)
            if low:
                scores = scores + bias
            probs = jnp.exp(scores - total)
            grad_probs = dot(v_ref[low:high], grads, NT)
            grad_scores = (probs * (grad_probs - delta)).astype(LOW)
            dv_acc[low:high] += dot(probs.astype(LOW), grads, NN)
            dk_acc[low:high] += dot(grad_scores, queries, NN)
            part = dot(grad_scores, keys[low:high], TN)
            dq = part if dq is None else dq + part
    dq_ref[...] = (dq * scale).astype(LOW)

    @pl.when(step == pl.num_programs(1) - 1)
    def _():
        dk_ref[...] = dk_acc[...].astype(LOW)
        dv_ref[...] = dv_acc[...].astype(LOW)


def attend_back_kernel(split, count, waits, *refs):
    ins, rest = refs[:7], refs[7:]
    grads, outs, rest = rest[:count], rest[count : count + 3], rest[count + 3 :]
    sums, accs, rest = rest[:count], rest[count : count + 2], rest[count + 2 :]
    at = pl.program_id(0) * pl.num_programs(1) + pl.program_id(1)
    if count:
        ring = ScatterRing(grads, sums, rest)

        @pl.when(at == 0)
        def _():
            ring.load_all()
            meet(ring.sides)
            ring.start()

        for step, when in enumerate(waits):

            @pl.when(at == when)
            def _():
                ring.step(step + 1)

    attend_back_pair(split, (*ins, *outs, *accs))
    if count:

        @pl.when(at == pl.num_programs(0) * pl.num_programs(1) - 1)
        def _():
            for step in range(len(waits) + 1, ring.STEPS + 1):
                ring.step(step)
            ring.end()


def attend_back(joint, bias, mixed, grad, lse, split, heads, grads, ident, waits):
    rows, pairs, count, block = joint.shape[0], heads // 2, len(grads), joint.shape[0] // 2
    whole = lambda part: pl.BlockSpec((rows, LANES), lambda h, i: (0, part * pairs + h))
    some = pl.BlockSpec((block, LANES), lambda h, i: (i, h))
    extra = dict(collective_id=ident, has_side_effects=True) if count else {}
    found = pl.pallas_call(
        functools.partial(attend_back_kernel, split, count, waits),
        grid=(pairs, 2),
        in_specs=[
            pl.BlockSpec((rows - split, 1), lambda h, i: (0, 0)),
            some,
            whole(1),
            whole(2),
            some,
            some,
            pl.BlockSpec((1, 8, block), lambda h, i: (h, 0, i)),
            *[ANY] * count,
        ],
        out_specs=[some, whole(0), whole(0), *[WHOLE] * count],
        out_shape=[
            *[jax.ShapeDtypeStruct((rows, heads * HEAD_DIM), LOW)] * 3,
            *[jax.ShapeDtypeStruct((g.shape[0] // RING, g.shape[1]), WIDE) for g in grads],
        ],
        scratch_shapes=[
            *[pltpu.VMEM((rows, LANES), WIDE)] * 2,
            *(ScatterRing.scratch([g.shape for g in grads]) if count else []),
        ],
        compiler_params=pltpu.CompilerParams(vmem_limit_bytes=VMEM_LIMIT, **extra),
        name="attend_back",
    )(bias.T, joint, joint, joint, mixed, grad, lse, *grads)
    return found[:3], found[3:]


def local(size, image, text, cond, w_ada, w_qkv, w_out, w_up, w_down, grad_image, grad_text):
    index = lax.axis_index("tensor")
    seqs = size
    image_rows, width = image.shape[1], image.shape[2]
    text_tokens = text.shape[1]
    text_own = -(-text_tokens // 4)
    text_rows = -(-text_own // TEXT_TILE) * TEXT_TILE
    pool_rows = -(-text_own // POOL_TILE) * POOL_TILE
    width_here = w_ada.shape[-1]
    ada_rows = w_ada.shape[1]
    heads_here = w_qkv.shape[-1] // HEAD_DIM

    def blocks_of(weight):
        return [weight[stream].astype(LOW).reshape(weight.shape[1], -1) for stream in range(2)]

    up_blocks, down_blocks = blocks_of(w_up), blocks_of(w_down)

    units = up_blocks[1].shape[1] // size
    text_up = lax.all_to_all(
        up_blocks[1].reshape(-1, size, units), "dp", split_axis=1, concat_axis=0, tiled=True
    ).reshape(width, units)
    text_down = down_blocks[1]

    def pool_start(rows):
        copies = jnp.broadcast_to(rows[None, :pool_rows], (size, pool_rows, width))
        rows = lax.all_to_all(copies, "dp", split_axis=0, concat_axis=0, tiled=True)
        return rows.reshape(-1, width)

    def unpool_end(here, far):
        return own_pool((here + far.astype(WIDE)).astype(LOW))

    def own_pool(part):
        part = part.reshape(size, pool_rows, width)
        part = lax.all_to_all(part, "dp", split_axis=0, concat_axis=0, tiled=True)
        total = jnp.sum(part.astype(WIDE), axis=0)
        return jnp.pad(total, ((0, text_rows - pool_rows), (0, 0)))


    cond_low = jax.nn.silu(cond).astype(LOW)
    cond_rows = cond_low.reshape(seqs, ada_rows)
    ada_low = w_ada.astype(LOW)

    def own_text(rows):
        padded = jnp.pad(rows, ((0, 4 * text_own - text_tokens), (0, 0)))
        own = lax.dynamic_slice_in_dim(padded, index * text_own, text_own, 0)
        return jnp.pad(own, ((0, text_rows - text_own), (0, 0)))

    cot_rows = [grad_image[0], own_text(grad_text[0])]
    x_rows = [image[0], own_text(text[0])]
    if size == RING:
        ada_rows_low = ada_low.transpose(0, 2, 1, 3).reshape(12, ada_rows, width_here)
        attn_rows, ffn_rows, qkv_full, pooled_grad, modulation, cond_rows = first_ring(
            x_rows, cot_rows, cond_rows, ada_rows_low, blocks_of(w_qkv), pool_rows, 1
        )
        modulation, cond_rows = modulation.reshape(2, 6, width), cond_rows.astype(LOW)
    else:
        cond_rows = lax.all_to_all(cond_rows, "dp", split_axis=0, concat_axis=0, tiled=True)
        mod_parts = jnp.einsum("nd,sdkf->nskf", cond_rows, ada_low, preferred_element_type=WIDE)
        mod_parts = lax.all_to_all(mod_parts, "dp", split_axis=0, concat_axis=0, tiled=True)
        modulation = lax.all_gather(jnp.sum(mod_parts, axis=0), "tensor", axis=2, tiled=True)

    def mod_row(stream, which):
        return modulation[stream, which][None, :]

    split_at = 4 * image_rows
    places = jnp.arange(4 * text_rows)
    token = ((places // text_rows) ^ index) * text_own + places % text_rows
    is_key = (places % text_rows < text_own) & (token < text_tokens)
    bias = jnp.where(is_key, 0.0, -1e30).astype(WIDE)[None, :]

    streams = [rows.astype(WIDE) for rows in x_rows]
    cotangent = [rows.astype(WIDE) for rows in cot_rows]
    normed_in = [layer_norm(residual) for residual in streams]
    first_in = [
        (normed_in[s] * (1.0 + mod_row(s, 1)) + mod_row(s, 0)).astype(LOW) for s in range(2)
    ]
    ffn_grad = [(mod_row(s, 5) * cotangent[s]).astype(LOW) for s in range(2)]
    if size != RING:
        attn_rows = [gather_rows(rows) for rows in first_in]
        ffn_rows, pooled_grad = gather_rows(ffn_grad[0]), pool_start(ffn_grad[1])
        qkv_full = gather_dp(blocks_of(w_qkv), size, 1)
    joint = jnp.concatenate(
        [dot(attn_rows[s], qkv_full[s], NN).astype(LOW) for s in range(2)], axis=0
    )
    text_ffn_moved = gather_start(pooled_grad)
    ffn_blocks = [up_blocks[0], down_blocks[0]]
    if size == RING:
        mods = jnp.concatenate(
            [row for s in range(2) for row in (mod_row(s, 2), 1.0 + mod_row(s, 4), mod_row(s, 3))]
            + [jnp.zeros((2, width), WIDE)],
            axis=0,
        )
        found = middle_ring(
            joint, bias, x_rows, mods, split_at, heads_here, blocks_of(w_out), ffn_blocks,
            pool_rows, 2,
        )
        mixed, log_total, *found = found
        branches, middle, mlp_rows, pooled_in = found[:2], found[2:4], found[5], found[6]
        out_full, up_full, down_full = found[7:9], found[9], found[10]
    else:
        mixed, log_total, _ = attend(joint, bias, split_at, heads_here, [], 0, ())
        *out_full, up_full, down_full = gather_dp(blocks_of(w_out) + ffn_blocks, size, 2)
        branches = [
            scatter_rows(dot(mixed[:split_at], out_full[0], NN)),
            scatter_rows(dot(mixed[split_at:], out_full[1], NN)),
        ]
        middle = [streams[s] + mod_row(s, 2) * branches[s] for s in range(2)]
        second_in = [
            (layer_norm(middle[s]) * (1.0 + mod_row(s, 4)) + mod_row(s, 3)).astype(LOW)
            for s in range(2)
        ]
        mlp_rows, pooled_in = gather_rows(second_in[0]), pool_start(second_in[1])
    mixed, *text_ffn_moved = lax.optimization_barrier((mixed, *text_ffn_moved))
    text_ffn_rows = gather_end(pooled_grad, *text_ffn_moved)
    mixed_rows = [mixed[:split_at], mixed[split_at:]]
    normed_mid = [layer_norm(residual) for residual in middle]

    def gelu_back(pre_act, hidden_grad):
        return jax.vjp(gelu_tanh, pre_act)[1](hidden_grad)[0].astype(LOW)

    text_moved = gather_start(pooled_in)
    pre_act = dot(mlp_rows, up_full, NN)
    hidden = gelu_tanh(pre_act).astype(LOW)
    pre_grad = gelu_back(pre_act, dot(ffn_rows, down_full, NT))
    pre_grad, *text_moved = lax.optimization_barrier((pre_grad, *text_moved))
    text_mlp_rows = gather_end(pooled_in, *text_moved)
    text_pre_act = dot(text_mlp_rows, text_up, NN)
    text_hidden = gelu_tanh(text_pre_act).astype(LOW)
    text_pre_grad = gelu_back(text_pre_act, dot(text_ffn_rows, text_down, NT))
    text_here, text_there = scatter_start(dot(text_pre_grad, text_up, NT))
    text_far = lax.ppermute(text_there, "tensor", CHIP)
    pre_grad, text_there = lax.optimization_barrier((pre_grad, text_there))
    second_part = dot(pre_grad, up_full, NT).astype(LOW)
    down_grad = dot(hidden, ffn_rows, TN).astype(LOW)
    up_grad = dot(mlp_rows, pre_grad, TN).astype(LOW)
    here, there = scatter_start(dot(hidden, down_full, NN))
    up_grad, down_grad, second_part, there, text_far = lax.optimization_barrier(
        (up_grad, down_grad, second_part, there, text_far)
    )
    second_grad, ffn = [None, None], [None, None]
    text_second = (text_here + text_far.astype(WIDE)).astype(LOW)
    text_here, text_there = scatter_start(dot(text_hidden, text_down, NN))
    text_down_grad = dot(text_hidden, text_ffn_rows, TN)
    text_up_grad = dot(text_mlp_rows, text_pre_grad, TN)
    if size == RING:
        mods = jnp.concatenate(
            [row for s in range(2) for row in (mod_row(s, 2), 1.0 + mod_row(s, 4))]
            + [jnp.zeros((4, width), WIDE)],
            axis=0,
        )
        found = back_ring(
            joint, bias, mixed, log_total, split_at, heads_here, text_second, middle,
            cot_rows, mods, second_part, out_full,
            [down_grad, up_grad], [there, text_there], 5,
        )
        *grads, image_second, image_middle, text_middle = found[:6]
        middle_grad, branch_rows = [image_middle, text_middle], found[6:8]
        far, text_far, down_sum, up_sum, text_sum = found[8:]
        second_grad = [image_second, text_sum]
    else:
        second_grad = [scatter_rows(second_part), own_pool(text_second)]
        middle_grad, branch_rows = [None, None], [None, None]
        for s in range(2):
            wide = second_grad[s] * (1.0 + mod_row(s, 4))
            middle_grad[s] = cotangent[s] + jax.vjp(layer_norm, middle[s])[1](wide)[0]
            branch_rows[s] = gather_rows((mod_row(s, 2) * middle_grad[s]).astype(LOW))
        mixed_grad = jnp.concatenate(
            [dot(branch_rows[s], out_full[s], NT).astype(LOW) for s in range(2)], axis=0
        )
        grads = attend_back(
            joint, bias, mixed, mixed_grad, log_total, split_at, heads_here, [], 0, ()
        )[0]
        grads = list(grads)
        down_sum, up_sum = scatter_dp([down_grad, up_grad], size, 5)
        far = lax.ppermute(there, "tensor", CHIP)
        text_far = lax.ppermute(text_there, "tensor", CHIP)
    ffn[0], ffn[1] = here + far.astype(WIDE), unpool_end(text_here, text_far)
    results = [(middle[s] + mod_row(s, 5) * ffn[s]).astype(LOW) for s in range(2)]
    gate_terms = [jnp.sum(cotangent[s] * ffn[s], axis=0)[None] for s in range(2)]
    out_grad = [dot(mixed_rows[s], branch_rows[s], TN).astype(LOW) for s in range(2)]
    text_up_grad, grads[0] = lax.optimization_barrier((text_up_grad, grads[0]))
    text_up_grad = lax.all_to_all(
        text_up_grad.astype(LOW).reshape(size, -1, units),
        "dp", split_axis=0, concat_axis=2, tiled=True,
    )
    joint_grad = jnp.concatenate(grads, axis=1)
    joint_rows = [joint_grad[:split_at], joint_grad[split_at:]]
    qkv_grad = [dot(attn_rows[s], joint_rows[s], TN).astype(LOW) for s in range(2)]
    first_parts = [dot(joint_rows[s], qkv_full[s], NT).astype(LOW) for s in range(2)]
    here, there = scatter_start(
        jnp.concatenate(
            [
                part[b * (part.shape[0] // 4) : (b + 1) * (part.shape[0] // 4)]
                for b in range(4)
                for part in first_parts
            ]
        )
    )
    other = []
    for s in range(2):
        other += [
            jnp.zeros((2, width), WIDE),
            jnp.sum(middle_grad[s] * branches[s], axis=0)[None],
            jnp.sum(second_grad[s], axis=0)[None],
            jnp.sum(second_grad[s] * normed_mid[s], axis=0)[None],
            gate_terms[s],
        ]
    other = jnp.concatenate(other + [jnp.zeros((4, width), WIDE)], axis=0)
    if size == RING:
        scale = jnp.concatenate([1.0 + mod_row(s, 1) for s in range(2)], axis=0)
        image_input, mod_sum, mod_grad, text_out, text_grad, *found = tail_ring(
            here, there, scale, other, x_rows, middle_grad, results[1], qkv_grad + out_grad,
            width_here, 6,
        )
        qkv_image, qkv_text, out_image, out_text = found
        qkv_sums, out_sum = [qkv_image, qkv_text], [out_image, out_text]
        mod_sum = mod_sum[:12].reshape(2, 6, width_here)
        mod_grad = mod_grad[:, :12].reshape(seqs, 2, 6, width_here)
        mod_grad, text_up_grad = lax.optimization_barrier((mod_grad, text_up_grad))
    else:
        *qkv_sums, out_image, out_text = scatter_dp(qkv_grad + out_grad, size, 6)
        out_sum = [out_image, out_text]
        far = lax.ppermute(there, "tensor", CHIP)
        first_rows = here + far.astype(WIDE)
        first_grad = [first_rows[:image_rows], first_rows[image_rows:]]
        input_grad, first_terms = [None, None], []
        for s in range(2):
            wide = first_grad[s] * (1.0 + mod_row(s, 1))
            input_grad[s] = middle_grad[s] + jax.vjp(layer_norm, streams[s])[1](wide)[0]
            shift = jnp.sum(first_grad[s], axis=0)
            gain = jnp.sum(first_grad[s] * normed_in[s], axis=0)
            first_terms.append(jnp.stack([shift, gain]))
        image_input = input_grad[0]
        text_out = lax.all_gather(results[1], "tensor", axis=0)
        text_grad = lax.all_gather(input_grad[1], "tensor", axis=0)
        mod_terms = other[:12].reshape(2, 6, width).at[:, :2].set(jnp.stack(first_terms))
        mod_split = mod_terms.reshape(2, 6, 4, width_here).transpose(2, 0, 1, 3)
        mod_sum = jnp.sum(
            lax.all_to_all(mod_split, "tensor", split_axis=0, concat_axis=0, tiled=True), axis=0
        )
        mod_low = jnp.broadcast_to(mod_sum.astype(LOW)[None], (seqs,) + mod_sum.shape)
        mod_grad = lax.all_to_all(mod_low, "dp", split_axis=0, concat_axis=0, tiled=True)
    shift_grad = mod_sum[:, 3]
    text_up_grad = text_up_grad.reshape(-1, size * units).astype(WIDE)
    ada_grad = jnp.einsum("nd,nskf->sdkf", cond_rows, mod_grad, preferred_element_type=WIDE)
    act_parts = jnp.einsum("nskf,sdkf->nd", mod_grad, ada_low, preferred_element_type=WIDE)
    act_parts = lax.all_to_all(act_parts, "dp", split_axis=0, concat_axis=0, tiled=True)
    act_grad = lax.psum(act_parts.reshape(1, width), "tensor")
    cond_grad = jax.vjp(jax.nn.silu, cond)[1](act_grad)[0]

    def whole_text(blocks):
        return blocks[:, :text_own].reshape(4 * text_own, width)[:text_tokens][None]

    down_sum = jnp.stack([down_sum, text_down_grad])
    up_sum = jnp.stack([up_sum, text_up_grad])
    qkv_sum, out_sum = jnp.stack(qkv_sums), jnp.stack(out_sum)

    return (
        results[0][None],
        whole_text(text_out),
        image_input[None],
        whole_text(text_grad),
        cond_grad,
        shift_grad[None],
        ada_grad,
        qkv_sum.reshape(w_qkv.shape),
        out_sum.reshape(w_out.shape),
        up_sum,
        down_sum,
    )


def solution(mesh):
    size = mesh.shape["dp"]

    def step(*args):
        return local(size, *args)

    return jax.shard_map(
        step,
        mesh=mesh,
        in_specs=(
            P("dp", "tensor", None),
            P("dp", None, None),
            P("dp", None),
            P(None, "dp", None, "tensor"),
            P(None, "dp", None, "tensor"),
            P(None, ("tensor", "dp"), None),
            P(None, "dp", "tensor"),
            P(None, ("tensor", "dp"), None),
            P("dp", "tensor", None),
            P("dp", None, None),
        ),
        out_specs=(
            P("dp", "tensor", None),
            P("dp", None, None),
            P("dp", "tensor", None),
            P("dp", None, None),
            P("dp", None),
            P("dp", None, "tensor"),
            P(None, "dp", None, "tensor"),
            P(None, "dp", None, "tensor"),
            P(None, ("tensor", "dp"), None),
            P(None, "dp", "tensor"),
            P(None, ("tensor", "dp"), None),
        ),
        check_vma=False,
    )
```

```python
import functools

import jax
import jax.numpy as jnp
from jax import lax
from jax.experimental import pallas as pl
from jax.experimental.pallas import tpu as pltpu
from jax.sharding import PartitionSpec as P

HEAD_DIM = 64
EPS = 1e-06
LOW = jnp.bfloat16
WIDE = jnp.float32
TEXT_TILE = 64
POOL_TILE = 16
LANES = 128
NT, NN, TN = ((1,), (1,)), ((1,), (0,)), ((0,), (0,))


def dot(left, right, dims):
    return lax.dot_general(left, right, (dims, ((), ())), preferred_element_type=WIDE)


def layer_norm(values):
    average = jnp.mean(values, axis=-1, keepdims=True)
    centred = values - average
    spread = jnp.mean(centred * centred, axis=-1, keepdims=True)
    return centred * lax.rsqrt(spread + EPS)


def gelu_tanh(values):
    return jax.nn.gelu(values, approximate=True)


MESH = pl.DeviceIdType.MESH
RING = 8


def ring_dp(place):
    place = place % RING
    return 2 * place + (place // (RING // 2)) * (2 * RING - 1 - 4 * place)


def ring_place():
    index = lax.axis_index("dp")
    return index // 2 + (index % 2) * (RING - 1 - 2 * (index // 2))


def ring_sides(place):
    tensor = lax.axis_index("tensor")
    return (ring_dp(place + 1), tensor), (ring_dp(place + RING - 1), tensor)


def meet(sides):
    barrier = pltpu.get_barrier_semaphore()
    for side in sides:
        pl.semaphore_signal(barrier, inc=1, device_id=side, device_id_type=MESH)
    pl.semaphore_wait(barrier, len(sides))


def half_of(rows, columns, way):
    if rows // 2 % 16 == 0:
        return way * (rows // 2), rows // 2, 0, columns
    return 0, rows, way * (columns // 2), columns // 2


class GatherRing:
    STEPS = RING // 2

    def __init__(self, blocks, fulls, sems):
        self.blocks, self.fulls = blocks, fulls
        self.own_sem, self.send_sem, self.recv_sem = sems
        self.place = ring_place()
        self.sides = ring_sides(self.place)

    @staticmethod
    def scratch(count):
        steps = RING // 2
        return [
            pltpu.SemaphoreType.DMA((count,)),
            pltpu.SemaphoreType.DMA((count, 2, steps)),
            pltpu.SemaphoreType.DMA((count, 2, steps)),
        ]

    def copy(self, i, way, step):
        rows, columns = self.blocks[i].shape
        at = self.place + (RING - step if way == 0 else step)
        top, high, left, wide = 0, rows, 0, columns
        if step == self.STEPS - 1:
            top, high, left, wide = half_of(rows, columns, way)
        there = self.fulls[i].at[pl.ds(ring_dp(at) * rows + top, high), pl.ds(left, wide)]
        here = there if step else self.blocks[i]
        return pltpu.make_async_remote_copy(
            src_ref=here,
            dst_ref=there,
            send_sem=self.send_sem.at[i, way, step],
            recv_sem=self.recv_sem.at[i, way, step],
            device_id=self.sides[way],
            device_id_type=MESH,
        )

    def own(self, i):
        rows = self.blocks[i].shape[0]
        start = ring_dp(self.place) * rows
        return pltpu.make_async_copy(
            self.blocks[i], self.fulls[i].at[pl.ds(start, rows)], self.own_sem.at[i]
        )

    def start(self):
        for i in range(len(self.blocks)):
            for way in range(2):
                self.copy(i, way, 0).start()
            self.own(i).start()

    def step(self, step):
        for i in range(len(self.blocks)):
            for way in range(2):
                self.copy(i, way, step - 1).wait_recv()
                if step < self.STEPS:
                    self.copy(i, way, step).start()

    def end(self):
        for i in range(len(self.blocks)):
            self.own(i).wait()
            for way in range(2):
                for step in range(self.STEPS):
                    self.copy(i, way, step).wait_send()


class ScatterRing:
    STEPS = RING - 1

    def __init__(self, grads, sums, scratch):
        self.grads, self.sums = grads, sums
        count = len(grads)
        self.mine, self.got = scratch[:count], scratch[count : 2 * count]
        self.mine_sem, self.send_sem, self.recv_sem = scratch[2 * count :]
        self.place = ring_place()
        self.sides = ring_sides(self.place)

    @staticmethod
    def scratch(shapes):
        sizes = [half_of(rows // RING, columns, 0) for rows, columns in shapes]
        halves = [(2, RING, high, wide) for _, high, _, wide in sizes]
        gots = [(2, RING - 1, high, wide) for _, high, _, wide in sizes]
        count = len(shapes)
        return [
            *[pltpu.VMEM(shape, LOW) for shape in halves],
            *[pltpu.VMEM(shape, LOW) for shape in gots],
            pltpu.SemaphoreType.DMA((count, 2, RING)),
            pltpu.SemaphoreType.DMA((count, 2, RING - 1)),
            pltpu.SemaphoreType.DMA((count, 2, RING - 1)),
        ]

    def load(self, i, way, step):
        rows, columns = self.grads[i].shape[0] // RING, self.grads[i].shape[1]
        at = self.place + (2 * RING - step - 1 if way == 0 else step + 1)
        top, high, left, wide = half_of(rows, columns, way)
        return pltpu.make_async_copy(
            self.grads[i].at[pl.ds(ring_dp(at) * rows + top, high), pl.ds(left, wide)],
            self.mine[i].at[way, step],
            self.mine_sem.at[i, way, step],
        )

    def copy(self, i, way, step):
        return pltpu.make_async_remote_copy(
            src_ref=self.mine[i].at[way, step],
            dst_ref=self.got[i].at[way, step],
            send_sem=self.send_sem.at[i, way, step],
            recv_sem=self.recv_sem.at[i, way, step],
            device_id=self.sides[way],
            device_id_type=MESH,
        )

    def load_all(self):
        for step in range(RING):
            for i in range(len(self.grads)):
                for way in range(2):
                    self.load(i, way, step).start()

    def start(self):
        for i in range(len(self.grads)):
            for way in range(2):
                self.load(i, way, 0).wait()
                self.copy(i, way, 0).start()

    def step(self, step):
        for i in range(len(self.grads)):
            rows, columns = self.grads[i].shape[0] // RING, self.grads[i].shape[1]
            for way in range(2):
                top, high, left, wide = half_of(rows, columns, way)
                self.load(i, way, step).wait()
                self.copy(i, way, step - 1).wait_recv()
                total = self.mine[i][way, step].astype(WIDE) + self.got[i][way, step - 1].astype(WIDE)
                if step < self.STEPS:
                    self.mine[i][way, step] = total.astype(LOW)
                    self.copy(i, way, step).start()
                else:
                    self.sums[i][pl.ds(top, high), pl.ds(left, wide)] = total

    def end(self):
        for i in range(len(self.grads)):
            for way in range(2):
                for step in range(self.STEPS):
                    self.copy(i, way, step).wait_send()


ANY = pl.BlockSpec(memory_space=pl.ANY)
WHOLE = pl.BlockSpec(memory_space=pltpu.VMEM)
VMEM_LIMIT = 56 << 20


def gather_kernel(count, *refs):
    ring = GatherRing(refs[:count], refs[count : 2 * count], refs[2 * count :])
    meet(ring.sides)
    ring.start()
    for step in range(1, ring.STEPS + 1):
        ring.step(step)
    ring.end()


def gather_ring(blocks, ident):
    count = len(blocks)
    return pl.pallas_call(
        functools.partial(gather_kernel, count),
        out_shape=[
            jax.ShapeDtypeStruct((RING * block.shape[0], block.shape[1]), block.dtype)
            for block in blocks
        ],
        in_specs=[ANY] * count,
        out_specs=[ANY] * count,
        scratch_shapes=GatherRing.scratch(count),
        compiler_params=pltpu.CompilerParams(
            collective_id=ident, has_side_effects=True, vmem_limit_bytes=VMEM_LIMIT
        ),
        name="gather_ring",
    )(*blocks)


def scatter_kernel(count, *refs):
    ring = ScatterRing(refs[:count], refs[count : 2 * count], refs[2 * count :])
    ring.load_all()
    meet(ring.sides)
    ring.start()
    for step in range(1, ring.STEPS + 1):
        ring.step(step)
    ring.end()


def scatter_ring(grads, ident):
    count = len(grads)
    return pl.pallas_call(
        functools.partial(scatter_kernel, count),
        out_shape=[
            jax.ShapeDtypeStruct((grad.shape[0] // RING, grad.shape[1]), WIDE) for grad in grads
        ],
        in_specs=[ANY] * count,
        out_specs=[WHOLE] * count,
        scratch_shapes=ScatterRing.scratch([grad.shape for grad in grads]),
        compiler_params=pltpu.CompilerParams(
            collective_id=ident, has_side_effects=True, vmem_limit_bytes=VMEM_LIMIT
        ),
        name="scatter_ring",
    )(*grads)


def gather_dp(blocks, size, ident):
    if size == RING:
        return gather_ring(blocks, ident)
    return [lax.all_gather(block, "dp", axis=0, tiled=True) for block in blocks]


def scatter_dp(grads, size, ident):
    if size == RING:
        return scatter_ring(grads, ident)
    return [
        lax.psum_scatter(grad, "dp", scatter_dimension=0, tiled=True).astype(WIDE)
        for grad in grads
    ]


def beside(ring, blocks, size, ident, before, after):
    blocks = lax.optimization_barrier(tuple(blocks) + tuple(before))[: len(blocks)]
    found = tuple(ring(list(blocks), size, ident))
    held = lax.optimization_barrier(found + tuple(after))
    return held[: len(found)], held[len(found) :]


CORE = [(i, i ^ 1) for i in range(4)]
CHIP = [(i, i ^ 2) for i in range(4)]


def gather_start(own):
    near = lax.ppermute(own, "tensor", CORE)
    far = lax.ppermute(own, "tensor", CHIP)
    return near, far


def gather_end(own, near, far):
    last = lax.ppermute(far, "tensor", CORE)
    return jnp.concatenate([own, near, far, last], axis=0)


def gather_rows(own):
    return gather_end(own, *gather_start(own))


def scatter_start(partial):
    rows = partial.shape[0] // 4
    low = partial.astype(LOW)
    part = [low[b * rows : (b + 1) * rows] for b in range(4)]
    sent = lax.ppermute(jnp.concatenate([part[1], part[3]]), "tensor", CORE)
    here = part[0].astype(WIDE) + sent[:rows].astype(WIDE)
    return here, (part[2].astype(WIDE) + sent[rows:].astype(WIDE)).astype(LOW)


def scatter_rows(partial):
    here, there = scatter_start(partial)
    return here + lax.ppermute(there, "tensor", CHIP).astype(WIDE)


def tensor_peer(hop):
    index = lax.axis_index("tensor")
    if hop == 1:
        return index + 1 - 2 * (index % 2)
    return (index + 2) % 4 if hop == 2 else 3 - index


def tail_kernel(columns, count, *refs):
    d_parts, scale, other, x_image, x_text, mid_image, mid_text, text_out, ada = refs[:3], *refs[3:11]
    qkv_weights, grads, refs = refs[11:13], refs[13 : 13 + count], refs[13 + count :]
    image_grad, mod_sum, mod_all, cond_sum, *wholes = refs[:6]
    sums, refs = refs[6 : 6 + count], refs[6 + count :]
    far, text_grad, terms, parts, low, slots, far_sem, part_sem, slot_sem, text_sem = refs[:10]
    weights, sent, got, far_sent, here, acts, act_got, act_rows, weight_sem, act_sem, act_row_sem = refs[10:21]
    ring = ScatterRing(grads, sums, refs[21:])
    me, index = lax.axis_index("dp"), lax.axis_index("tensor")
    far_copy = pltpu.make_async_remote_copy(
        src_ref=far_sent, dst_ref=far, send_sem=far_sem.at[0, 1], recv_sem=far_sem.at[1, 1],
        device_id=(me, tensor_peer(2)), device_id_type=MESH,
    )
    weight_copies = [
        pltpu.make_async_copy(qkv_weights[s], weights.at[s], weight_sem.at[s]) for s in range(2)
    ]

    def first_part(b):
        found = []
        for s, rows in ((0, x_image.shape[0]), (1, x_text.shape[0])):
            low_row = b * rows + (0 if s == 0 else 4 * x_image.shape[0])
            total = None
            for p in range(3):
                wide = d_parts[p].shape[1]
                weight = weights[s, :, p * wide : (p + 1) * wide]
                part = dot(d_parts[p][low_row : low_row + rows], weight, NT)
                total = part if total is None else total + part
            found.append(total)
        return jnp.concatenate(found, axis=0)

    def act_copy(hop):
        return pltpu.make_async_remote_copy(
            src_ref=acts, dst_ref=act_got.at[hop - 1],
            send_sem=act_sem.at[0, hop - 1], recv_sem=act_sem.at[1, hop - 1],
            device_id=(me, tensor_peer(hop)), device_id_type=MESH,
        )

    def act_row_copy(hop):
        peer = (me + hop) % RING
        return pltpu.make_async_remote_copy(
            src_ref=act_rows.at[peer], dst_ref=cond_sum.at[me],
            send_sem=act_row_sem.at[0, hop - 1], recv_sem=act_row_sem.at[1, hop - 1],
            device_id=(peer, index), device_id_type=MESH,
        )

    def part_copy(hop):
        peer = tensor_peer(hop)
        start = pl.multiple_of(peer * columns, LANES)
        return pltpu.make_async_remote_copy(
            src_ref=terms.at[:, pl.ds(start, columns)], dst_ref=parts.at[hop - 1],
            send_sem=part_sem.at[0, hop - 1], recv_sem=part_sem.at[1, hop - 1],
            device_id=(me, peer), device_id_type=MESH,
        )

    def slot_copy(hop):
        return pltpu.make_async_remote_copy(
            src_ref=low, dst_ref=slots.at[me],
            send_sem=slot_sem.at[0, hop - 1], recv_sem=slot_sem.at[1, hop - 1],
            device_id=((me + hop) % RING, index), device_id_type=MESH,
        )

    def text_copy(i, hop):
        source = (text_out, text_grad)[i]
        return pltpu.make_async_remote_copy(
            src_ref=source, dst_ref=wholes[i].at[index],
            send_sem=text_sem.at[i, 0, hop], recv_sem=text_sem.at[i, 1, hop],
            device_id=(me, tensor_peer(hop)), device_id_type=MESH,
        )

    def text_own(i):
        source = (text_out, text_grad)[i]
        return pltpu.make_async_copy(source, wholes[i].at[index], text_sem.at[i, 0, 0])

    def rows_back(first, x, middle, gain):
        x = x.astype(WIDE)
        centred = x - jnp.mean(x, axis=-1, keepdims=True)
        spread = lax.rsqrt(jnp.mean(centred * centred, axis=-1, keepdims=True) + EPS)
        normed = centred * spread
        wide = first * gain
        inner = jnp.mean(wide, axis=-1, keepdims=True)
        cross = jnp.mean(wide * normed, axis=-1, keepdims=True)
        sums = jnp.sum(first, axis=0, keepdims=True), jnp.sum(first * normed, axis=0, keepdims=True)
        return middle + (wide - inner - normed * cross) * spread, *sums

    for copy in weight_copies:
        copy.start()
    ring.load_all()
    meet(
        [(me, tensor_peer(hop)) for hop in (1, 2, 3)]
        + [((me + hop) % RING, index) for hop in range(1, RING)]
    )
    ring.start()
    for copy in weight_copies:
        copy.wait()
    near = exchange_sums(first_part, sent, got, far_sem, me)
    ring.step(1)
    here[...] = first_part(0)
    far_sent[...] = first_part(2).astype(LOW)
    near.wait()
    far_sent[...] = (far_sent[...].astype(WIDE) + got[1].astype(WIDE)).astype(LOW)
    far_copy.start()
    here[...] += got[0].astype(WIDE)
    ring.step(2)
    far_copy.wait()
    terms[...] = other[...]
    chunk = 64

    def image_chunk(at, totals):
        rows = pl.ds(pl.multiple_of(at * chunk, chunk), chunk)
        first = here[rows] + far[rows].astype(WIDE)
        out, shift, gain = rows_back(first, x_image[rows], mid_image[rows], scale[0:1])
        image_grad[rows] = out
        return totals[0] + shift, totals[1] + gain

    zero = jnp.zeros((1, here.shape[1]), WIDE)
    image_rows = x_image.shape[0]
    shift, gain = lax.fori_loop(0, image_rows // chunk, image_chunk, (zero, zero))
    terms[0:1] = shift
    terms[1:2] = gain
    ring.step(3)
    text_first = here[image_rows:] + far[image_rows:].astype(WIDE)
    out, shift, gain = rows_back(text_first, x_text[...], mid_text[...], scale[1:2])
    text_grad[...] = out
    for i in range(2):
        text_own(i).start()
        for hop in (1, 2, 3):
            text_copy(i, hop).start()
    terms[6:7] = shift
    terms[7:8] = gain
    for hop in (1, 2, 3):
        part_copy(hop).start()
    ring.step(4)
    for hop in (1, 2, 3):
        part_copy(hop).wait()
    own = terms[:, pl.ds(pl.multiple_of(index * columns, LANES), columns)]
    total = own + parts[0] + parts[1] + parts[2]
    mod_sum[...] = total
    low[...] = total.astype(LOW)
    slots[pl.ds(me, 1)] = total.astype(LOW)[None]
    for hop in range(1, RING):
        slot_copy(hop).start()
    ring.step(5)
    for hop in range(1, RING):
        slot_copy(hop).wait()
    mod_all[...] = slots[...]
    wide = slots[...].astype(WIDE)
    total = None
    for which in range(12):
        rows = jnp.concatenate([wide[n, which : which + 1] for n in range(RING)], axis=0)
        part = dot(rows.astype(LOW), ada[which], NT)
        total = part if total is None else total + part
    acts[...] = total
    for hop in (1, 2, 3):
        act_copy(hop).start()
    for i in range(2):
        text_own(i).wait()
        for hop in (1, 2, 3):
            text_copy(i, hop).wait()
    ring.step(6)
    for hop in (1, 2, 3):
        act_copy(hop).wait()
    total = acts[...] + act_got[0] + act_got[1] + act_got[2]
    for n in range(RING):
        act_rows[n] = jnp.broadcast_to(total[n : n + 1], act_rows.shape[1:])
    for hop in range(1, RING):
        act_row_copy(hop).start()
    cond_sum[pl.ds(me, 1)] = act_rows[pl.ds(me, 1)]
    ring.step(7)
    for hop in range(1, RING):
        act_row_copy(hop).wait()
    ring.end()


def tail_ring(d_parts, weights, scale, other, x, middle, text_out, ada, grads, ident):
    width, shapes = scale.shape[1], [grad.shape for grad in grads]
    rows, text_rows = x[0].shape[0], x[1].shape[0]
    both, (_, depth, columns) = rows + text_rows, ada.shape
    return pl.pallas_call(
        functools.partial(tail_kernel, columns, len(grads)),
        out_shape=[
            jax.ShapeDtypeStruct((rows, width), WIDE),
            jax.ShapeDtypeStruct((16, columns), WIDE),
            jax.ShapeDtypeStruct((RING, 16, columns), LOW),
            jax.ShapeDtypeStruct((RING, 8, depth), WIDE),
            jax.ShapeDtypeStruct((4, text_rows, width), LOW),
            jax.ShapeDtypeStruct((4, text_rows, width), WIDE),
            *[jax.ShapeDtypeStruct((r // RING, c), WIDE) for r, c in shapes],
        ],
        in_specs=[WHOLE] * 11 + [ANY] * (2 + len(grads)),
        out_specs=[WHOLE] * 4 + [ANY] * 2 + [WHOLE] * len(grads),
        scratch_shapes=[
            pltpu.VMEM((both, width), LOW),
            pltpu.VMEM((text_rows, width), WIDE),
            pltpu.VMEM((16, width), WIDE),
            pltpu.VMEM((3, 16, columns), WIDE),
            pltpu.VMEM((16, columns), LOW),
            pltpu.VMEM((RING, 16, columns), LOW),
            pltpu.SemaphoreType.DMA((2, 2)),
            pltpu.SemaphoreType.DMA((2, 3)),
            pltpu.SemaphoreType.DMA((2, RING - 1)),
            pltpu.SemaphoreType.DMA((2, 2, 4)),
            pltpu.VMEM((2, *weights[0].shape), LOW),
            *[pltpu.VMEM((2, both, width), LOW)] * 2,
            pltpu.VMEM((both, width), LOW),
            pltpu.VMEM((both, width), WIDE),
            pltpu.VMEM((RING, depth), WIDE),
            pltpu.VMEM((3, RING, depth), WIDE),
            pltpu.VMEM((RING, 8, depth), WIDE),
            pltpu.SemaphoreType.DMA((2,)),
            pltpu.SemaphoreType.DMA((2, 3)),
            pltpu.SemaphoreType.DMA((2, RING - 1)),
            *ScatterRing.scratch(shapes),
        ],
        compiler_params=pltpu.CompilerParams(
            collective_id=ident, has_side_effects=True, vmem_limit_bytes=VMEM_LIMIT
        ),
        name="tail_ring",
    )(*d_parts, scale, other, *x, *middle, text_out, ada, *weights, *grads)


def head_lanes(head):
    lane = lax.broadcasted_iota(jnp.int32, (1, LANES), 1)
    return (lane < HEAD_DIM) if head == 0 else (lane >= HEAD_DIM)


def attend_pair(split, bias_ref, q_ref, k_ref, v_ref, out_ref, lse_ref):
    scale = HEAD_DIM ** (-0.5)
    bias = bias_ref[...]
    outs, totals = [], []
    for head in range(2):
        mine = head_lanes(head)
        queries = jnp.where(mine, q_ref[...] * scale, 0).astype(LOW)
        image = dot(queries, k_ref[:split], NT)
        text = dot(queries, k_ref[split:], NT) + bias
        top = jnp.maximum(
            jnp.max(image, axis=1, keepdims=True), jnp.max(text, axis=1, keepdims=True)
        )
        image = jnp.exp(image - top).astype(LOW)
        text = jnp.exp(text - top).astype(LOW)
        values = jnp.where(mine, v_ref[...], 1).astype(LOW)
        both = dot(image, values[:split], NN) + dot(text, values[split:], NN)
        sums = pltpu.roll(both, HEAD_DIM, 1)
        outs.append(both / sums)
        totals.append(top + jnp.log(sums))
    first = head_lanes(0)
    out_ref[...] = jnp.where(first, outs[0], outs[1]).astype(out_ref.dtype)
    flipped = jnp.where(first, totals[0], totals[1]).T
    lse_ref[0] = jnp.concatenate([flipped[:4], flipped[HEAD_DIM : HEAD_DIM + 4]], axis=0)


def first_kernel(chunk, *refs):
    x_image, x_text, cot_image, cot_text, cond, ada, *blocks = refs[:8]
    outs, fulls, pool, (mods, conds), refs = refs[8:11], refs[11:13], refs[13:14], refs[14:16], refs[16:]
    mines, pooled, (row_sem, own_sem) = refs[:3], refs[3], refs[4:6]
    cond_got, parts, got, cond_sem, part_sem, mod_sem = refs[6:12]
    ring = GatherRing(blocks, fulls, refs[12:15])
    text_ring = GatherRing([pooled], pool, refs[15:18])
    me, index = lax.axis_index("dp"), lax.axis_index("tensor")
    width, columns = mods.shape[1], ada.shape[2]

    def dp_copy(hop, source, target, sem):
        peer = (me + hop) % RING
        return pltpu.make_async_remote_copy(
            src_ref=source.at[peer], dst_ref=target.at[me],
            send_sem=sem.at[0, hop - 1], recv_sem=sem.at[1, hop - 1],
            device_id=(peer, index), device_id_type=MESH,
        )

    def mod_copy(hop):
        here = mods.at[:, pl.ds(pl.multiple_of(index * columns, LANES), columns)]
        return pltpu.make_async_remote_copy(
            src_ref=here, dst_ref=here,
            send_sem=mod_sem.at[0, hop - 1], recv_sem=mod_sem.at[1, hop - 1],
            device_id=(me, tensor_peer(hop)), device_id_type=MESH,
        )

    def row_copy(i, source, slot, hop, sem):
        rows = mines[i].shape[0]
        return pltpu.make_async_remote_copy(
            src_ref=source, dst_ref=outs[i].at[pl.ds(slot * rows, rows)],
            send_sem=row_sem.at[i, 0, sem], recv_sem=row_sem.at[i, 1, sem],
            device_id=(me, tensor_peer(hop)), device_id_type=MESH,
        )

    def own(i):
        rows = mines[i].shape[0]
        return pltpu.make_async_copy(mines[i], outs[i].at[pl.ds(0, rows)], own_sem.at[i])

    def to_far(i):
        return row_copy(i, mines[i], 2, 2, 0)

    def to_near(i):
        return row_copy(i, mines[i], 1, 1, 1)

    def forward(i):
        rows = mines[i].shape[0]
        return row_copy(i, outs[i].at[pl.ds(2 * rows, rows)], 3, 1, 2)

    def send(i):
        to_far(i).start()
        to_near(i).start()
        own(i).start()

    def norm_rows(x, stream):
        x = x.astype(WIDE)
        centred = x - jnp.mean(x, axis=-1, keepdims=True)
        spread = lax.rsqrt(jnp.mean(centred * centred, axis=-1, keepdims=True) + EPS)
        gain, shift = 1.0 + mods[6 * stream + 1 : 6 * stream + 2], mods[6 * stream : 6 * stream + 1]
        return (centred * spread * gain + shift).astype(LOW)

    def over_chunks(body):
        def step(i, _):
            body(pl.ds(pl.multiple_of(i * chunk, chunk), chunk))
            return 0

        lax.fori_loop(0, x_image.shape[0] // chunk, step, 0)

    meet(
        [(me, tensor_peer(hop)) for hop in (1, 2, 3)]
        + [((me + hop) % RING, index) for hop in range(1, RING)]
    )
    for hop in range(1, RING):
        dp_copy(hop, cond, cond_got, cond_sem).start()
    cond_got[pl.ds(me, 1)] = cond[pl.ds(me, 1)]
    parts[...] = jnp.zeros_like(parts)
    for hop in range(1, RING):
        dp_copy(hop, cond, cond_got, cond_sem).wait()
    rows = jnp.concatenate([cond_got[n, 0:1] for n in range(RING)], axis=0)
    conds[...] = rows
    rows = rows.astype(LOW)
    for which in range(12):
        part = dot(rows, ada[which], NN)
        for n in range(RING):
            parts[n, which : which + 1] = part[n : n + 1]
    for hop in range(1, RING):
        dp_copy(hop, parts, got, part_sem).start()
    ring.start()
    got[pl.ds(me, 1)] = parts[pl.ds(me, 1)]
    for hop in range(1, RING):
        dp_copy(hop, parts, got, part_sem).wait()
    mods[:, pl.ds(pl.multiple_of(index * columns, LANES), columns)] = jnp.sum(got[...], axis=0)
    for hop in (1, 2, 3):
        mod_copy(hop).start()
    for hop in (1, 2, 3):
        mod_copy(hop).wait()
    pooled[...] = (mods[11:12] * cot_text[: pooled.shape[0]].astype(WIDE)).astype(LOW)
    text_ring.start()

    def norm_chunk(some):
        mines[0][some] = norm_rows(x_image[some], 0)

    def grad_chunk(some):
        mines[2][some] = (mods[5:6] * cot_image[some].astype(WIDE)).astype(LOW)

    over_chunks(norm_chunk)
    send(0)
    mines[1][...] = norm_rows(x_text[...], 1)
    send(1)
    over_chunks(grad_chunk)
    send(2)
    ring.step(1)
    text_ring.step(1)
    for i in range(2):
        to_far(i).wait()
        forward(i).start()
    ring.step(2)
    text_ring.step(2)
    to_far(2).wait()
    forward(2).start()
    ring.step(3)
    text_ring.step(3)
    for i in range(3):
        own(i).wait()
        to_near(i).wait()
        forward(i).wait()
    text_ring.step(4)
    ring.step(4)
    text_ring.end()
    ring.end()


def first_ring(x, cotangent, cond, ada, blocks, pool_rows, ident):
    width, columns, depth = x[0].shape[1], ada.shape[2], ada.shape[1]
    rows = [x[0].shape[0], x[1].shape[0], x[0].shape[0]]
    fulls = [block.shape for block in blocks] + [(pool_rows, width)]
    cond = jnp.broadcast_to(cond.astype(WIDE)[:, None], (RING, 8, depth))
    found = pl.pallas_call(
        functools.partial(first_kernel, 64),
        in_specs=[WHOLE] * 6 + [ANY] * 2,
        out_specs=[ANY] * 6 + [WHOLE] * 2,
        out_shape=[
            *[jax.ShapeDtypeStruct((4 * n, width), LOW) for n in rows],
            *[jax.ShapeDtypeStruct((RING * n, wide), LOW) for n, wide in fulls],
            jax.ShapeDtypeStruct((16, width), WIDE),
            jax.ShapeDtypeStruct((RING, depth), WIDE),
        ],
        scratch_shapes=[
            *[pltpu.VMEM((n, width), LOW) for n in rows],
            pltpu.VMEM((pool_rows, width), LOW),
            pltpu.SemaphoreType.DMA((3, 2, 3)),
            pltpu.SemaphoreType.DMA((3,)),
            pltpu.VMEM((RING, 8, depth), WIDE),
            *[pltpu.VMEM((RING, 16, columns), WIDE)] * 2,
            *[pltpu.SemaphoreType.DMA((2, RING - 1))] * 2,
            pltpu.SemaphoreType.DMA((2, 3)),
            *GatherRing.scratch(2),
            *GatherRing.scratch(1),
        ],
        compiler_params=pltpu.CompilerParams(
            collective_id=ident, has_side_effects=True, vmem_limit_bytes=VMEM_LIMIT
        ),
        name="first_ring",
    )(*x, *cotangent, cond, ada, *blocks)
    return found[:2], found[2], found[3:5], found[5], found[6][:12], found[7]


def exchange_sums(part, sent, got, sems, me):
    copy = pltpu.make_async_remote_copy(
        src_ref=sent, dst_ref=got, send_sem=sems.at[0, 0], recv_sem=sems.at[1, 0],
        device_id=(me, tensor_peer(1)), device_id_type=MESH,
    )
    sent[0] = part(1).astype(LOW)
    sent[1] = part(3).astype(LOW)
    copy.start()
    return copy


def middle_kernel(split, chunk, *refs):
    bias_ref, q_ref, k_ref, v_ref, x_image, x_text, mods = refs[:7]
    out_blocks, ffn_blocks, refs = refs[7:9], refs[9:11], refs[11:]
    mixed, lse_ref, *wide_outs, text_in, image_in = refs[:8]
    branch_image, branch_text, mid_image, mid_text = wide_outs
    pool, out_fulls, ffn_fulls, refs = refs[8:9], refs[9:11], refs[11:13], refs[13:]
    weights, sent, got, far_sent, far_got, here, mine = refs[:7]
    sems, weight_sem, row_sem, own_sem = refs[7:11]
    first = GatherRing(out_blocks, out_fulls, refs[11:14])
    second = GatherRing(ffn_blocks, ffn_fulls, refs[14:17])
    third = GatherRing([text_in.at[pl.ds(0, pool[0].shape[0] // RING)]], pool, refs[17:20])
    me = lax.axis_index("dp")
    block = q_ref.shape[0]
    pair, at = pl.program_id(0), pl.program_id(0) * 2 + pl.program_id(1)
    rows = x_image.shape[0]

    @pl.when(at == 0)
    def _():
        meet([*first.sides, *[(me, tensor_peer(hop)) for hop in (1, 2)]])
        first.start()

    for step in range(1, 5):

        @pl.when(at == step)
        def _():
            first.step(step)

    weight_copies = [
        pltpu.make_async_copy(out_fulls[s], weights.at[s], weight_sem.at[s]) for s in range(2)
    ]

    @pl.when(at == 4)
    def _():
        first.end()
        second.start()
        for copy in weight_copies:
            copy.start()

    place = (
        pl.ds(pl.multiple_of(pl.program_id(1) * block, block), block),
        pl.ds(pl.multiple_of(pair * LANES, LANES), LANES),
    )
    attend_pair(split, bias_ref, q_ref, k_ref, v_ref, mixed.at[place], lse_ref)

    @pl.when(at == 2 * pl.num_programs(0) - 1)
    def _():
        for copy in weight_copies:
            copy.wait()
        text_rows = x_text.shape[0]

        def part(b):
            image = dot(mixed[b * rows : (b + 1) * rows], weights[0], NN)
            low = split + b * text_rows
            text = dot(mixed[low : low + text_rows], weights[1], NN)
            return jnp.concatenate([image, text], axis=0)

        near = exchange_sums(part, sent, got, sems, me)
        here[...] = part(0)
        far_sent[...] = part(2).astype(LOW)
        near.wait()
        far_sent[...] = (far_sent[...].astype(WIDE) + got[1].astype(WIDE)).astype(LOW)
        far = pltpu.make_async_remote_copy(
            src_ref=far_sent, dst_ref=far_got, send_sem=sems.at[0, 1], recv_sem=sems.at[1, 1],
            device_id=(me, tensor_peer(2)), device_id_type=MESH,
        )
        far.start()
        here[...] += got[0].astype(WIDE)
        second.step(1)
        far.wait()

        def norm_rows(x, branch, stream):
            middle = x.astype(WIDE) + mods[3 * stream : 3 * stream + 1] * branch
            centred = middle - jnp.mean(middle, axis=-1, keepdims=True)
            spread = lax.rsqrt(jnp.mean(centred * centred, axis=-1, keepdims=True) + EPS)
            gain, shift = mods[3 * stream + 1 : 3 * stream + 2], mods[3 * stream + 2 : 3 * stream + 3]
            return middle, (centred * spread * gain + shift).astype(LOW)

        def image_chunk(i, _):
            some = pl.ds(pl.multiple_of(i * chunk, chunk), chunk)
            branch = here[some] + far_got[some].astype(WIDE)
            branch_image[some] = branch
            middle, low = norm_rows(x_image[some], branch, 0)
            mid_image[some] = middle
            mine[some] = low
            return 0

        lax.fori_loop(0, rows // chunk, image_chunk, 0)

        def row_copy(source, slot, hop, sem):
            return pltpu.make_async_remote_copy(
                src_ref=source, dst_ref=image_in.at[pl.ds(slot * rows, rows)],
                send_sem=row_sem.at[0, sem], recv_sem=row_sem.at[1, sem],
                device_id=(me, tensor_peer(hop)), device_id_type=MESH,
            )

        own = pltpu.make_async_copy(mine, image_in.at[pl.ds(0, rows)], own_sem.at[0])
        to_far, to_near = row_copy(mine, 2, 2, 0), row_copy(mine, 1, 1, 1)
        to_far.start()
        to_near.start()
        own.start()
        branch = here[rows:] + far_got[rows:].astype(WIDE)
        branch_text[...] = branch
        middle, low = norm_rows(x_text[...], branch, 1)
        mid_text[...] = middle
        text_in[...] = low
        third.start()
        second.step(2)
        third.step(1)
        to_far.wait()
        last = row_copy(image_in.at[pl.ds(2 * rows, rows)], 3, 1, 2)
        last.start()
        third.step(2)
        second.step(3)
        third.step(3)
        own.wait()
        to_near.wait()
        last.wait()
        third.step(4)
        second.step(4)
        second.end()
        third.end()


def middle_ring(joint, bias, x, mods, split, heads, out_blocks, ffn_blocks, pool_rows, ident):
    rows, pairs, block = joint.shape[0], heads // 2, joint.shape[0] // 2
    whole = lambda part: pl.BlockSpec((rows, LANES), lambda h, i: (0, part * pairs + h))
    image_rows, width = x[0].shape
    text_rows = x[1].shape[0]
    both = image_rows + text_rows
    depth = heads * HEAD_DIM
    found = pl.pallas_call(
        functools.partial(middle_kernel, split, 64),
        grid=(pairs, 2),
        in_specs=[
            pl.BlockSpec((1, rows - split), lambda h, i: (0, 0)),
            pl.BlockSpec((block, LANES), lambda h, i: (i, h)),
            whole(1),
            whole(2),
            *[WHOLE] * 3,
            *[ANY] * 4,
        ],
        out_specs=[
            WHOLE,
            pl.BlockSpec((1, 8, block), lambda h, i: (h, 0, i)),
            *[WHOLE] * 5,
            *[ANY] * 6,
        ],
        out_shape=[
            jax.ShapeDtypeStruct((rows, depth), LOW),
            jax.ShapeDtypeStruct((pairs, 8, rows), WIDE),
            *[jax.ShapeDtypeStruct((n, width), WIDE) for n in (image_rows, text_rows) * 2],
            jax.ShapeDtypeStruct((text_rows, width), LOW),
            jax.ShapeDtypeStruct((4 * image_rows, width), LOW),
            jax.ShapeDtypeStruct((RING * pool_rows, width), LOW),
            *[
                jax.ShapeDtypeStruct((RING * b.shape[0], b.shape[1]), b.dtype)
                for b in (*out_blocks, *ffn_blocks)
            ],
        ],
        scratch_shapes=[
            pltpu.VMEM((2, depth, width), LOW),
            pltpu.VMEM((2, both, width), LOW),
            pltpu.VMEM((2, both, width), LOW),
            pltpu.VMEM((both, width), LOW),
            pltpu.VMEM((both, width), LOW),
            pltpu.VMEM((both, width), WIDE),
            pltpu.VMEM((image_rows, width), LOW),
            pltpu.SemaphoreType.DMA((2, 2)),
            pltpu.SemaphoreType.DMA((2,)),
            pltpu.SemaphoreType.DMA((2, 3)),
            pltpu.SemaphoreType.DMA((1,)),
            *GatherRing.scratch(2),
            *GatherRing.scratch(2),
            *GatherRing.scratch(1),
        ],
        compiler_params=pltpu.CompilerParams(
            collective_id=ident, has_side_effects=True, vmem_limit_bytes=VMEM_LIMIT
        ),
        name="middle_ring",
    )(bias, joint, joint, joint, *x, mods, *out_blocks, *ffn_blocks)
    return found


def back_kernel(split, chunk, *refs):
    bias_ref, q_ref, k_ref, v_ref, o_ref, lse_ref = refs[:6]
    mid_image, mid_text, cot_image, cot_text, mods, text_part = refs[6:12]
    partial, out_weights, grads, theirs = refs[12], refs[13:15], refs[15:17], refs[17:19]
    units, refs = refs[19], refs[20:]
    dq_ref, dk_ref, dv_ref, image_second, image_grad, text_grad = refs[:6]
    image_rows, text_rows, *fars = refs[6:10]
    sums, text_second, units_got, refs = refs[10:12], refs[12], refs[13], refs[14:]
    dk_acc, dv_acc, weights, parts, got, far_sent, far_got, rows_in, mixed_grad = refs[:9]
    part_sem, sems, row_sem, weight_sem, rows_sem, far_sem, text_sum, units_sem = refs[9:17]
    ring = ScatterRing(grads, sums, refs[17:24])
    text_ring = ScatterRing([text_part], [text_sum], refs[24:])
    me, index = lax.axis_index("dp"), lax.axis_index("tensor")
    rows, texts = mid_image.shape[0], mid_text.shape[0]
    block = q_ref.shape[0]
    at = pl.program_id(0) * pl.num_programs(1) + pl.program_id(1)
    last = pl.num_programs(0) * pl.num_programs(1) - 1

    def part_of(b):
        return partial.at[pl.ds(b * rows, rows)]

    def keep(i):
        return pltpu.make_async_copy(part_of(2 * i), parts.at[i], part_sem.at[i])

    def near(i):
        return pltpu.make_async_remote_copy(
            src_ref=part_of(2 * i + 1), dst_ref=got.at[i],
            send_sem=sems.at[0, i], recv_sem=sems.at[1, i],
            device_id=(me, tensor_peer(1)), device_id_type=MESH,
        )

    def row_copy(source, slot, hop, sem, s):
        some = (pl.ds(0, rows), pl.ds(rows, texts))[s]
        return pltpu.make_async_remote_copy(
            src_ref=rows_in.at[source, some], dst_ref=rows_in.at[slot, some],
            send_sem=row_sem.at[0, s, sem], recv_sem=row_sem.at[1, s, sem],
            device_id=(me, tensor_peer(hop)), device_id_type=MESH,
        )

    def to_far(s):
        return row_copy(0, 2, 2, 0, s)

    def to_near(s):
        return row_copy(0, 1, 1, 1, s)

    def forward(s):
        return row_copy(2, 3, 1, 2, s)

    def units_copy(hop):
        peer = (me + hop) % RING
        return pltpu.make_async_remote_copy(
            src_ref=units.at[peer], dst_ref=units_got.at[me],
            send_sem=units_sem.at[0, hop - 1], recv_sem=units_sem.at[1, hop - 1],
            device_id=(peer, index), device_id_type=MESH,
        )

    def units_own():
        return pltpu.make_async_copy(units.at[me], units_got.at[me], units_sem.at[0, RING - 1])

    def weight(s):
        return pltpu.make_async_copy(out_weights[s], weights.at[s], weight_sem.at[s])

    def save(b, s):
        low, high, whole = ((0, rows, image_rows), (rows, texts, text_rows))[s]
        return pltpu.make_async_copy(
            rows_in.at[b, pl.ds(low, high)], whole.at[pl.ds(b * high, high)], rows_sem.at[s, b]
        )

    def rows_back(second, middle, cotangent, stream):
        centred = middle - jnp.mean(middle, axis=-1, keepdims=True)
        spread = lax.rsqrt(jnp.mean(centred * centred, axis=-1, keepdims=True) + EPS)
        normed = centred * spread
        wide = second * mods[2 * stream + 1 : 2 * stream + 2]
        inner = jnp.mean(wide, axis=-1, keepdims=True)
        cross = jnp.mean(wide * normed, axis=-1, keepdims=True)
        grad = cotangent.astype(WIDE) + (wide - inner - normed * cross) * spread
        return grad, (mods[2 * stream : 2 * stream + 1] * grad).astype(LOW)

    @pl.when(at == 0)
    def _():
        for i in range(2):
            keep(i).start()
            weight(i).start()
        text_ring.load_all()
        ring.load_all()
        meet(
            [((me + hop) % RING, index) for hop in range(1, RING)]
            + [(me, tensor_peer(hop)) for hop in (1, 2)]
        )
        for i in range(2):
            near(i).start()
        text_ring.start()
        for i in range(2):
            keep(i).wait()
            near(i).wait()
        far_sent[...] = (parts[1].astype(WIDE) + got[1].astype(WIDE)).astype(LOW)
        far = pltpu.make_async_remote_copy(
            src_ref=far_sent, dst_ref=far_got, send_sem=sems.at[0, 2], recv_sem=sems.at[1, 2],
            device_id=(me, tensor_peer(2)), device_id_type=MESH,
        )
        far.start()
        for step in range(1, 6):
            text_ring.step(step)
        ring.start()
        far.wait()

        def image_chunk(i, _):
            some = pl.ds(pl.multiple_of(i * chunk, chunk), chunk)
            second = parts[0, some].astype(WIDE) + got[0, some].astype(WIDE)
            second = second + far_got[some].astype(WIDE)
            image_second[some] = second
            grad, low = rows_back(second, mid_image[some], cot_image[some], 0)
            image_grad[some] = grad
            rows_in[0, some] = low
            return 0

        lax.fori_loop(0, rows // chunk, image_chunk, 0)
        to_far(0).start()
        to_near(0).start()
        for step in (6, 7):
            text_ring.step(step)
        pooled = text_sum.shape[0]
        text_second[...] = jnp.zeros_like(text_second)
        text_second[:pooled] = text_sum[...]
        grad, low = rows_back(text_second[...], mid_text[...], cot_text[...], 1)
        text_grad[...] = grad
        rows_in[0, rows:] = low
        to_far(1).start()
        to_near(1).start()
        ring.step(1)
        for s in range(2):
            to_far(s).wait()
            forward(s).start()
        for s in range(2):
            weight(s).wait()
            to_near(s).wait()

        def through(b):
            image = dot(rows_in[b, :rows], weights[0], NT).astype(LOW)
            mixed_grad[b * rows : (b + 1) * rows] = image
            text = dot(rows_in[b, rows:], weights[1], NT).astype(LOW)
            mixed_grad[split + b * texts : split + (b + 1) * texts] = text

        for b in range(3):
            through(b)
        ring.step(2)
        for s in range(2):
            forward(s).wait()
        through(3)
        for b in range(4):
            for s in range(2):
                save(b, s).start()

    far_copies = [
        pltpu.make_async_remote_copy(
            src_ref=theirs[s], dst_ref=fars[s], send_sem=far_sem.at[0, s], recv_sem=far_sem.at[1, s],
            device_id=(me, tensor_peer(2)), device_id_type=MESH,
        )
        for s in range(2)
    ]

    @pl.when(at == 1)
    def _():
        for copy in far_copies:
            copy.start()
        units_own().start()
        for hop in range(1, RING):
            units_copy(hop).start()

    for step, when in ((3, 1), (4, 6), (5, 11)):

        @pl.when(at == when)
        def _():
            ring.step(step)

    place = (
        pl.ds(pl.multiple_of(pl.program_id(1) * block, block), block),
        pl.ds(pl.multiple_of(pl.program_id(0) * LANES, LANES), LANES),
    )
    attend_back_pair(
        split,
        (bias_ref, q_ref, k_ref, v_ref, o_ref, mixed_grad.at[place], lse_ref)
        + (dq_ref, dk_ref, dv_ref, dk_acc, dv_acc),
    )

    @pl.when(at == last)
    def _():
        ring.step(6)
        ring.step(7)
        ring.end()
        text_ring.end()
        for copy in far_copies:
            copy.wait()
        units_own().wait()
        for hop in range(1, RING):
            units_copy(hop).wait()
        for b in range(4):
            for s in range(2):
                save(b, s).wait()


def back_ring(
    joint, bias, mixed, lse, split, heads, text_part, middle, cotangent, mods, partial,
    out_weights, grads, theirs, units, ident, block=256,
):
    rows, pairs = joint.shape[0], heads // 2
    whole = lambda part: pl.BlockSpec((rows, LANES), lambda h, i: (0, part * pairs + h))
    some = pl.BlockSpec((block, LANES), lambda h, i: (i, h))
    image_rows, width = middle[0].shape
    texts = middle[1].shape[0]
    depth, pooled = heads * HEAD_DIM, text_part.shape[0] // RING
    found = pl.pallas_call(
        functools.partial(back_kernel, split, 64),
        grid=(pairs, rows // block),
        in_specs=[
            pl.BlockSpec((rows - split, 1), lambda h, i: (0, 0)),
            some,
            whole(1),
            whole(2),
            some,
            pl.BlockSpec((1, 8, block), lambda h, i: (h, 0, i)),
            *[WHOLE] * 5,
            *[ANY] * 9,
        ],
        out_specs=[some, whole(0), whole(0), *[WHOLE] * 3, *[ANY] * 4, *[WHOLE] * 3, ANY],
        out_shape=[
            *[jax.ShapeDtypeStruct((rows, depth), LOW)] * 3,
            *[jax.ShapeDtypeStruct((n, width), WIDE) for n in (image_rows, image_rows, texts)],
            *[jax.ShapeDtypeStruct((4 * n, width), LOW) for n in (image_rows, texts)],
            *[jax.ShapeDtypeStruct(t.shape, t.dtype) for t in theirs],
            *[jax.ShapeDtypeStruct((g.shape[0] // RING, g.shape[1]), WIDE) for g in grads],
            jax.ShapeDtypeStruct((texts, width), WIDE),
            jax.ShapeDtypeStruct(units.shape, units.dtype),
        ],
        scratch_shapes=[
            *[pltpu.VMEM((rows, LANES), WIDE)] * 2,
            pltpu.VMEM((2, depth, width), LOW),
            *[pltpu.VMEM((2, image_rows, width), LOW)] * 2,
            *[pltpu.VMEM((image_rows, width), LOW)] * 2,
            pltpu.VMEM((4, image_rows + texts, width), LOW),
            pltpu.VMEM((rows, depth), LOW),
            pltpu.SemaphoreType.DMA((2,)),
            pltpu.SemaphoreType.DMA((2, 3)),
            pltpu.SemaphoreType.DMA((2, 2, 3)),
            pltpu.SemaphoreType.DMA((2,)),
            pltpu.SemaphoreType.DMA((2, 4)),
            pltpu.SemaphoreType.DMA((2, 2)),
            pltpu.VMEM((pooled, width), WIDE),
            pltpu.SemaphoreType.DMA((2, RING)),
            *ScatterRing.scratch([g.shape for g in grads]),
            *ScatterRing.scratch([text_part.shape]),
        ],
        compiler_params=pltpu.CompilerParams(
            collective_id=ident, has_side_effects=True, vmem_limit_bytes=VMEM_LIMIT
        ),
        name="back_ring",
    )(
        bias.T, joint, joint, joint, mixed, lse, *middle, *cotangent, mods, text_part,
        partial, *out_weights, *grads, *theirs, units,
    )
    return found


def attend_kernel(split, count, waits, *refs):
    bias_ref, q_ref, k_ref, v_ref = refs[:4]
    blocks, (out_ref, lse_ref) = refs[4 : 4 + count], refs[4 + count : 6 + count]
    at = pl.program_id(0) * pl.num_programs(1) + pl.program_id(1)
    if count:
        ring = GatherRing(blocks, refs[6 + count : 6 + 2 * count], refs[6 + 2 * count :])

        @pl.when(at == 0)
        def _():
            meet(ring.sides)
            ring.start()

        for step, when in enumerate(waits):

            @pl.when(at == when)
            def _():
                ring.step(step + 1)

    attend_pair(split, bias_ref, q_ref, k_ref, v_ref, out_ref, lse_ref)
    if count:

        @pl.when(at == pl.num_programs(0) * pl.num_programs(1) - 1)
        def _():
            for step in range(len(waits) + 1, ring.STEPS + 1):
                ring.step(step)
            ring.end()


def attend(joint, bias, split, heads, blocks, ident, waits):
    rows, pairs, count, block = joint.shape[0], heads // 2, len(blocks), joint.shape[0] // 2
    whole = lambda part: pl.BlockSpec((rows, LANES), lambda h, i: (0, part * pairs + h))
    extra = dict(collective_id=ident, has_side_effects=True) if count else {}
    found = pl.pallas_call(
        functools.partial(attend_kernel, split, count, waits),
        grid=(pairs, 2),
        in_specs=[
            pl.BlockSpec((1, rows - split), lambda h, i: (0, 0)),
            pl.BlockSpec((block, LANES), lambda h, i: (i, h)),
            whole(1),
            whole(2),
            *[ANY] * count,
        ],
        out_specs=[
            pl.BlockSpec((block, LANES), lambda h, i: (i, h)),
            pl.BlockSpec((1, 8, block), lambda h, i: (h, 0, i)),
            *[ANY] * count,
        ],
        out_shape=[
            jax.ShapeDtypeStruct((rows, heads * HEAD_DIM), LOW),
            jax.ShapeDtypeStruct((pairs, 8, rows), WIDE),
            *[jax.ShapeDtypeStruct((RING * b.shape[0], b.shape[1]), b.dtype) for b in blocks],
        ],
        scratch_shapes=GatherRing.scratch(count) if count else [],
        compiler_params=pltpu.CompilerParams(vmem_limit_bytes=VMEM_LIMIT, **extra),
        name="attend",
    )(bias, joint, joint, joint, *blocks)
    return found[0], found[1], found[2:]


def attend_back_pair(split, refs):
    (bias_ref, q_ref, k_ref, v_ref, o_ref, g_ref, lse_ref, dq_ref, dk_ref, dv_ref, dk_acc, dv_acc) = refs
    step = pl.program_id(1)
    scale = HEAD_DIM ** (-0.5)

    @pl.when(step == 0)
    def _():
        dk_acc[...] = jnp.zeros_like(dk_acc)
        dv_acc[...] = jnp.zeros_like(dv_acc)

    product = (g_ref[...].astype(WIDE) * o_ref[...].astype(WIDE)).T
    bias = bias_ref[...]
    dq = None
    for head in range(2):
        mine = head_lanes(head)
        queries = jnp.where(mine, q_ref[...] * scale, 0).astype(LOW)
        grads = jnp.where(mine, g_ref[...], 0).astype(LOW)
        keys = jnp.where(mine, k_ref[...], 0).astype(LOW)
        own = product[head * HEAD_DIM : (head + 1) * HEAD_DIM]
        delta = jnp.sum(own, axis=0, keepdims=True)
        total = lse_ref[0][4 * head : 4 * head + 1]
        for low, high in ((0, split), (split, k_ref.shape[0])):
            scores = dot(k_ref[low:high], queries, NT)
            if low:
                scores = scores + bias
            probs = jnp.exp(scores - total)
            grad_probs = dot(v_ref[low:high], grads, NT)
            grad_scores = (probs * (grad_probs - delta)).astype(LOW)
            dv_acc[low:high] += dot(probs.astype(LOW), grads, NN)
            dk_acc[low:high] += dot(grad_scores, queries, NN)
            part = dot(grad_scores, keys[low:high], TN)
            dq = part if dq is None else dq + part
    dq_ref[...] = (dq * scale).astype(LOW)

    @pl.when(step == pl.num_programs(1) - 1)
    def _():
        dk_ref[...] = dk_acc[...].astype(LOW)
        dv_ref[...] = dv_acc[...].astype(LOW)


def attend_back_kernel(split, count, waits, *refs):
    ins, rest = refs[:7], refs[7:]
    grads, outs, rest = rest[:count], rest[count : count + 3], rest[count + 3 :]
    sums, accs, rest = rest[:count], rest[count : count + 2], rest[count + 2 :]
    at = pl.program_id(0) * pl.num_programs(1) + pl.program_id(1)
    if count:
        ring = ScatterRing(grads, sums, rest)

        @pl.when(at == 0)
        def _():
            ring.load_all()
            meet(ring.sides)
            ring.start()

        for step, when in enumerate(waits):

            @pl.when(at == when)
            def _():
                ring.step(step + 1)

    attend_back_pair(split, (*ins, *outs, *accs))
    if count:

        @pl.when(at == pl.num_programs(0) * pl.num_programs(1) - 1)
        def _():
            for step in range(len(waits) + 1, ring.STEPS + 1):
                ring.step(step)
            ring.end()


def attend_back(joint, bias, mixed, grad, lse, split, heads, grads, ident, waits):
    rows, pairs, count, block = joint.shape[0], heads // 2, len(grads), joint.shape[0] // 2
    whole = lambda part: pl.BlockSpec((rows, LANES), lambda h, i: (0, part * pairs + h))
    some = pl.BlockSpec((block, LANES), lambda h, i: (i, h))
    extra = dict(collective_id=ident, has_side_effects=True) if count else {}
    found = pl.pallas_call(
        functools.partial(attend_back_kernel, split, count, waits),
        grid=(pairs, 2),
        in_specs=[
            pl.BlockSpec((rows - split, 1), lambda h, i: (0, 0)),
            some,
            whole(1),
            whole(2),
            some,
            some,
            pl.BlockSpec((1, 8, block), lambda h, i: (h, 0, i)),
            *[ANY] * count,
        ],
        out_specs=[some, whole(0), whole(0), *[WHOLE] * count],
        out_shape=[
            *[jax.ShapeDtypeStruct((rows, heads * HEAD_DIM), LOW)] * 3,
            *[jax.ShapeDtypeStruct((g.shape[0] // RING, g.shape[1]), WIDE) for g in grads],
        ],
        scratch_shapes=[
            *[pltpu.VMEM((rows, LANES), WIDE)] * 2,
            *(ScatterRing.scratch([g.shape for g in grads]) if count else []),
        ],
        compiler_params=pltpu.CompilerParams(vmem_limit_bytes=VMEM_LIMIT, **extra),
        name="attend_back",
    )(bias.T, joint, joint, joint, mixed, grad, lse, *grads)
    return found[:3], found[3:]


def local(size, image, text, cond, w_ada, w_qkv, w_out, w_up, w_down, grad_image, grad_text):
    index = lax.axis_index("tensor")
    seqs = size
    image_rows, width = image.shape[1], image.shape[2]
    text_tokens = text.shape[1]
    text_own = -(-text_tokens // 4)
    text_rows = -(-text_own // TEXT_TILE) * TEXT_TILE
    pool_rows = -(-text_own // POOL_TILE) * POOL_TILE
    width_here = w_ada.shape[-1]
    ada_rows = w_ada.shape[1]
    heads_here = w_qkv.shape[-1] // HEAD_DIM

    def blocks_of(weight):
        return [weight[stream].astype(LOW).reshape(weight.shape[1], -1) for stream in range(2)]

    up_blocks, down_blocks = blocks_of(w_up), blocks_of(w_down)

    units = up_blocks[1].shape[1] // size
    text_up = lax.all_to_all(
        up_blocks[1].reshape(-1, size, units), "dp", split_axis=1, concat_axis=0, tiled=True
    ).reshape(width, units)
    text_down = down_blocks[1]

    def pool_start(rows):
        copies = jnp.broadcast_to(rows[None, :pool_rows], (size, pool_rows, width))
        rows = lax.all_to_all(copies, "dp", split_axis=0, concat_axis=0, tiled=True)
        return rows.reshape(-1, width)

    def own_pool(part):
        part = part.reshape(size, pool_rows, width)
        part = lax.all_to_all(part, "dp", split_axis=0, concat_axis=0, tiled=True)
        total = jnp.sum(part.astype(WIDE), axis=0)
        return jnp.pad(total, ((0, text_rows - pool_rows), (0, 0)))


    cond_low = jax.nn.silu(cond).astype(LOW)
    cond_rows = cond_low.reshape(seqs, ada_rows)
    ada_low = w_ada.astype(LOW)

    def own_text(rows):
        padded = jnp.pad(rows, ((0, 4 * text_own - text_tokens), (0, 0)))
        own = lax.dynamic_slice_in_dim(padded, index * text_own, text_own, 0)
        return jnp.pad(own, ((0, text_rows - text_own), (0, 0)))

    cot_rows = [grad_image[0], own_text(grad_text[0])]
    x_rows = [image[0], own_text(text[0])]
    if size == RING:
        ada_rows_low = ada_low.transpose(0, 2, 1, 3).reshape(12, ada_rows, width_here)
        attn_rows, ffn_rows, qkv_full, pooled_grad, modulation, cond_rows = first_ring(
            x_rows, cot_rows, cond_rows, ada_rows_low, blocks_of(w_qkv), pool_rows, 1
        )
        modulation, cond_rows = modulation.reshape(2, 6, width), cond_rows.astype(LOW)
    else:
        cond_rows = lax.all_to_all(cond_rows, "dp", split_axis=0, concat_axis=0, tiled=True)
        mod_parts = jnp.einsum("nd,sdkf->nskf", cond_rows, ada_low, preferred_element_type=WIDE)
        mod_parts = lax.all_to_all(mod_parts, "dp", split_axis=0, concat_axis=0, tiled=True)
        modulation = lax.all_gather(jnp.sum(mod_parts, axis=0), "tensor", axis=2, tiled=True)

    def mod_row(stream, which):
        return modulation[stream, which][None, :]

    split_at = 4 * image_rows
    places = jnp.arange(4 * text_rows)
    token = ((places // text_rows) ^ index) * text_own + places % text_rows
    is_key = (places % text_rows < text_own) & (token < text_tokens)
    bias = jnp.where(is_key, 0.0, -1e30).astype(WIDE)[None, :]

    streams = [rows.astype(WIDE) for rows in x_rows]
    cotangent = [rows.astype(WIDE) for rows in cot_rows]
    normed_in = [layer_norm(residual) for residual in streams]
    first_in = [
        (normed_in[s] * (1.0 + mod_row(s, 1)) + mod_row(s, 0)).astype(LOW) for s in range(2)
    ]
    ffn_grad = [(mod_row(s, 5) * cotangent[s]).astype(LOW) for s in range(2)]
    if size != RING:
        attn_rows = [gather_rows(rows) for rows in first_in]
        ffn_rows, pooled_grad = gather_rows(ffn_grad[0]), pool_start(ffn_grad[1])
        qkv_full = gather_dp(blocks_of(w_qkv), size, 1)
    joint = jnp.concatenate(
        [dot(attn_rows[s], qkv_full[s], NN).astype(LOW) for s in range(2)], axis=0
    )
    text_ffn_moved = gather_start(pooled_grad)
    ffn_blocks = [up_blocks[0], down_blocks[0]]
    if size == RING:
        mods = jnp.concatenate(
            [row for s in range(2) for row in (mod_row(s, 2), 1.0 + mod_row(s, 4), mod_row(s, 3))]
            + [jnp.zeros((2, width), WIDE)],
            axis=0,
        )
        found = middle_ring(
            joint, bias, x_rows, mods, split_at, heads_here, blocks_of(w_out), ffn_blocks,
            pool_rows, 2,
        )
        mixed, log_total, *found = found
        branches, middle, mlp_rows, pooled_in = found[:2], found[2:4], found[5], found[6]
        out_full, up_full, down_full = found[7:9], found[9], found[10]
    else:
        mixed, log_total, _ = attend(joint, bias, split_at, heads_here, [], 0, ())
        *out_full, up_full, down_full = gather_dp(blocks_of(w_out) + ffn_blocks, size, 2)
        branches = [
            scatter_rows(dot(mixed[:split_at], out_full[0], NN)),
            scatter_rows(dot(mixed[split_at:], out_full[1], NN)),
        ]
        middle = [streams[s] + mod_row(s, 2) * branches[s] for s in range(2)]
        second_in = [
            (layer_norm(middle[s]) * (1.0 + mod_row(s, 4)) + mod_row(s, 3)).astype(LOW)
            for s in range(2)
        ]
        mlp_rows, pooled_in = gather_rows(second_in[0]), pool_start(second_in[1])
    mixed, *text_ffn_moved = lax.optimization_barrier((mixed, *text_ffn_moved))
    text_ffn_rows = gather_end(pooled_grad, *text_ffn_moved)
    mixed_rows = [mixed[:split_at], mixed[split_at:]]
    normed_mid = [layer_norm(residual) for residual in middle]

    def gelu_back(pre_act, hidden_grad):
        return jax.vjp(gelu_tanh, pre_act)[1](hidden_grad)[0].astype(LOW)

    text_moved = gather_start(pooled_in)
    pre_act = dot(mlp_rows, up_full, NN)
    hidden = gelu_tanh(pre_act).astype(LOW)
    pre_grad = gelu_back(pre_act, dot(ffn_rows, down_full, NT))
    pre_grad, *text_moved = lax.optimization_barrier((pre_grad, *text_moved))
    text_mlp_rows = gather_end(pooled_in, *text_moved)
    text_pre_act = dot(text_mlp_rows, text_up, NN)
    text_hidden = gelu_tanh(text_pre_act).astype(LOW)
    text_pre_grad = gelu_back(text_pre_act, dot(text_ffn_rows, text_down, NT))
    text_here, text_there = scatter_start(dot(text_pre_grad, text_up, NT))
    text_far = lax.ppermute(text_there, "tensor", CHIP)
    pre_grad, text_there = lax.optimization_barrier((pre_grad, text_there))
    second_part = dot(pre_grad, up_full, NT).astype(LOW)
    down_grad = dot(hidden, ffn_rows, TN).astype(LOW)
    up_grad = dot(mlp_rows, pre_grad, TN).astype(LOW)
    here, there = scatter_start(dot(hidden, down_full, NN))
    up_grad, down_grad, second_part, there, text_far = lax.optimization_barrier(
        (up_grad, down_grad, second_part, there, text_far)
    )
    second_grad, ffn = [None, None], [None, None]
    text_second = (text_here + text_far.astype(WIDE)).astype(LOW)
    text_here, text_there = scatter_start(dot(text_hidden, text_down, NN))
    text_down_grad = dot(text_hidden, text_ffn_rows, TN)
    text_up_grad = dot(text_mlp_rows, text_pre_grad, TN).astype(LOW).reshape(size, -1, units)
    if size == RING:
        mods = jnp.concatenate(
            [row for s in range(2) for row in (mod_row(s, 2), 1.0 + mod_row(s, 4))]
            + [jnp.zeros((4, width), WIDE)],
            axis=0,
        )
        found = back_ring(
            joint, bias, mixed, log_total, split_at, heads_here, text_second, middle,
            cot_rows, mods, second_part, out_full,
            [down_grad, up_grad], [there, text_there], text_up_grad, 5,
        )
        *grads, image_second, image_middle, text_middle = found[:6]
        middle_grad, branch_rows = [image_middle, text_middle], found[6:8]
        far, text_far, down_sum, up_sum, text_sum, text_up_grad = found[8:]
        text_up_grad = text_up_grad.transpose(1, 0, 2)
        second_grad = [image_second, text_sum]
    else:
        second_grad = [scatter_rows(second_part), own_pool(text_second)]
        middle_grad, branch_rows = [None, None], [None, None]
        for s in range(2):
            wide = second_grad[s] * (1.0 + mod_row(s, 4))
            middle_grad[s] = cotangent[s] + jax.vjp(layer_norm, middle[s])[1](wide)[0]
            branch_rows[s] = gather_rows((mod_row(s, 2) * middle_grad[s]).astype(LOW))
        mixed_grad = jnp.concatenate(
            [dot(branch_rows[s], out_full[s], NT).astype(LOW) for s in range(2)], axis=0
        )
        grads = attend_back(
            joint, bias, mixed, mixed_grad, log_total, split_at, heads_here, [], 0, ()
        )[0]
        grads = list(grads)
        down_sum, up_sum = scatter_dp([down_grad, up_grad], size, 5)
        far = lax.ppermute(there, "tensor", CHIP)
        text_far = lax.ppermute(text_there, "tensor", CHIP)
        text_up_grad = lax.all_to_all(
            text_up_grad, "dp", split_axis=0, concat_axis=2, tiled=True
        )
    text_ffn = (text_here + text_far.astype(WIDE)).astype(LOW)
    text_ffn, *grads = lax.optimization_barrier((text_ffn, *grads))
    ffn[0], ffn[1] = here + far.astype(WIDE), own_pool(text_ffn)
    results = [(middle[s] + mod_row(s, 5) * ffn[s]).astype(LOW) for s in range(2)]
    gate_terms = [jnp.sum(cotangent[s] * ffn[s], axis=0)[None] for s in range(2)]
    out_grad = [dot(mixed_rows[s], branch_rows[s], TN).astype(LOW) for s in range(2)]
    joint_grad = jnp.concatenate(grads, axis=1)
    joint_rows = [joint_grad[:split_at], joint_grad[split_at:]]
    qkv_grad = [dot(attn_rows[s], joint_rows[s], TN).astype(LOW) for s in range(2)]
    other = []
    for s in range(2):
        other += [
            jnp.zeros((2, width), WIDE),
            jnp.sum(middle_grad[s] * branches[s], axis=0)[None],
            jnp.sum(second_grad[s], axis=0)[None],
            jnp.sum(second_grad[s] * normed_mid[s], axis=0)[None],
            gate_terms[s],
        ]
    other = jnp.concatenate(other + [jnp.zeros((4, width), WIDE)], axis=0)
    if size == RING:
        scale = jnp.concatenate([1.0 + mod_row(s, 1) for s in range(2)], axis=0)
        image_input, mod_sum, mod_grad, act_grad, text_out, text_grad, *found = tail_ring(
            grads, qkv_full, scale, other, x_rows, middle_grad, results[1], ada_rows_low,
            qkv_grad + out_grad, 6,
        )
        act_grad = act_grad[:, 0].reshape(1, width)
        qkv_image, qkv_text, out_image, out_text = found
        qkv_sums, out_sum = [qkv_image, qkv_text], [out_image, out_text]
        mod_sum = mod_sum[:12].reshape(2, 6, width_here)
        mod_grad = mod_grad[:, :12].reshape(seqs, 2, 6, width_here)
        mod_grad, text_up_grad = lax.optimization_barrier((mod_grad, text_up_grad))
    else:
        *qkv_sums, out_image, out_text = scatter_dp(qkv_grad + out_grad, size, 6)
        out_sum = [out_image, out_text]
        first_parts = [dot(joint_rows[s], qkv_full[s], NT).astype(LOW) for s in range(2)]
        here, there = scatter_start(
            jnp.concatenate(
                [
                    part[b * (part.shape[0] // 4) : (b + 1) * (part.shape[0] // 4)]
                    for b in range(4)
                    for part in first_parts
                ]
            )
        )
        far = lax.ppermute(there, "tensor", CHIP)
        first_rows = here + far.astype(WIDE)
        first_grad = [first_rows[:image_rows], first_rows[image_rows:]]
        input_grad, first_terms = [None, None], []
        for s in range(2):
            wide = first_grad[s] * (1.0 + mod_row(s, 1))
            input_grad[s] = middle_grad[s] + jax.vjp(layer_norm, streams[s])[1](wide)[0]
            shift = jnp.sum(first_grad[s], axis=0)
            gain = jnp.sum(first_grad[s] * normed_in[s], axis=0)
            first_terms.append(jnp.stack([shift, gain]))
        image_input = input_grad[0]
        text_out = lax.all_gather(results[1], "tensor", axis=0)
        text_grad = lax.all_gather(input_grad[1], "tensor", axis=0)
        mod_terms = other[:12].reshape(2, 6, width).at[:, :2].set(jnp.stack(first_terms))
        mod_split = mod_terms.reshape(2, 6, 4, width_here).transpose(2, 0, 1, 3)
        mod_sum = jnp.sum(
            lax.all_to_all(mod_split, "tensor", split_axis=0, concat_axis=0, tiled=True), axis=0
        )
        mod_low = jnp.broadcast_to(mod_sum.astype(LOW)[None], (seqs,) + mod_sum.shape)
        mod_grad = lax.all_to_all(mod_low, "dp", split_axis=0, concat_axis=0, tiled=True)
        act_parts = jnp.einsum("nskf,sdkf->nd", mod_grad, ada_low, preferred_element_type=WIDE)
        act_parts = lax.all_to_all(act_parts, "dp", split_axis=0, concat_axis=0, tiled=True)
        act_grad = lax.psum(act_parts.reshape(1, width), "tensor")
    shift_grad = mod_sum[:, 3]
    text_up_grad = text_up_grad.reshape(-1, size * units).astype(WIDE)
    ada_grad = jnp.einsum("nd,nskf->sdkf", cond_rows, mod_grad, preferred_element_type=WIDE)
    cond_grad = jax.vjp(jax.nn.silu, cond)[1](act_grad)[0]

    def whole_text(blocks):
        return blocks[:, :text_own].reshape(4 * text_own, width)[:text_tokens][None]

    down_sum = jnp.stack([down_sum, text_down_grad])
    up_sum = jnp.stack([up_sum, text_up_grad])
    qkv_sum, out_sum = jnp.stack(qkv_sums), jnp.stack(out_sum)

    return (
        results[0][None],
        whole_text(text_out),
        image_input[None],
        whole_text(text_grad),
        cond_grad,
        shift_grad[None],
        ada_grad,
        qkv_sum.reshape(w_qkv.shape),
        out_sum.reshape(w_out.shape),
        up_sum,
        down_sum,
    )


def solution(mesh):
    size = mesh.shape["dp"]

    def step(*args):
        return local(size, *args)

    return jax.shard_map(
        step,
        mesh=mesh,
        in_specs=(
            P("dp", "tensor", None),
            P("dp", None, None),
            P("dp", None),
            P(None, "dp", None, "tensor"),
            P(None, "dp", None, "tensor"),
            P(None, ("tensor", "dp"), None),
            P(None, "dp", "tensor"),
            P(None, ("tensor", "dp"), None),
            P("dp", "tensor", None),
            P("dp", None, None),
        ),
        out_specs=(
            P("dp", "tensor", None),
            P("dp", None, None),
            P("dp", "tensor", None),
            P("dp", None, None),
            P("dp", None),
            P("dp", None, "tensor"),
            P(None, "dp", None, "tensor"),
            P(None, "dp", None, "tensor"),
            P(None, ("tensor", "dp"), None),
            P(None, "dp", "tensor"),
            P(None, ("tensor", "dp"), None),
        ),
        check_vma=False,
    )
```

```python
import functools

import jax
import jax.numpy as jnp
from jax import lax
from jax.experimental import pallas as pl
from jax.experimental.pallas import tpu as pltpu
from jax.sharding import PartitionSpec as P

HEAD_DIM = 64
EPS = 1e-06
LOW = jnp.bfloat16
WIDE = jnp.float32
TEXT_TILE = 64
POOL_TILE = 16
LANES = 128
NT, NN, TN = ((1,), (1,)), ((1,), (0,)), ((0,), (0,))


def dot(left, right, dims):
    return lax.dot_general(left, right, (dims, ((), ())), preferred_element_type=WIDE)


def layer_norm(values):
    average = jnp.mean(values, axis=-1, keepdims=True)
    centred = values - average
    spread = jnp.mean(centred * centred, axis=-1, keepdims=True)
    return centred * lax.rsqrt(spread + EPS)


def gelu_tanh(values):
    return jax.nn.gelu(values, approximate=True)


MESH = pl.DeviceIdType.MESH
RING = 8


def ring_dp(place):
    place = place % RING
    return 2 * place + (place // (RING // 2)) * (2 * RING - 1 - 4 * place)


def ring_place():
    index = lax.axis_index("dp")
    return index // 2 + (index % 2) * (RING - 1 - 2 * (index // 2))


def ring_sides(place):
    tensor = lax.axis_index("tensor")
    return (ring_dp(place + 1), tensor), (ring_dp(place + RING - 1), tensor)


def meet(sides):
    barrier = pltpu.get_barrier_semaphore()
    for side in sides:
        pl.semaphore_signal(barrier, inc=1, device_id=side, device_id_type=MESH)
    pl.semaphore_wait(barrier, len(sides))


def half_of(rows, columns, way):
    if rows // 2 % 16 == 0:
        return way * (rows // 2), rows // 2, 0, columns
    return 0, rows, way * (columns // 2), columns // 2


class GatherRing:
    STEPS = RING // 2

    def __init__(self, blocks, fulls, sems):
        self.blocks, self.fulls = blocks, fulls
        self.own_sem, self.send_sem, self.recv_sem = sems
        self.place = ring_place()
        self.sides = ring_sides(self.place)

    @staticmethod
    def scratch(count):
        steps = RING // 2
        return [
            pltpu.SemaphoreType.DMA((count,)),
            pltpu.SemaphoreType.DMA((count, 2, steps)),
            pltpu.SemaphoreType.DMA((count, 2, steps)),
        ]

    def copy(self, i, way, step):
        rows, columns = self.blocks[i].shape
        at = self.place + (RING - step if way == 0 else step)
        top, high, left, wide = 0, rows, 0, columns
        if step == self.STEPS - 1:
            top, high, left, wide = half_of(rows, columns, way)
        there = self.fulls[i].at[pl.ds(ring_dp(at) * rows + top, high), pl.ds(left, wide)]
        here = there if step else self.blocks[i]
        return pltpu.make_async_remote_copy(
            src_ref=here,
            dst_ref=there,
            send_sem=self.send_sem.at[i, way, step],
            recv_sem=self.recv_sem.at[i, way, step],
            device_id=self.sides[way],
            device_id_type=MESH,
        )

    def own(self, i):
        rows = self.blocks[i].shape[0]
        start = ring_dp(self.place) * rows
        return pltpu.make_async_copy(
            self.blocks[i], self.fulls[i].at[pl.ds(start, rows)], self.own_sem.at[i]
        )

    def start(self):
        for i in range(len(self.blocks)):
            for way in range(2):
                self.copy(i, way, 0).start()
            self.own(i).start()

    def step(self, step):
        for i in range(len(self.blocks)):
            for way in range(2):
                self.copy(i, way, step - 1).wait_recv()
                if step < self.STEPS:
                    self.copy(i, way, step).start()

    def end(self):
        for i in range(len(self.blocks)):
            self.own(i).wait()
            for way in range(2):
                for step in range(self.STEPS):
                    self.copy(i, way, step).wait_send()


class ScatterRing:
    STEPS = RING - 1

    def __init__(self, grads, sums, scratch):
        self.grads, self.sums = grads, sums
        count = len(grads)
        self.mine, self.got = scratch[:count], scratch[count : 2 * count]
        self.mine_sem, self.send_sem, self.recv_sem = scratch[2 * count :]
        self.place = ring_place()
        self.sides = ring_sides(self.place)

    @staticmethod
    def scratch(shapes):
        sizes = [half_of(rows // RING, columns, 0) for rows, columns in shapes]
        halves = [(2, RING, high, wide) for _, high, _, wide in sizes]
        gots = [(2, RING - 1, high, wide) for _, high, _, wide in sizes]
        count = len(shapes)
        return [
            *[pltpu.VMEM(shape, LOW) for shape in halves],
            *[pltpu.VMEM(shape, LOW) for shape in gots],
            pltpu.SemaphoreType.DMA((count, 2, RING)),
            pltpu.SemaphoreType.DMA((count, 2, RING - 1)),
            pltpu.SemaphoreType.DMA((count, 2, RING - 1)),
        ]

    def load(self, i, way, step):
        rows, columns = self.grads[i].shape[0] // RING, self.grads[i].shape[1]
        at = self.place + (2 * RING - step - 1 if way == 0 else step + 1)
        top, high, left, wide = half_of(rows, columns, way)
        return pltpu.make_async_copy(
            self.grads[i].at[pl.ds(ring_dp(at) * rows + top, high), pl.ds(left, wide)],
            self.mine[i].at[way, step],
            self.mine_sem.at[i, way, step],
        )

    def copy(self, i, way, step):
        return pltpu.make_async_remote_copy(
            src_ref=self.mine[i].at[way, step],
            dst_ref=self.got[i].at[way, step],
            send_sem=self.send_sem.at[i, way, step],
            recv_sem=self.recv_sem.at[i, way, step],
            device_id=self.sides[way],
            device_id_type=MESH,
        )

    def load_all(self):
        for step in range(RING):
            for i in range(len(self.grads)):
                for way in range(2):
                    self.load(i, way, step).start()

    def start(self):
        for i in range(len(self.grads)):
            for way in range(2):
                self.load(i, way, 0).wait()
                self.copy(i, way, 0).start()

    def step(self, step):
        for i in range(len(self.grads)):
            rows, columns = self.grads[i].shape[0] // RING, self.grads[i].shape[1]
            for way in range(2):
                top, high, left, wide = half_of(rows, columns, way)
                self.load(i, way, step).wait()
                self.copy(i, way, step - 1).wait_recv()
                total = self.mine[i][way, step].astype(WIDE) + self.got[i][way, step - 1].astype(WIDE)
                if step < self.STEPS:
                    self.mine[i][way, step] = total.astype(LOW)
                    self.copy(i, way, step).start()
                else:
                    self.sums[i][pl.ds(top, high), pl.ds(left, wide)] = total

    def end(self):
        for i in range(len(self.grads)):
            for way in range(2):
                for step in range(self.STEPS):
                    self.copy(i, way, step).wait_send()


ANY = pl.BlockSpec(memory_space=pl.ANY)
WHOLE = pl.BlockSpec(memory_space=pltpu.VMEM)
VMEM_LIMIT = 56 << 20


def gather_kernel(count, *refs):
    ring = GatherRing(refs[:count], refs[count : 2 * count], refs[2 * count :])
    meet(ring.sides)
    ring.start()
    for step in range(1, ring.STEPS + 1):
        ring.step(step)
    ring.end()


def gather_ring(blocks, ident):
    count = len(blocks)
    return pl.pallas_call(
        functools.partial(gather_kernel, count),
        out_shape=[
            jax.ShapeDtypeStruct((RING * block.shape[0], block.shape[1]), block.dtype)
            for block in blocks
        ],
        in_specs=[ANY] * count,
        out_specs=[ANY] * count,
        scratch_shapes=GatherRing.scratch(count),
        compiler_params=pltpu.CompilerParams(
            collective_id=ident, has_side_effects=True, vmem_limit_bytes=VMEM_LIMIT
        ),
        name="gather_ring",
    )(*blocks)


def scatter_kernel(count, *refs):
    ring = ScatterRing(refs[:count], refs[count : 2 * count], refs[2 * count :])
    ring.load_all()
    meet(ring.sides)
    ring.start()
    for step in range(1, ring.STEPS + 1):
        ring.step(step)
    ring.end()


def scatter_ring(grads, ident):
    count = len(grads)
    return pl.pallas_call(
        functools.partial(scatter_kernel, count),
        out_shape=[
            jax.ShapeDtypeStruct((grad.shape[0] // RING, grad.shape[1]), WIDE) for grad in grads
        ],
        in_specs=[ANY] * count,
        out_specs=[WHOLE] * count,
        scratch_shapes=ScatterRing.scratch([grad.shape for grad in grads]),
        compiler_params=pltpu.CompilerParams(
            collective_id=ident, has_side_effects=True, vmem_limit_bytes=VMEM_LIMIT
        ),
        name="scatter_ring",
    )(*grads)


def gather_dp(blocks, size, ident):
    if size == RING:
        return gather_ring(blocks, ident)
    return [lax.all_gather(block, "dp", axis=0, tiled=True) for block in blocks]


def scatter_dp(grads, size, ident):
    if size == RING:
        return scatter_ring(grads, ident)
    return [
        lax.psum_scatter(grad, "dp", scatter_dimension=0, tiled=True).astype(WIDE)
        for grad in grads
    ]


def beside(ring, blocks, size, ident, before, after):
    blocks = lax.optimization_barrier(tuple(blocks) + tuple(before))[: len(blocks)]
    found = tuple(ring(list(blocks), size, ident))
    held = lax.optimization_barrier(found + tuple(after))
    return held[: len(found)], held[len(found) :]


CORE = [(i, i ^ 1) for i in range(4)]
CHIP = [(i, i ^ 2) for i in range(4)]


def gather_start(own):
    near = lax.ppermute(own, "tensor", CORE)
    far = lax.ppermute(own, "tensor", CHIP)
    return near, far


def gather_end(own, near, far):
    last = lax.ppermute(far, "tensor", CORE)
    return jnp.concatenate([own, near, far, last], axis=0)


def gather_rows(own):
    return gather_end(own, *gather_start(own))


def scatter_start(partial):
    rows = partial.shape[0] // 4
    low = partial.astype(LOW)
    part = [low[b * rows : (b + 1) * rows] for b in range(4)]
    sent = lax.ppermute(jnp.concatenate([part[1], part[3]]), "tensor", CORE)
    here = part[0].astype(WIDE) + sent[:rows].astype(WIDE)
    return here, (part[2].astype(WIDE) + sent[rows:].astype(WIDE)).astype(LOW)


def scatter_rows(partial):
    here, there = scatter_start(partial)
    return here + lax.ppermute(there, "tensor", CHIP).astype(WIDE)


def tensor_peer(hop):
    index = lax.axis_index("tensor")
    if hop == 1:
        return index + 1 - 2 * (index % 2)
    return (index + 2) % 4 if hop == 2 else 3 - index


def tail_kernel(columns, count, *refs):
    d_parts, scale, other, x_image, x_text, mid_image, mid_text, text_out, ada = refs[:3], *refs[3:11]
    qkv_weights, grads, refs = refs[11:13], refs[13 : 13 + count], refs[13 + count :]
    image_grad, mod_sum, mod_all, cond_sum, *wholes = refs[:6]
    sums, refs = refs[6 : 6 + count], refs[6 + count :]
    far, text_grad, terms, parts, low, slots, far_sem, part_sem, slot_sem, text_sem = refs[:10]
    weights, sent, got, far_sent, here, acts, act_got, act_rows, weight_sem, act_sem, act_row_sem = refs[10:21]
    ring = ScatterRing(grads, sums, refs[21:])
    me, index = lax.axis_index("dp"), lax.axis_index("tensor")
    far_copy = pltpu.make_async_remote_copy(
        src_ref=far_sent, dst_ref=far, send_sem=far_sem.at[0, 1], recv_sem=far_sem.at[1, 1],
        device_id=(me, tensor_peer(2)), device_id_type=MESH,
    )
    weight_copies = [
        pltpu.make_async_copy(qkv_weights[s], weights.at[s], weight_sem.at[s]) for s in range(2)
    ]

    def first_part(b):
        found = []
        for s, rows in ((0, x_image.shape[0]), (1, x_text.shape[0])):
            low_row = b * rows + (0 if s == 0 else 4 * x_image.shape[0])
            total = None
            for p in range(3):
                wide = d_parts[p].shape[1]
                weight = weights[s, :, p * wide : (p + 1) * wide]
                part = dot(d_parts[p][low_row : low_row + rows], weight, NT)
                total = part if total is None else total + part
            found.append(total)
        return jnp.concatenate(found, axis=0)

    def act_copy(hop):
        return pltpu.make_async_remote_copy(
            src_ref=acts, dst_ref=act_got.at[hop - 1],
            send_sem=act_sem.at[0, hop - 1], recv_sem=act_sem.at[1, hop - 1],
            device_id=(me, tensor_peer(hop)), device_id_type=MESH,
        )

    def act_row_copy(hop):
        peer = (me + hop) % RING
        return pltpu.make_async_remote_copy(
            src_ref=act_rows.at[peer], dst_ref=cond_sum.at[me],
            send_sem=act_row_sem.at[0, hop - 1], recv_sem=act_row_sem.at[1, hop - 1],
            device_id=(peer, index), device_id_type=MESH,
        )

    def part_copy(hop):
        peer = tensor_peer(hop)
        start = pl.multiple_of(peer * columns, LANES)
        return pltpu.make_async_remote_copy(
            src_ref=terms.at[:, pl.ds(start, columns)], dst_ref=parts.at[hop - 1],
            send_sem=part_sem.at[0, hop - 1], recv_sem=part_sem.at[1, hop - 1],
            device_id=(me, peer), device_id_type=MESH,
        )

    def slot_copy(hop):
        return pltpu.make_async_remote_copy(
            src_ref=low, dst_ref=slots.at[me],
            send_sem=slot_sem.at[0, hop - 1], recv_sem=slot_sem.at[1, hop - 1],
            device_id=((me + hop) % RING, index), device_id_type=MESH,
        )

    def text_copy(i, hop):
        source = (text_out, text_grad)[i]
        return pltpu.make_async_remote_copy(
            src_ref=source, dst_ref=wholes[i].at[index],
            send_sem=text_sem.at[i, 0, hop], recv_sem=text_sem.at[i, 1, hop],
            device_id=(me, tensor_peer(hop)), device_id_type=MESH,
        )

    def text_own(i):
        source = (text_out, text_grad)[i]
        return pltpu.make_async_copy(source, wholes[i].at[index], text_sem.at[i, 0, 0])

    def rows_back(first, x, middle, gain):
        x = x.astype(WIDE)
        centred = x - jnp.mean(x, axis=-1, keepdims=True)
        spread = lax.rsqrt(jnp.mean(centred * centred, axis=-1, keepdims=True) + EPS)
        normed = centred * spread
        wide = first * gain
        inner = jnp.mean(wide, axis=-1, keepdims=True)
        cross = jnp.mean(wide * normed, axis=-1, keepdims=True)
        sums = jnp.sum(first, axis=0, keepdims=True), jnp.sum(first * normed, axis=0, keepdims=True)
        return middle + (wide - inner - normed * cross) * spread, *sums

    for copy in weight_copies:
        copy.start()
    ring.load_all()
    meet(
        [(me, tensor_peer(hop)) for hop in (1, 2, 3)]
        + [((me + hop) % RING, index) for hop in range(1, RING)]
    )
    ring.start()
    for copy in weight_copies:
        copy.wait()
    near = exchange_sums(first_part, sent, got, far_sem, me)
    ring.step(1)
    here[...] = first_part(0)
    far_sent[...] = first_part(2).astype(LOW)
    near.wait()
    far_sent[...] = (far_sent[...].astype(WIDE) + got[1].astype(WIDE)).astype(LOW)
    far_copy.start()
    here[...] += got[0].astype(WIDE)
    ring.step(2)
    far_copy.wait()
    terms[...] = other[...]
    chunk = 64

    def image_chunk(at, totals):
        rows = pl.ds(pl.multiple_of(at * chunk, chunk), chunk)
        first = here[rows] + far[rows].astype(WIDE)
        out, shift, gain = rows_back(first, x_image[rows], mid_image[rows], scale[0:1])
        image_grad[rows] = out
        return totals[0] + shift, totals[1] + gain

    zero = jnp.zeros((1, here.shape[1]), WIDE)
    image_rows = x_image.shape[0]
    shift, gain = lax.fori_loop(0, image_rows // chunk, image_chunk, (zero, zero))
    terms[0:1] = shift
    terms[1:2] = gain
    ring.step(3)
    text_first = here[image_rows:] + far[image_rows:].astype(WIDE)
    out, shift, gain = rows_back(text_first, x_text[...], mid_text[...], scale[1:2])
    text_grad[...] = out
    for i in range(2):
        text_own(i).start()
        for hop in (1, 2, 3):
            text_copy(i, hop).start()
    terms[6:7] = shift
    terms[7:8] = gain
    for hop in (1, 2, 3):
        part_copy(hop).start()
    ring.step(4)
    for hop in (1, 2, 3):
        part_copy(hop).wait()
    own = terms[:, pl.ds(pl.multiple_of(index * columns, LANES), columns)]
    total = own + parts[0] + parts[1] + parts[2]
    mod_sum[...] = total
    low[...] = total.astype(LOW)
    slots[pl.ds(me, 1)] = total.astype(LOW)[None]
    for hop in range(1, RING):
        slot_copy(hop).start()
    ring.step(5)
    for hop in range(1, RING):
        slot_copy(hop).wait()
    mod_all[...] = slots[...]
    wide = slots[...].astype(WIDE)
    total = None
    for which in range(12):
        rows = jnp.concatenate([wide[n, which : which + 1] for n in range(RING)], axis=0)
        part = dot(rows.astype(LOW), ada[which], NT)
        total = part if total is None else total + part
    acts[...] = total
    for hop in (1, 2, 3):
        act_copy(hop).start()
    for i in range(2):
        text_own(i).wait()
        for hop in (1, 2, 3):
            text_copy(i, hop).wait()
    ring.step(6)
    for hop in (1, 2, 3):
        act_copy(hop).wait()
    total = acts[...] + act_got[0] + act_got[1] + act_got[2]
    for n in range(RING):
        act_rows[n] = jnp.broadcast_to(total[n : n + 1], act_rows.shape[1:])
    for hop in range(1, RING):
        act_row_copy(hop).start()
    cond_sum[pl.ds(me, 1)] = act_rows[pl.ds(me, 1)]
    ring.step(7)
    for hop in range(1, RING):
        act_row_copy(hop).wait()
    ring.end()


def tail_ring(d_parts, weights, scale, other, x, middle, text_out, ada, grads, ident):
    width, shapes = scale.shape[1], [grad.shape for grad in grads]
    rows, text_rows = x[0].shape[0], x[1].shape[0]
    both, (_, depth, columns) = rows + text_rows, ada.shape
    return pl.pallas_call(
        functools.partial(tail_kernel, columns, len(grads)),
        out_shape=[
            jax.ShapeDtypeStruct((rows, width), WIDE),
            jax.ShapeDtypeStruct((16, columns), WIDE),
            jax.ShapeDtypeStruct((RING, 16, columns), LOW),
            jax.ShapeDtypeStruct((RING, 8, depth), WIDE),
            jax.ShapeDtypeStruct((4, text_rows, width), LOW),
            jax.ShapeDtypeStruct((4, text_rows, width), WIDE),
            *[jax.ShapeDtypeStruct((r // RING, c), WIDE) for r, c in shapes],
        ],
        in_specs=[WHOLE] * 11 + [ANY] * (2 + len(grads)),
        out_specs=[WHOLE] * 4 + [ANY] * 2 + [WHOLE] * len(grads),
        scratch_shapes=[
            pltpu.VMEM((both, width), LOW),
            pltpu.VMEM((text_rows, width), WIDE),
            pltpu.VMEM((16, width), WIDE),
            pltpu.VMEM((3, 16, columns), WIDE),
            pltpu.VMEM((16, columns), LOW),
            pltpu.VMEM((RING, 16, columns), LOW),
            pltpu.SemaphoreType.DMA((2, 2)),
            pltpu.SemaphoreType.DMA((2, 3)),
            pltpu.SemaphoreType.DMA((2, RING - 1)),
            pltpu.SemaphoreType.DMA((2, 2, 4)),
            pltpu.VMEM((2, *weights[0].shape), LOW),
            *[pltpu.VMEM((2, both, width), LOW)] * 2,
            pltpu.VMEM((both, width), LOW),
            pltpu.VMEM((both, width), WIDE),
            pltpu.VMEM((RING, depth), WIDE),
            pltpu.VMEM((3, RING, depth), WIDE),
            pltpu.VMEM((RING, 8, depth), WIDE),
            pltpu.SemaphoreType.DMA((2,)),
            pltpu.SemaphoreType.DMA((2, 3)),
            pltpu.SemaphoreType.DMA((2, RING - 1)),
            *ScatterRing.scratch(shapes),
        ],
        compiler_params=pltpu.CompilerParams(
            collective_id=ident, has_side_effects=True, vmem_limit_bytes=VMEM_LIMIT
        ),
        name="tail_ring",
    )(*d_parts, scale, other, *x, *middle, text_out, ada, *weights, *grads)


def head_lanes(head):
    lane = lax.broadcasted_iota(jnp.int32, (1, LANES), 1)
    return (lane < HEAD_DIM) if head == 0 else (lane >= HEAD_DIM)


def attend_pair(split, bias_ref, q_ref, k_ref, v_ref, out_ref, lse_ref):
    scale = HEAD_DIM ** (-0.5)
    bias = bias_ref[...]
    outs, totals = [], []
    for head in range(2):
        mine = head_lanes(head)
        queries = jnp.where(mine, q_ref[...] * scale, 0).astype(LOW)
        image = dot(queries, k_ref[:split], NT)
        text = dot(queries, k_ref[split:], NT) + bias
        top = jnp.maximum(
            jnp.max(image, axis=1, keepdims=True), jnp.max(text, axis=1, keepdims=True)
        )
        image = jnp.exp(image - top).astype(LOW)
        text = jnp.exp(text - top).astype(LOW)
        values = jnp.where(mine, v_ref[...], 1).astype(LOW)
        both = dot(image, values[:split], NN) + dot(text, values[split:], NN)
        sums = pltpu.roll(both, HEAD_DIM, 1)
        outs.append(both / sums)
        totals.append(top + jnp.log(sums))
    first = head_lanes(0)
    out_ref[...] = jnp.where(first, outs[0], outs[1]).astype(out_ref.dtype)
    flipped = jnp.where(first, totals[0], totals[1]).T
    lse_ref[0] = jnp.concatenate([flipped[:4], flipped[HEAD_DIM : HEAD_DIM + 4]], axis=0)


def first_kernel(chunk, *refs):
    x_image, x_text, cot_image, cot_text, cond, ada, *blocks = refs[:8]
    outs, fulls, pool, (mods, conds), refs = refs[8:11], refs[11:13], refs[13:14], refs[14:16], refs[16:]
    mines, pooled, (row_sem, own_sem) = refs[:3], refs[3], refs[4:6]
    cond_got, parts, got, cond_sem, part_sem, mod_sem = refs[6:12]
    ring = GatherRing(blocks, fulls, refs[12:15])
    text_ring = GatherRing([pooled], pool, refs[15:18])
    me, index = lax.axis_index("dp"), lax.axis_index("tensor")
    width, columns = mods.shape[1], ada.shape[2]

    def dp_copy(hop, source, target, sem):
        peer = (me + hop) % RING
        return pltpu.make_async_remote_copy(
            src_ref=source.at[peer], dst_ref=target.at[me],
            send_sem=sem.at[0, hop - 1], recv_sem=sem.at[1, hop - 1],
            device_id=(peer, index), device_id_type=MESH,
        )

    def mod_copy(hop):
        here = mods.at[:, pl.ds(pl.multiple_of(index * columns, LANES), columns)]
        return pltpu.make_async_remote_copy(
            src_ref=here, dst_ref=here,
            send_sem=mod_sem.at[0, hop - 1], recv_sem=mod_sem.at[1, hop - 1],
            device_id=(me, tensor_peer(hop)), device_id_type=MESH,
        )

    def row_copy(i, source, slot, hop, sem):
        rows = mines[i].shape[0]
        return pltpu.make_async_remote_copy(
            src_ref=source, dst_ref=outs[i].at[pl.ds(slot * rows, rows)],
            send_sem=row_sem.at[i, 0, sem], recv_sem=row_sem.at[i, 1, sem],
            device_id=(me, tensor_peer(hop)), device_id_type=MESH,
        )

    def own(i):
        rows = mines[i].shape[0]
        return pltpu.make_async_copy(mines[i], outs[i].at[pl.ds(0, rows)], own_sem.at[i])

    def to_far(i):
        return row_copy(i, mines[i], 2, 2, 0)

    def to_near(i):
        return row_copy(i, mines[i], 1, 1, 1)

    def forward(i):
        rows = mines[i].shape[0]
        return row_copy(i, outs[i].at[pl.ds(2 * rows, rows)], 3, 1, 2)

    def send(i):
        to_far(i).start()
        to_near(i).start()
        own(i).start()

    def norm_rows(x, stream):
        x = x.astype(WIDE)
        centred = x - jnp.mean(x, axis=-1, keepdims=True)
        spread = lax.rsqrt(jnp.mean(centred * centred, axis=-1, keepdims=True) + EPS)
        gain, shift = 1.0 + mods[6 * stream + 1 : 6 * stream + 2], mods[6 * stream : 6 * stream + 1]
        return (centred * spread * gain + shift).astype(LOW)

    def over_chunks(body):
        def step(i, _):
            body(pl.ds(pl.multiple_of(i * chunk, chunk), chunk))
            return 0

        lax.fori_loop(0, x_image.shape[0] // chunk, step, 0)

    meet(
        [(me, tensor_peer(hop)) for hop in (1, 2, 3)]
        + [((me + hop) % RING, index) for hop in range(1, RING)]
    )
    for hop in range(1, RING):
        dp_copy(hop, cond, cond_got, cond_sem).start()
    cond_got[pl.ds(me, 1)] = cond[pl.ds(me, 1)]
    parts[...] = jnp.zeros_like(parts)
    for hop in range(1, RING):
        dp_copy(hop, cond, cond_got, cond_sem).wait()
    rows = jnp.concatenate([cond_got[n, 0:1] for n in range(RING)], axis=0)
    conds[...] = rows
    rows = rows.astype(LOW)
    for which in range(12):
        part = dot(rows, ada[which], NN)
        for n in range(RING):
            parts[n, which : which + 1] = part[n : n + 1]
    for hop in range(1, RING):
        dp_copy(hop, parts, got, part_sem).start()
    ring.start()
    got[pl.ds(me, 1)] = parts[pl.ds(me, 1)]
    for hop in range(1, RING):
        dp_copy(hop, parts, got, part_sem).wait()
    mods[:, pl.ds(pl.multiple_of(index * columns, LANES), columns)] = jnp.sum(got[...], axis=0)
    for hop in (1, 2, 3):
        mod_copy(hop).start()
    for hop in (1, 2, 3):
        mod_copy(hop).wait()
    pooled[...] = (mods[11:12] * cot_text[: pooled.shape[0]].astype(WIDE)).astype(LOW)
    text_ring.start()

    def norm_chunk(some):
        mines[0][some] = norm_rows(x_image[some], 0)

    def grad_chunk(some):
        mines[2][some] = (mods[5:6] * cot_image[some].astype(WIDE)).astype(LOW)

    over_chunks(norm_chunk)
    send(0)
    mines[1][...] = norm_rows(x_text[...], 1)
    send(1)
    over_chunks(grad_chunk)
    send(2)
    ring.step(1)
    text_ring.step(1)
    for i in range(2):
        to_far(i).wait()
        forward(i).start()
    ring.step(2)
    text_ring.step(2)
    to_far(2).wait()
    forward(2).start()
    ring.step(3)
    text_ring.step(3)
    for i in range(3):
        own(i).wait()
        to_near(i).wait()
        forward(i).wait()
    text_ring.step(4)
    ring.step(4)
    text_ring.end()
    ring.end()


def first_ring(x, cotangent, cond, ada, blocks, pool_rows, ident):
    width, columns, depth = x[0].shape[1], ada.shape[2], ada.shape[1]
    rows = [x[0].shape[0], x[1].shape[0], x[0].shape[0]]
    fulls = [block.shape for block in blocks] + [(pool_rows, width)]
    cond = jnp.broadcast_to(cond.astype(WIDE)[:, None], (RING, 8, depth))
    found = pl.pallas_call(
        functools.partial(first_kernel, 64),
        in_specs=[WHOLE] * 6 + [ANY] * 2,
        out_specs=[ANY] * 6 + [WHOLE] * 2,
        out_shape=[
            *[jax.ShapeDtypeStruct((4 * n, width), LOW) for n in rows],
            *[jax.ShapeDtypeStruct((RING * n, wide), LOW) for n, wide in fulls],
            jax.ShapeDtypeStruct((16, width), WIDE),
            jax.ShapeDtypeStruct((RING, depth), WIDE),
        ],
        scratch_shapes=[
            *[pltpu.VMEM((n, width), LOW) for n in rows],
            pltpu.VMEM((pool_rows, width), LOW),
            pltpu.SemaphoreType.DMA((3, 2, 3)),
            pltpu.SemaphoreType.DMA((3,)),
            pltpu.VMEM((RING, 8, depth), WIDE),
            *[pltpu.VMEM((RING, 16, columns), WIDE)] * 2,
            *[pltpu.SemaphoreType.DMA((2, RING - 1))] * 2,
            pltpu.SemaphoreType.DMA((2, 3)),
            *GatherRing.scratch(2),
            *GatherRing.scratch(1),
        ],
        compiler_params=pltpu.CompilerParams(
            collective_id=ident, has_side_effects=True, vmem_limit_bytes=VMEM_LIMIT
        ),
        name="first_ring",
    )(*x, *cotangent, cond, ada, *blocks)
    return found[:2], found[2], found[3:5], found[5], found[6][:12], found[7]


def exchange_sums(part, sent, got, sems, me):
    copy = pltpu.make_async_remote_copy(
        src_ref=sent, dst_ref=got, send_sem=sems.at[0, 0], recv_sem=sems.at[1, 0],
        device_id=(me, tensor_peer(1)), device_id_type=MESH,
    )
    sent[0] = part(1).astype(LOW)
    sent[1] = part(3).astype(LOW)
    copy.start()
    return copy


def middle_kernel(split, chunk, *refs):
    bias_ref, q_ref, k_ref, v_ref, x_image, x_text, mods = refs[:7]
    out_blocks, ffn_blocks, refs = refs[7:9], refs[9:11], refs[11:]
    mixed, lse_ref, *wide_outs, text_in, image_in = refs[:8]
    branch_image, branch_text, mid_image, mid_text = wide_outs
    pool, out_fulls, ffn_fulls, refs = refs[8:9], refs[9:11], refs[11:13], refs[13:]
    weights, sent, got, far_sent, far_got, here, mine = refs[:7]
    sems, weight_sem, row_sem, own_sem = refs[7:11]
    first = GatherRing(out_blocks, out_fulls, refs[11:14])
    second = GatherRing(ffn_blocks, ffn_fulls, refs[14:17])
    third = GatherRing([text_in.at[pl.ds(0, pool[0].shape[0] // RING)]], pool, refs[17:20])
    me = lax.axis_index("dp")
    block = q_ref.shape[0]
    pair, at = pl.program_id(0), pl.program_id(0) * 2 + pl.program_id(1)
    rows = x_image.shape[0]

    @pl.when(at == 0)
    def _():
        meet([*first.sides, *[(me, tensor_peer(hop)) for hop in (1, 2)]])
        first.start()

    for step in range(1, 5):

        @pl.when(at == step)
        def _():
            first.step(step)
            if step == 3:
                second.start()

    weight_copies = [
        pltpu.make_async_copy(out_fulls[s], weights.at[s], weight_sem.at[s]) for s in range(2)
    ]

    @pl.when(at == 4)
    def _():
        first.end()
        for copy in weight_copies:
            copy.start()

    place = (
        pl.ds(pl.multiple_of(pl.program_id(1) * block, block), block),
        pl.ds(pl.multiple_of(pair * LANES, LANES), LANES),
    )
    attend_pair(split, bias_ref, q_ref, k_ref, v_ref, mixed.at[place], lse_ref)

    @pl.when(at == 2 * pl.num_programs(0) - 1)
    def _():
        for copy in weight_copies:
            copy.wait()
        text_rows = x_text.shape[0]

        def part(b):
            image = dot(mixed[b * rows : (b + 1) * rows], weights[0], NN)
            low = split + b * text_rows
            text = dot(mixed[low : low + text_rows], weights[1], NN)
            return jnp.concatenate([image, text], axis=0)

        near = exchange_sums(part, sent, got, sems, me)
        here[...] = part(0)
        far_sent[...] = part(2).astype(LOW)
        near.wait()
        far_sent[...] = (far_sent[...].astype(WIDE) + got[1].astype(WIDE)).astype(LOW)
        far = pltpu.make_async_remote_copy(
            src_ref=far_sent, dst_ref=far_got, send_sem=sems.at[0, 1], recv_sem=sems.at[1, 1],
            device_id=(me, tensor_peer(2)), device_id_type=MESH,
        )
        far.start()
        here[...] += got[0].astype(WIDE)
        second.step(1)
        far.wait()

        def norm_rows(x, branch, stream):
            middle = x.astype(WIDE) + mods[3 * stream : 3 * stream + 1] * branch
            centred = middle - jnp.mean(middle, axis=-1, keepdims=True)
            spread = lax.rsqrt(jnp.mean(centred * centred, axis=-1, keepdims=True) + EPS)
            gain, shift = mods[3 * stream + 1 : 3 * stream + 2], mods[3 * stream + 2 : 3 * stream + 3]
            return middle, (centred * spread * gain + shift).astype(LOW)

        def image_chunk(i, _):
            some = pl.ds(pl.multiple_of(i * chunk, chunk), chunk)
            branch = here[some] + far_got[some].astype(WIDE)
            branch_image[some] = branch
            middle, low = norm_rows(x_image[some], branch, 0)
            mid_image[some] = middle
            mine[some] = low
            return 0

        lax.fori_loop(0, rows // chunk, image_chunk, 0)

        def row_copy(source, slot, hop, sem):
            return pltpu.make_async_remote_copy(
                src_ref=source, dst_ref=image_in.at[pl.ds(slot * rows, rows)],
                send_sem=row_sem.at[0, sem], recv_sem=row_sem.at[1, sem],
                device_id=(me, tensor_peer(hop)), device_id_type=MESH,
            )

        own = pltpu.make_async_copy(mine, image_in.at[pl.ds(0, rows)], own_sem.at[0])
        to_far, to_near = row_copy(mine, 2, 2, 0), row_copy(mine, 1, 1, 1)
        to_far.start()
        to_near.start()
        own.start()
        branch = here[rows:] + far_got[rows:].astype(WIDE)
        branch_text[...] = branch
        middle, low = norm_rows(x_text[...], branch, 1)
        mid_text[...] = middle
        text_in[...] = low
        third.start()
        second.step(2)
        third.step(1)
        to_far.wait()
        last = row_copy(image_in.at[pl.ds(2 * rows, rows)], 3, 1, 2)
        last.start()
        third.step(2)
        second.step(3)
        third.step(3)
        own.wait()
        to_near.wait()
        last.wait()
        third.step(4)
        second.step(4)
        second.end()
        third.end()


def middle_ring(joint, bias, x, mods, split, heads, out_blocks, ffn_blocks, pool_rows, ident):
    rows, pairs, block = joint.shape[0], heads // 2, joint.shape[0] // 2
    whole = lambda part: pl.BlockSpec((rows, LANES), lambda h, i: (0, part * pairs + h))
    image_rows, width = x[0].shape
    text_rows = x[1].shape[0]
    both = image_rows + text_rows
    depth = heads * HEAD_DIM
    found = pl.pallas_call(
        functools.partial(middle_kernel, split, 64),
        grid=(pairs, 2),
        in_specs=[
            pl.BlockSpec((1, rows - split), lambda h, i: (0, 0)),
            pl.BlockSpec((block, LANES), lambda h, i: (i, h)),
            whole(1),
            whole(2),
            *[WHOLE] * 3,
            *[ANY] * 4,
        ],
        out_specs=[
            WHOLE,
            pl.BlockSpec((1, 8, block), lambda h, i: (h, 0, i)),
            *[WHOLE] * 5,
            *[ANY] * 6,
        ],
        out_shape=[
            jax.ShapeDtypeStruct((rows, depth), LOW),
            jax.ShapeDtypeStruct((pairs, 8, rows), WIDE),
            *[jax.ShapeDtypeStruct((n, width), WIDE) for n in (image_rows, text_rows) * 2],
            jax.ShapeDtypeStruct((text_rows, width), LOW),
            jax.ShapeDtypeStruct((4 * image_rows, width), LOW),
            jax.ShapeDtypeStruct((RING * pool_rows, width), LOW),
            *[
                jax.ShapeDtypeStruct((RING * b.shape[0], b.shape[1]), b.dtype)
                for b in (*out_blocks, *ffn_blocks)
            ],
        ],
        scratch_shapes=[
            pltpu.VMEM((2, depth, width), LOW),
            pltpu.VMEM((2, both, width), LOW),
            pltpu.VMEM((2, both, width), LOW),
            pltpu.VMEM((both, width), LOW),
            pltpu.VMEM((both, width), LOW),
            pltpu.VMEM((both, width), WIDE),
            pltpu.VMEM((image_rows, width), LOW),
            pltpu.SemaphoreType.DMA((2, 2)),
            pltpu.SemaphoreType.DMA((2,)),
            pltpu.SemaphoreType.DMA((2, 3)),
            pltpu.SemaphoreType.DMA((1,)),
            *GatherRing.scratch(2),
            *GatherRing.scratch(2),
            *GatherRing.scratch(1),
        ],
        compiler_params=pltpu.CompilerParams(
            collective_id=ident, has_side_effects=True, vmem_limit_bytes=VMEM_LIMIT
        ),
        name="middle_ring",
    )(bias, joint, joint, joint, *x, mods, *out_blocks, *ffn_blocks)
    return found


def back_kernel(split, chunk, *refs):
    bias_ref, q_ref, k_ref, v_ref, o_ref, lse_ref = refs[:6]
    mid_image, mid_text, cot_image, cot_text, mods, text_part = refs[6:12]
    partial, out_weights, grads, theirs = refs[12], refs[13:15], refs[15:17], refs[17:19]
    units, refs = refs[19], refs[20:]
    dq_ref, dk_ref, dv_ref, image_second, image_grad, text_grad = refs[:6]
    image_rows, text_rows, *fars = refs[6:10]
    sums, text_second, units_got, refs = refs[10:12], refs[12], refs[13], refs[14:]
    dk_acc, dv_acc, weights, parts, got, far_sent, far_got, rows_in, mixed_grad = refs[:9]
    part_sem, sems, row_sem, weight_sem, rows_sem, far_sem, text_sum, units_sem = refs[9:17]
    ring = ScatterRing(grads, sums, refs[17:24])
    text_ring = ScatterRing([text_part], [text_sum], refs[24:])
    me, index = lax.axis_index("dp"), lax.axis_index("tensor")
    rows, texts = mid_image.shape[0], mid_text.shape[0]
    block = q_ref.shape[0]
    at = pl.program_id(0) * pl.num_programs(1) + pl.program_id(1)
    last = pl.num_programs(0) * pl.num_programs(1) - 1

    def part_of(b):
        return partial.at[pl.ds(b * rows, rows)]

    def keep(i):
        return pltpu.make_async_copy(part_of(2 * i), parts.at[i], part_sem.at[i])

    def near(i):
        return pltpu.make_async_remote_copy(
            src_ref=part_of(2 * i + 1), dst_ref=got.at[i],
            send_sem=sems.at[0, i], recv_sem=sems.at[1, i],
            device_id=(me, tensor_peer(1)), device_id_type=MESH,
        )

    def row_copy(source, slot, hop, sem, s):
        some = (pl.ds(0, rows), pl.ds(rows, texts))[s]
        return pltpu.make_async_remote_copy(
            src_ref=rows_in.at[source, some], dst_ref=rows_in.at[slot, some],
            send_sem=row_sem.at[0, s, sem], recv_sem=row_sem.at[1, s, sem],
            device_id=(me, tensor_peer(hop)), device_id_type=MESH,
        )

    def to_far(s):
        return row_copy(0, 2, 2, 0, s)

    def to_near(s):
        return row_copy(0, 1, 1, 1, s)

    def forward(s):
        return row_copy(2, 3, 1, 2, s)

    def units_copy(hop):
        peer = (me + hop) % RING
        return pltpu.make_async_remote_copy(
            src_ref=units.at[peer], dst_ref=units_got.at[me],
            send_sem=units_sem.at[0, hop - 1], recv_sem=units_sem.at[1, hop - 1],
            device_id=(peer, index), device_id_type=MESH,
        )

    def units_own():
        return pltpu.make_async_copy(units.at[me], units_got.at[me], units_sem.at[0, RING - 1])

    def weight(s):
        return pltpu.make_async_copy(out_weights[s], weights.at[s], weight_sem.at[s])

    def save(b, s):
        low, high, whole = ((0, rows, image_rows), (rows, texts, text_rows))[s]
        return pltpu.make_async_copy(
            rows_in.at[b, pl.ds(low, high)], whole.at[pl.ds(b * high, high)], rows_sem.at[s, b]
        )

    def rows_back(second, middle, cotangent, stream):
        centred = middle - jnp.mean(middle, axis=-1, keepdims=True)
        spread = lax.rsqrt(jnp.mean(centred * centred, axis=-1, keepdims=True) + EPS)
        normed = centred * spread
        wide = second * mods[2 * stream + 1 : 2 * stream + 2]
        inner = jnp.mean(wide, axis=-1, keepdims=True)
        cross = jnp.mean(wide * normed, axis=-1, keepdims=True)
        grad = cotangent.astype(WIDE) + (wide - inner - normed * cross) * spread
        return grad, (mods[2 * stream : 2 * stream + 1] * grad).astype(LOW)

    @pl.when(at == 0)
    def _():
        for i in range(2):
            keep(i).start()
            weight(i).start()
        text_ring.load_all()
        ring.load_all()
        meet(
            [((me + hop) % RING, index) for hop in range(1, RING)]
            + [(me, tensor_peer(hop)) for hop in (1, 2)]
        )
        for i in range(2):
            near(i).start()
        text_ring.start()
        units_own().start()
        for hop in range(1, RING):
            units_copy(hop).start()
        for i in range(2):
            keep(i).wait()
            near(i).wait()
        far_sent[...] = (parts[1].astype(WIDE) + got[1].astype(WIDE)).astype(LOW)
        far = pltpu.make_async_remote_copy(
            src_ref=far_sent, dst_ref=far_got, send_sem=sems.at[0, 2], recv_sem=sems.at[1, 2],
            device_id=(me, tensor_peer(2)), device_id_type=MESH,
        )
        far.start()
        for step in range(1, 6):
            text_ring.step(step)
        ring.start()
        far.wait()

        def image_chunk(i, _):
            some = pl.ds(pl.multiple_of(i * chunk, chunk), chunk)
            second = parts[0, some].astype(WIDE) + got[0, some].astype(WIDE)
            second = second + far_got[some].astype(WIDE)
            image_second[some] = second
            grad, low = rows_back(second, mid_image[some], cot_image[some], 0)
            image_grad[some] = grad
            rows_in[0, some] = low
            return 0

        lax.fori_loop(0, rows // chunk, image_chunk, 0)
        to_far(0).start()
        to_near(0).start()
        for step in (6, 7):
            text_ring.step(step)
        pooled = text_sum.shape[0]
        text_second[...] = jnp.zeros_like(text_second)
        text_second[:pooled] = text_sum[...]
        grad, low = rows_back(text_second[...], mid_text[...], cot_text[...], 1)
        text_grad[...] = grad
        rows_in[0, rows:] = low
        to_far(1).start()
        to_near(1).start()
        ring.step(1)
        for s in range(2):
            to_far(s).wait()
            forward(s).start()
        for s in range(2):
            weight(s).wait()
            to_near(s).wait()

        def through(b):
            image = dot(rows_in[b, :rows], weights[0], NT).astype(LOW)
            mixed_grad[b * rows : (b + 1) * rows] = image
            text = dot(rows_in[b, rows:], weights[1], NT).astype(LOW)
            mixed_grad[split + b * texts : split + (b + 1) * texts] = text

        for b in range(3):
            through(b)
        ring.step(2)
        for s in range(2):
            forward(s).wait()
        through(3)
        for b in range(4):
            for s in range(2):
                save(b, s).start()

    far_copies = [
        pltpu.make_async_remote_copy(
            src_ref=theirs[s], dst_ref=fars[s], send_sem=far_sem.at[0, s], recv_sem=far_sem.at[1, s],
            device_id=(me, tensor_peer(2)), device_id_type=MESH,
        )
        for s in range(2)
    ]

    @pl.when(at == 1)
    def _():
        for copy in far_copies:
            copy.start()

    for step, when in ((3, 1), (4, 6), (5, 11)):

        @pl.when(at == when)
        def _():
            ring.step(step)

    place = (
        pl.ds(pl.multiple_of(pl.program_id(1) * block, block), block),
        pl.ds(pl.multiple_of(pl.program_id(0) * LANES, LANES), LANES),
    )
    attend_back_pair(
        split,
        (bias_ref, q_ref, k_ref, v_ref, o_ref, mixed_grad.at[place], lse_ref)
        + (dq_ref, dk_ref, dv_ref, dk_acc, dv_acc),
    )

    @pl.when(at == last)
    def _():
        ring.step(6)
        ring.step(7)
        ring.end()
        text_ring.end()
        for copy in far_copies:
            copy.wait()
        units_own().wait()
        for hop in range(1, RING):
            units_copy(hop).wait()
        for b in range(4):
            for s in range(2):
                save(b, s).wait()


def back_ring(
    joint, bias, mixed, lse, split, heads, text_part, middle, cotangent, mods, partial,
    out_weights, grads, theirs, units, ident, block=256,
):
    rows, pairs = joint.shape[0], heads // 2
    whole = lambda part: pl.BlockSpec((rows, LANES), lambda h, i: (0, part * pairs + h))
    some = pl.BlockSpec((block, LANES), lambda h, i: (i, h))
    image_rows, width = middle[0].shape
    texts = middle[1].shape[0]
    depth, pooled = heads * HEAD_DIM, text_part.shape[0] // RING
    found = pl.pallas_call(
        functools.partial(back_kernel, split, 64),
        grid=(pairs, rows // block),
        in_specs=[
            pl.BlockSpec((rows - split, 1), lambda h, i: (0, 0)),
            some,
            whole(1),
            whole(2),
            some,
            pl.BlockSpec((1, 8, block), lambda h, i: (h, 0, i)),
            *[WHOLE] * 5,
            *[ANY] * 9,
        ],
        out_specs=[some, whole(0), whole(0), *[WHOLE] * 3, *[ANY] * 4, *[WHOLE] * 3, ANY],
        out_shape=[
            *[jax.ShapeDtypeStruct((rows, depth), LOW)] * 3,
            *[jax.ShapeDtypeStruct((n, width), WIDE) for n in (image_rows, image_rows, texts)],
            *[jax.ShapeDtypeStruct((4 * n, width), LOW) for n in (image_rows, texts)],
            *[jax.ShapeDtypeStruct(t.shape, t.dtype) for t in theirs],
            *[jax.ShapeDtypeStruct((g.shape[0] // RING, g.shape[1]), WIDE) for g in grads],
            jax.ShapeDtypeStruct((texts, width), WIDE),
            jax.ShapeDtypeStruct(units.shape, units.dtype),
        ],
        scratch_shapes=[
            *[pltpu.VMEM((rows, LANES), WIDE)] * 2,
            pltpu.VMEM((2, depth, width), LOW),
            *[pltpu.VMEM((2, image_rows, width), LOW)] * 2,
            *[pltpu.VMEM((image_rows, width), LOW)] * 2,
            pltpu.VMEM((4, image_rows + texts, width), LOW),
            pltpu.VMEM((rows, depth), LOW),
            pltpu.SemaphoreType.DMA((2,)),
            pltpu.SemaphoreType.DMA((2, 3)),
            pltpu.SemaphoreType.DMA((2, 2, 3)),
            pltpu.SemaphoreType.DMA((2,)),
            pltpu.SemaphoreType.DMA((2, 4)),
            pltpu.SemaphoreType.DMA((2, 2)),
            pltpu.VMEM((pooled, width), WIDE),
            pltpu.SemaphoreType.DMA((2, RING)),
            *ScatterRing.scratch([g.shape for g in grads]),
            *ScatterRing.scratch([text_part.shape]),
        ],
        compiler_params=pltpu.CompilerParams(
            collective_id=ident, has_side_effects=True, vmem_limit_bytes=VMEM_LIMIT
        ),
        name="back_ring",
    )(
        bias.T, joint, joint, joint, mixed, lse, *middle, *cotangent, mods, text_part,
        partial, *out_weights, *grads, *theirs, units,
    )
    return found


def attend_kernel(split, count, waits, *refs):
    bias_ref, q_ref, k_ref, v_ref = refs[:4]
    blocks, (out_ref, lse_ref) = refs[4 : 4 + count], refs[4 + count : 6 + count]
    at = pl.program_id(0) * pl.num_programs(1) + pl.program_id(1)
    if count:
        ring = GatherRing(blocks, refs[6 + count : 6 + 2 * count], refs[6 + 2 * count :])

        @pl.when(at == 0)
        def _():
            meet(ring.sides)
            ring.start()

        for step, when in enumerate(waits):

            @pl.when(at == when)
            def _():
                ring.step(step + 1)

    attend_pair(split, bias_ref, q_ref, k_ref, v_ref, out_ref, lse_ref)
    if count:

        @pl.when(at == pl.num_programs(0) * pl.num_programs(1) - 1)
        def _():
            for step in range(len(waits) + 1, ring.STEPS + 1):
                ring.step(step)
            ring.end()


def attend(joint, bias, split, heads, blocks, ident, waits):
    rows, pairs, count, block = joint.shape[0], heads // 2, len(blocks), joint.shape[0] // 2
    whole = lambda part: pl.BlockSpec((rows, LANES), lambda h, i: (0, part * pairs + h))
    extra = dict(collective_id=ident, has_side_effects=True) if count else {}
    found = pl.pallas_call(
        functools.partial(attend_kernel, split, count, waits),
        grid=(pairs, 2),
        in_specs=[
            pl.BlockSpec((1, rows - split), lambda h, i: (0, 0)),
            pl.BlockSpec((block, LANES), lambda h, i: (i, h)),
            whole(1),
            whole(2),
            *[ANY] * count,
        ],
        out_specs=[
            pl.BlockSpec((block, LANES), lambda h, i: (i, h)),
            pl.BlockSpec((1, 8, block), lambda h, i: (h, 0, i)),
            *[ANY] * count,
        ],
        out_shape=[
            jax.ShapeDtypeStruct((rows, heads * HEAD_DIM), LOW),
            jax.ShapeDtypeStruct((pairs, 8, rows), WIDE),
            *[jax.ShapeDtypeStruct((RING * b.shape[0], b.shape[1]), b.dtype) for b in blocks],
        ],
        scratch_shapes=GatherRing.scratch(count) if count else [],
        compiler_params=pltpu.CompilerParams(vmem_limit_bytes=VMEM_LIMIT, **extra),
        name="attend",
    )(bias, joint, joint, joint, *blocks)
    return found[0], found[1], found[2:]


def attend_back_pair(split, refs):
    (bias_ref, q_ref, k_ref, v_ref, o_ref, g_ref, lse_ref, dq_ref, dk_ref, dv_ref, dk_acc, dv_acc) = refs
    step = pl.program_id(1)
    scale = HEAD_DIM ** (-0.5)

    @pl.when(step == 0)
    def _():
        dk_acc[...] = jnp.zeros_like(dk_acc)
        dv_acc[...] = jnp.zeros_like(dv_acc)

    product = (g_ref[...].astype(WIDE) * o_ref[...].astype(WIDE)).T
    bias = bias_ref[...]
    dq = None
    for head in range(2):
        mine = head_lanes(head)
        queries = jnp.where(mine, q_ref[...] * scale, 0).astype(LOW)
        grads = jnp.where(mine, g_ref[...], 0).astype(LOW)
        keys = jnp.where(mine, k_ref[...], 0).astype(LOW)
        own = product[head * HEAD_DIM : (head + 1) * HEAD_DIM]
        delta = jnp.sum(own, axis=0, keepdims=True)
        total = lse_ref[0][4 * head : 4 * head + 1]
        for low, high in ((0, split), (split, k_ref.shape[0])):
            scores = dot(k_ref[low:high], queries, NT)
            if low:
                scores = scores + bias
            probs = jnp.exp(scores - total)
            grad_probs = dot(v_ref[low:high], grads, NT)
            grad_scores = (probs * (grad_probs - delta)).astype(LOW)
            dv_acc[low:high] += dot(probs.astype(LOW), grads, NN)
            dk_acc[low:high] += dot(grad_scores, queries, NN)
            part = dot(grad_scores, keys[low:high], TN)
            dq = part if dq is None else dq + part
    dq_ref[...] = (dq * scale).astype(LOW)

    @pl.when(step == pl.num_programs(1) - 1)
    def _():
        dk_ref[...] = dk_acc[...].astype(LOW)
        dv_ref[...] = dv_acc[...].astype(LOW)


def attend_back_kernel(split, count, waits, *refs):
    ins, rest = refs[:7], refs[7:]
    grads, outs, rest = rest[:count], rest[count : count + 3], rest[count + 3 :]
    sums, accs, rest = rest[:count], rest[count : count + 2], rest[count + 2 :]
    at = pl.program_id(0) * pl.num_programs(1) + pl.program_id(1)
    if count:
        ring = ScatterRing(grads, sums, rest)

        @pl.when(at == 0)
        def _():
            ring.load_all()
            meet(ring.sides)
            ring.start()

        for step, when in enumerate(waits):

            @pl.when(at == when)
            def _():
                ring.step(step + 1)

    attend_back_pair(split, (*ins, *outs, *accs))
    if count:

        @pl.when(at == pl.num_programs(0) * pl.num_programs(1) - 1)
        def _():
            for step in range(len(waits) + 1, ring.STEPS + 1):
                ring.step(step)
            ring.end()


def attend_back(joint, bias, mixed, grad, lse, split, heads, grads, ident, waits):
    rows, pairs, count, block = joint.shape[0], heads // 2, len(grads), joint.shape[0] // 2
    whole = lambda part: pl.BlockSpec((rows, LANES), lambda h, i: (0, part * pairs + h))
    some = pl.BlockSpec((block, LANES), lambda h, i: (i, h))
    extra = dict(collective_id=ident, has_side_effects=True) if count else {}
    found = pl.pallas_call(
        functools.partial(attend_back_kernel, split, count, waits),
        grid=(pairs, 2),
        in_specs=[
            pl.BlockSpec((rows - split, 1), lambda h, i: (0, 0)),
            some,
            whole(1),
            whole(2),
            some,
            some,
            pl.BlockSpec((1, 8, block), lambda h, i: (h, 0, i)),
            *[ANY] * count,
        ],
        out_specs=[some, whole(0), whole(0), *[WHOLE] * count],
        out_shape=[
            *[jax.ShapeDtypeStruct((rows, heads * HEAD_DIM), LOW)] * 3,
            *[jax.ShapeDtypeStruct((g.shape[0] // RING, g.shape[1]), WIDE) for g in grads],
        ],
        scratch_shapes=[
            *[pltpu.VMEM((rows, LANES), WIDE)] * 2,
            *(ScatterRing.scratch([g.shape for g in grads]) if count else []),
        ],
        compiler_params=pltpu.CompilerParams(vmem_limit_bytes=VMEM_LIMIT, **extra),
        name="attend_back",
    )(bias.T, joint, joint, joint, mixed, grad, lse, *grads)
    return found[:3], found[3:]


def local(size, image, text, cond, w_ada, w_qkv, w_out, w_up, w_down, grad_image, grad_text):
    index = lax.axis_index("tensor")
    seqs = size
    image_rows, width = image.shape[1], image.shape[2]
    text_tokens = text.shape[1]
    text_own = -(-text_tokens // 4)
    text_rows = -(-text_own // TEXT_TILE) * TEXT_TILE
    pool_rows = -(-text_own // POOL_TILE) * POOL_TILE
    width_here = w_ada.shape[-1]
    ada_rows = w_ada.shape[1]
    heads_here = w_qkv.shape[-1] // HEAD_DIM

    def blocks_of(weight):
        return [weight[stream].astype(LOW).reshape(weight.shape[1], -1) for stream in range(2)]

    up_blocks, down_blocks = blocks_of(w_up), blocks_of(w_down)

    units = up_blocks[1].shape[1] // size
    text_up = lax.all_to_all(
        up_blocks[1].reshape(-1, size, units), "dp", split_axis=1, concat_axis=0, tiled=True
    ).reshape(width, units)
    text_down = down_blocks[1]

    def pool_start(rows):
        copies = jnp.broadcast_to(rows[None, :pool_rows], (size, pool_rows, width))
        rows = lax.all_to_all(copies, "dp", split_axis=0, concat_axis=0, tiled=True)
        return rows.reshape(-1, width)

    def own_pool(part):
        part = part.reshape(size, pool_rows, width)
        part = lax.all_to_all(part, "dp", split_axis=0, concat_axis=0, tiled=True)
        total = jnp.sum(part.astype(WIDE), axis=0)
        return jnp.pad(total, ((0, text_rows - pool_rows), (0, 0)))


    cond_low = jax.nn.silu(cond).astype(LOW)
    cond_rows = cond_low.reshape(seqs, ada_rows)
    ada_low = w_ada.astype(LOW)

    def own_text(rows):
        padded = jnp.pad(rows, ((0, 4 * text_own - text_tokens), (0, 0)))
        own = lax.dynamic_slice_in_dim(padded, index * text_own, text_own, 0)
        return jnp.pad(own, ((0, text_rows - text_own), (0, 0)))

    cot_rows = [grad_image[0], own_text(grad_text[0])]
    x_rows = [image[0], own_text(text[0])]
    if size == RING:
        ada_rows_low = ada_low.transpose(0, 2, 1, 3).reshape(12, ada_rows, width_here)
        attn_rows, ffn_rows, qkv_full, pooled_grad, modulation, cond_rows = first_ring(
            x_rows, cot_rows, cond_rows, ada_rows_low, blocks_of(w_qkv), pool_rows, 1
        )
        modulation, cond_rows = modulation.reshape(2, 6, width), cond_rows.astype(LOW)
    else:
        cond_rows = lax.all_to_all(cond_rows, "dp", split_axis=0, concat_axis=0, tiled=True)
        mod_parts = jnp.einsum("nd,sdkf->nskf", cond_rows, ada_low, preferred_element_type=WIDE)
        mod_parts = lax.all_to_all(mod_parts, "dp", split_axis=0, concat_axis=0, tiled=True)
        modulation = lax.all_gather(jnp.sum(mod_parts, axis=0), "tensor", axis=2, tiled=True)

    def mod_row(stream, which):
        return modulation[stream, which][None, :]

    split_at = 4 * image_rows
    places = jnp.arange(4 * text_rows)
    token = ((places // text_rows) ^ index) * text_own + places % text_rows
    is_key = (places % text_rows < text_own) & (token < text_tokens)
    bias = jnp.where(is_key, 0.0, -1e30).astype(WIDE)[None, :]

    streams = [rows.astype(WIDE) for rows in x_rows]
    cotangent = [rows.astype(WIDE) for rows in cot_rows]
    normed_in = [layer_norm(residual) for residual in streams]
    first_in = [
        (normed_in[s] * (1.0 + mod_row(s, 1)) + mod_row(s, 0)).astype(LOW) for s in range(2)
    ]
    ffn_grad = [(mod_row(s, 5) * cotangent[s]).astype(LOW) for s in range(2)]
    if size != RING:
        attn_rows = [gather_rows(rows) for rows in first_in]
        ffn_rows, pooled_grad = gather_rows(ffn_grad[0]), pool_start(ffn_grad[1])
        qkv_full = gather_dp(blocks_of(w_qkv), size, 1)
    joint = jnp.concatenate(
        [dot(attn_rows[s], qkv_full[s], NN).astype(LOW) for s in range(2)], axis=0
    )
    text_ffn_moved = gather_start(pooled_grad)
    ffn_blocks = [up_blocks[0], down_blocks[0]]
    if size == RING:
        mods = jnp.concatenate(
            [row for s in range(2) for row in (mod_row(s, 2), 1.0 + mod_row(s, 4), mod_row(s, 3))]
            + [jnp.zeros((2, width), WIDE)],
            axis=0,
        )
        found = middle_ring(
            joint, bias, x_rows, mods, split_at, heads_here, blocks_of(w_out), ffn_blocks,
            pool_rows, 2,
        )
        mixed, log_total, *found = found
        branches, middle, mlp_rows, pooled_in = found[:2], found[2:4], found[5], found[6]
        out_full, up_full, down_full = found[7:9], found[9], found[10]
    else:
        mixed, log_total, _ = attend(joint, bias, split_at, heads_here, [], 0, ())
        *out_full, up_full, down_full = gather_dp(blocks_of(w_out) + ffn_blocks, size, 2)
        branches = [
            scatter_rows(dot(mixed[:split_at], out_full[0], NN)),
            scatter_rows(dot(mixed[split_at:], out_full[1], NN)),
        ]
        middle = [streams[s] + mod_row(s, 2) * branches[s] for s in range(2)]
        second_in = [
            (layer_norm(middle[s]) * (1.0 + mod_row(s, 4)) + mod_row(s, 3)).astype(LOW)
            for s in range(2)
        ]
        mlp_rows, pooled_in = gather_rows(second_in[0]), pool_start(second_in[1])
    mixed, *text_ffn_moved = lax.optimization_barrier((mixed, *text_ffn_moved))
    text_ffn_rows = gather_end(pooled_grad, *text_ffn_moved)
    mixed_rows = [mixed[:split_at], mixed[split_at:]]
    normed_mid = [layer_norm(residual) for residual in middle]

    def gelu_back(pre_act, hidden_grad):
        return jax.vjp(gelu_tanh, pre_act)[1](hidden_grad)[0].astype(LOW)

    text_moved = gather_start(pooled_in)
    pre_act = dot(mlp_rows, up_full, NN)
    hidden = gelu_tanh(pre_act).astype(LOW)
    pre_grad = gelu_back(pre_act, dot(ffn_rows, down_full, NT))
    pre_grad, *text_moved = lax.optimization_barrier((pre_grad, *text_moved))
    text_mlp_rows = gather_end(pooled_in, *text_moved)
    text_pre_act = dot(text_mlp_rows, text_up, NN)
    text_hidden = gelu_tanh(text_pre_act).astype(LOW)
    text_pre_grad = gelu_back(text_pre_act, dot(text_ffn_rows, text_down, NT))
    text_here, text_there = scatter_start(dot(text_pre_grad, text_up, NT))
    text_far = lax.ppermute(text_there, "tensor", CHIP)
    pre_grad, text_there = lax.optimization_barrier((pre_grad, text_there))
    second_part = dot(pre_grad, up_full, NT).astype(LOW)
    down_grad = dot(hidden, ffn_rows, TN).astype(LOW)
    up_grad = dot(mlp_rows, pre_grad, TN).astype(LOW)
    here, there = scatter_start(dot(hidden, down_full, NN))
    up_grad, down_grad, second_part, there, text_far = lax.optimization_barrier(
        (up_grad, down_grad, second_part, there, text_far)
    )
    second_grad, ffn = [None, None], [None, None]
    text_second = (text_here + text_far.astype(WIDE)).astype(LOW)
    text_here, text_there = scatter_start(dot(text_hidden, text_down, NN))
    text_down_grad = dot(text_hidden, text_ffn_rows, TN)
    text_up_grad = dot(text_mlp_rows, text_pre_grad, TN).astype(LOW).reshape(size, -1, units)
    if size == RING:
        mods = jnp.concatenate(
            [row for s in range(2) for row in (mod_row(s, 2), 1.0 + mod_row(s, 4))]
            + [jnp.zeros((4, width), WIDE)],
            axis=0,
        )
        found = back_ring(
            joint, bias, mixed, log_total, split_at, heads_here, text_second, middle,
            cot_rows, mods, second_part, out_full,
            [down_grad, up_grad], [there, text_there], text_up_grad, 5,
        )
        *grads, image_second, image_middle, text_middle = found[:6]
        middle_grad, branch_rows = [image_middle, text_middle], found[6:8]
        far, text_far, down_sum, up_sum, text_sum, text_up_grad = found[8:]
        text_up_grad = text_up_grad.transpose(1, 0, 2)
        second_grad = [image_second, text_sum]
    else:
        second_grad = [scatter_rows(second_part), own_pool(text_second)]
        middle_grad, branch_rows = [None, None], [None, None]
        for s in range(2):
            wide = second_grad[s] * (1.0 + mod_row(s, 4))
            middle_grad[s] = cotangent[s] + jax.vjp(layer_norm, middle[s])[1](wide)[0]
            branch_rows[s] = gather_rows((mod_row(s, 2) * middle_grad[s]).astype(LOW))
        mixed_grad = jnp.concatenate(
            [dot(branch_rows[s], out_full[s], NT).astype(LOW) for s in range(2)], axis=0
        )
        grads = attend_back(
            joint, bias, mixed, mixed_grad, log_total, split_at, heads_here, [], 0, ()
        )[0]
        grads = list(grads)
        down_sum, up_sum = scatter_dp([down_grad, up_grad], size, 5)
        far = lax.ppermute(there, "tensor", CHIP)
        text_far = lax.ppermute(text_there, "tensor", CHIP)
        text_up_grad = lax.all_to_all(
            text_up_grad, "dp", split_axis=0, concat_axis=2, tiled=True
        )
    text_ffn = (text_here + text_far.astype(WIDE)).astype(LOW)
    text_ffn, *held = lax.optimization_barrier(
        (text_ffn, *grads, *second_grad, *middle_grad, *branch_rows)
    )
    grads, second_grad, middle_grad, branch_rows = held[:3], held[3:5], held[5:7], held[7:]
    ffn[0], ffn[1] = here + far.astype(WIDE), own_pool(text_ffn)
    results = [(middle[s] + mod_row(s, 5) * ffn[s]).astype(LOW) for s in range(2)]
    gate_terms = [jnp.sum(cotangent[s] * ffn[s], axis=0)[None] for s in range(2)]
    out_grad = [dot(mixed_rows[s], branch_rows[s], TN).astype(LOW) for s in range(2)]
    joint_grad = jnp.concatenate(grads, axis=1)
    joint_rows = [joint_grad[:split_at], joint_grad[split_at:]]
    qkv_grad = [dot(attn_rows[s], joint_rows[s], TN).astype(LOW) for s in range(2)]
    other = []
    for s in range(2):
        other += [
            jnp.zeros((2, width), WIDE),
            jnp.sum(middle_grad[s] * branches[s], axis=0)[None],
            jnp.sum(second_grad[s], axis=0)[None],
            jnp.sum(second_grad[s] * normed_mid[s], axis=0)[None],
            gate_terms[s],
        ]
    other = jnp.concatenate(other + [jnp.zeros((4, width), WIDE)], axis=0)
    if size == RING:
        scale = jnp.concatenate([1.0 + mod_row(s, 1) for s in range(2)], axis=0)
        image_input, mod_sum, mod_grad, act_grad, text_out, text_grad, *found = tail_ring(
            grads, qkv_full, scale, other, x_rows, middle_grad, results[1], ada_rows_low,
            qkv_grad + out_grad, 6,
        )
        act_grad = act_grad[:, 0].reshape(1, width)
        qkv_image, qkv_text, out_image, out_text = found
        qkv_sums, out_sum = [qkv_image, qkv_text], [out_image, out_text]
        mod_sum = mod_sum[:12].reshape(2, 6, width_here)
        mod_grad = mod_grad[:, :12].reshape(seqs, 2, 6, width_here)
        mod_grad, text_up_grad = lax.optimization_barrier((mod_grad, text_up_grad))
    else:
        *qkv_sums, out_image, out_text = scatter_dp(qkv_grad + out_grad, size, 6)
        out_sum = [out_image, out_text]
        first_parts = [dot(joint_rows[s], qkv_full[s], NT).astype(LOW) for s in range(2)]
        here, there = scatter_start(
            jnp.concatenate(
                [
                    part[b * (part.shape[0] // 4) : (b + 1) * (part.shape[0] // 4)]
                    for b in range(4)
                    for part in first_parts
                ]
            )
        )
        far = lax.ppermute(there, "tensor", CHIP)
        first_rows = here + far.astype(WIDE)
        first_grad = [first_rows[:image_rows], first_rows[image_rows:]]
        input_grad, first_terms = [None, None], []
        for s in range(2):
            wide = first_grad[s] * (1.0 + mod_row(s, 1))
            input_grad[s] = middle_grad[s] + jax.vjp(layer_norm, streams[s])[1](wide)[0]
            shift = jnp.sum(first_grad[s], axis=0)
            gain = jnp.sum(first_grad[s] * normed_in[s], axis=0)
            first_terms.append(jnp.stack([shift, gain]))
        image_input = input_grad[0]
        text_out = lax.all_gather(results[1], "tensor", axis=0)
        text_grad = lax.all_gather(input_grad[1], "tensor", axis=0)
        mod_terms = other[:12].reshape(2, 6, width).at[:, :2].set(jnp.stack(first_terms))
        mod_split = mod_terms.reshape(2, 6, 4, width_here).transpose(2, 0, 1, 3)
        mod_sum = jnp.sum(
            lax.all_to_all(mod_split, "tensor", split_axis=0, concat_axis=0, tiled=True), axis=0
        )
        mod_low = jnp.broadcast_to(mod_sum.astype(LOW)[None], (seqs,) + mod_sum.shape)
        mod_grad = lax.all_to_all(mod_low, "dp", split_axis=0, concat_axis=0, tiled=True)
        act_parts = jnp.einsum("nskf,sdkf->nd", mod_grad, ada_low, preferred_element_type=WIDE)
        act_parts = lax.all_to_all(act_parts, "dp", split_axis=0, concat_axis=0, tiled=True)
        act_grad = lax.psum(act_parts.reshape(1, width), "tensor")
    shift_grad = mod_sum[:, 3]
    text_up_grad = text_up_grad.reshape(-1, size * units).astype(WIDE)
    ada_grad = jnp.einsum("nd,nskf->sdkf", cond_rows, mod_grad, preferred_element_type=WIDE)
    cond_grad = jax.vjp(jax.nn.silu, cond)[1](act_grad)[0]

    def whole_text(blocks):
        return blocks[:, :text_own].reshape(4 * text_own, width)[:text_tokens][None]

    down_sum = jnp.stack([down_sum, text_down_grad])
    up_sum = jnp.stack([up_sum, text_up_grad])
    qkv_sum, out_sum = jnp.stack(qkv_sums), jnp.stack(out_sum)

    return (
        results[0][None],
        whole_text(text_out),
        image_input[None],
        whole_text(text_grad),
        cond_grad,
        shift_grad[None],
        ada_grad,
        qkv_sum.reshape(w_qkv.shape),
        out_sum.reshape(w_out.shape),
        up_sum,
        down_sum,
    )


def solution(mesh):
    size = mesh.shape["dp"]

    def step(*args):
        return local(size, *args)

    return jax.shard_map(
        step,
        mesh=mesh,
        in_specs=(
            P("dp", "tensor", None),
            P("dp", None, None),
            P("dp", None),
            P(None, "dp", None, "tensor"),
            P(None, "dp", None, "tensor"),
            P(None, ("tensor", "dp"), None),
            P(None, "dp", "tensor"),
            P(None, ("tensor", "dp"), None),
            P("dp", "tensor", None),
            P("dp", None, None),
        ),
        out_specs=(
            P("dp", "tensor", None),
            P("dp", None, None),
            P("dp", "tensor", None),
            P("dp", None, None),
            P("dp", None),
            P("dp", None, "tensor"),
            P(None, "dp", None, "tensor"),
            P(None, "dp", None, "tensor"),
            P(None, ("tensor", "dp"), None),
            P(None, "dp", "tensor"),
            P(None, ("tensor", "dp"), None),
        ),
        check_vma=False,
    )
```
